32 devices in a mesh: group: 2 (over x), row: 8 (over z, y), col: 2 (over core).
Axes of the slice: x: 2, y: 2, z: 4, core: 2. Of those that a mesh axis runs over, the one named last changes fastest.
Arguments:
- pair: float32 [64, 32, 128], P(('group', 'row'), 'col'), parts along dimension 0, may hold values from -6 to 6
- token_mask: int32 [64], P('group'), parts along dimension 0, may hold values from 0 to 1, as said below
- chains: int32 [64], P('group'), parts along dimension 0, may hold values from 0 to 3, never falling along the last dimension, each value on 1 to 16 neighbouring positions
- chain_bias: float32 [128], replicated, may hold values from -4 to 4
- proj_weight: bfloat16 [2, 128, 512], replicated, may hold values from -0.5 to 0.5
- gate_weight: bfloat16 [2, 128, 128], replicated, may hold values from -0.5 to 0.5
- out_weight: bfloat16 [2, 128, 128], replicated, may hold values from -0.5 to 0.5
Outputs:
- updated: float32 [64, 32, 128], P(('group', 'row'), 'col'), parts along dimension 0
The draws below stay inside these ranges and needn't reach their ends.
There are 2 independent parts, one for each index of `group`. The reference program is written for one: setup_inputs(seed, part) draws one part's arguments, and reference() takes and returns one part's arrays. A program takes and returns all parts, laid end to end along the dimension named above; an argument that names none is the same for every part. Nothing has to cross between parts.
Inputs may be any that keep to these rules, and one draw needn't show every extreme that they name: token_mask is 1 on a leading run of at least 16 tokens and 0 after it; the last token is always padding. `chains`: chain numbers never fall along the crop; a chain holds at most 16 tokens.
All inputs are finite; a program needn't handle non-finite values.
Results may differ from the reference program's by a relative error of at most 0.003.
Values may be sent and summed in bfloat16 or wider, within the bound.
No kernel may reach another device: no remote copies, remote signals or barrier semaphores. Data moves between devices by JAX's collectives and lax.ppermute only.
A program may use at most 128 MiB of HBM per device.

```python
import math
import jax
import jax.numpy as jnp
import numpy as np
from jax import lax

PAIR_C = 128
HID = 128
CROP = 32


def draw_token_mask(key, part):
    key = jax.random.fold_in(key, 7)
    length = jax.random.randint(key, (), CROP // 2, CROP)
    return (jnp.arange(CROP) < length).astype(jnp.int32)


def levels(rng, extent, cuts, smallest, high):
    def one(dim, blocks):
        heights = jax.random.uniform(jax.random.fold_in(jax.random.fold_in(rng, 6), dim), (blocks,), jnp.float32, smallest / len(cuts), high / len(cuts))
        return jnp.repeat(jnp.exp(heights), extent[dim] // blocks).reshape((-1,) + (1,) * (len(extent) - dim - 1))

    level = one(*cuts[0])
    for cut in cuts[1:]:
        level = level * one(*cut)
    return level


def profile(number_of, total, reach, skew):
    loads = [(1 << 20) // math.isqrt(grade ** skew) + 1 for grade in range(2, number_of + 1)]
    spare, given = total - reach - (number_of - 1), [1] * (number_of - 1)
    while spare > 0:
        candidates = [i for i in range(number_of - 1) if given[i] < reach]
        pool, remaining = sum([loads[i] for i in candidates]), spare
        for i in candidates:
            more = min(reach - given[i], max(1, remaining * loads[i] // pool), spare)
            given[i] = given[i] + more
            spare = spare - more
    return np.array([reach] + given)


def ragged(key, amount, total, bound, slope):
    if amount == 2:
        one = jax.random.randint(key, (), max(1, total - bound), min(bound, total - 1) + 1)
        return jnp.stack([one, total - one])
    lengths = jnp.asarray(profile(amount, total, bound, slope), jnp.int32)
    couples = (amount - 1) // 2
    source_of, receiver = lengths[1:1 + 2 * couples:2], lengths[2:2 + 2 * couples:2]
    margin = jnp.minimum(source_of - 1, bound - receiver)
    passed = jax.random.randint(jax.random.fold_in(key, 1), (couples,), 0, 1 << 20) % (margin + 1)
    lengths = lengths.at[1:1 + 2 * couples:2].set(source_of - passed).at[2:2 + 2 * couples:2].set(receiver + passed)
    return lengths[jax.random.permutation(jax.random.fold_in(key, 2), amount)]


def scatter_about(key, shape, spread, reach, shards=(), kind=jnp.bfloat16):
    values = jax.random.normal(key, shape, jnp.float32) * spread
    if len(shards) > 0:
        values = levels(key, shape, shards, -0.22, 0.18) * values
    return jnp.clip(values, min=-reach, max=reach).astype(kind)


def setup_inputs(seed: int = 0, part: int = 0) -> dict:
    keys = jax.random.split(jax.random.key(seed), 8)
    part_splits = jax.random.split(jax.random.fold_in(keys[7], part), 8)
    return {
        "pair": scatter_about(part_splits[0], (CROP, CROP, PAIR_C), 1.0, 6.0, ((0, 8), (1, 2)), jnp.float32),
        "token_mask": draw_token_mask(jax.random.fold_in(jax.random.fold_in(keys[7], part), 71), part),
        "chains": jnp.searchsorted(jnp.cumsum(ragged(part_splits[2], 4, CROP, CROP // 2, 1)), jnp.arange(CROP), side="right").astype(jnp.int32),
        "chain_bias": scatter_about(keys[3], (PAIR_C,), 1.0, 4.0, (), jnp.float32),
        "proj_weight": scatter_about(keys[4], (2, PAIR_C, 4 * HID), PAIR_C ** -0.5, 0.5),
        "gate_weight": scatter_about(keys[5], (2, PAIR_C, PAIR_C), PAIR_C ** -0.5, 0.5),
        "out_weight": scatter_about(keys[6], (2, HID, PAIR_C), HID ** -0.5, 0.5),
    }


def layer_norm(values):
    mean = lax.optimization_barrier(jnp.mean(values, -1, keepdims=True))
    centred = values - mean
    var = lax.optimization_barrier(jnp.mean(centred * centred, -1, keepdims=True))
    return centred * lax.rsqrt(var + 1e-05)

def flat_dot(values, weight):
    shape = values.shape
    result = jnp.dot(values.reshape(-1, shape[-1]), weight, preferred_element_type=jnp.float32)
    return result.reshape(shape[:-1] + (weight.shape[1],))

def project(state, pmask, p_weight, g_weight):
    normed = layer_norm(state).astype(jnp.bfloat16)
    proj = flat_dot(normed, p_weight)
    hidden = p_weight.shape[1] // 4
    gate_a = proj[..., :hidden]
    value_a = proj[..., hidden:2 * hidden]
    gate_b = proj[..., 2 * hidden:3 * hidden]
    value_b = proj[..., 3 * hidden:]
    left = (jax.nn.sigmoid(gate_a) * value_a * pmask[..., None]).astype(jnp.bfloat16)
    right = (jax.nn.sigmoid(gate_b) * value_b * pmask[..., None]).astype(jnp.bfloat16)
    return (normed, left, right)

def finish(state, normed, tri, g_weight, o_weight):
    tnorm = layer_norm(tri).astype(jnp.bfloat16)
    gate = jax.nn.sigmoid(flat_dot(normed, g_weight))
    return state + gate * flat_dot(tnorm, o_weight)

def reference(pair, token_mask, chains, chain_bias, proj_weight, gate_weight, out_weight):
    same = (chains[:, None] == chains[None, :]).astype(jnp.float32)
    state = pair + same[..., None] * chain_bias
    maskf = token_mask.astype(jnp.float32)
    pmask = maskf[:, None] * maskf[None, :]
    normed, left, right = project(state, pmask, proj_weight[0], gate_weight[0])
    tri = jnp.einsum('ikh,jkh->ijh', left.astype(jnp.float32), right.astype(jnp.float32))
    state = finish(state, normed, tri, gate_weight[0], out_weight[0])
    normed, left, right = project(state, pmask, proj_weight[1], gate_weight[1])
    tri = jnp.einsum('kih,kjh->ijh', left.astype(jnp.float32), right.astype(jnp.float32))
    return finish(state, normed, tri, gate_weight[1], out_weight[1])
```

```python
import jax
import jax.numpy as jnp
from jax import lax
from jax.sharding import PartitionSpec as P


def layer_norm(values):
    mean = jnp.mean(values, -1, keepdims=True)
    centred = values - mean
    var = jnp.mean(centred * centred, -1, keepdims=True)
    return centred * lax.rsqrt(var + 1e-05)


def flat_dot(values, weight):
    shape = values.shape
    result = jnp.dot(values.reshape(-1, shape[-1]), weight, preferred_element_type=jnp.float32)
    return result.reshape(shape[:-1] + (weight.shape[1],))


def edge(normed, mask, weight):
    proj = flat_dot(normed, weight)
    hidden = weight.shape[1] // 2
    return (jax.nn.sigmoid(proj[..., :hidden]) * proj[..., hidden:] * mask[..., None]).astype(jnp.bfloat16)


def finish(state, normed, tri, g_weight, o_weight):
    tnorm = layer_norm(tri).astype(jnp.bfloat16)
    gate = jax.nn.sigmoid(flat_dot(normed, g_weight))
    return state + gate * flat_dot(tnorm, o_weight)


def project(state, pmask, p_weight):
    normed = layer_norm(state).astype(jnp.bfloat16)
    proj = flat_dot(normed, p_weight)
    hidden = p_weight.shape[1] // 4
    gate_a = proj[..., :hidden]
    value_a = proj[..., hidden : 2 * hidden]
    gate_b = proj[..., 2 * hidden : 3 * hidden]
    value_b = proj[..., 3 * hidden :]
    left = (jax.nn.sigmoid(gate_a) * value_a * pmask[..., None]).astype(jnp.bfloat16)
    right = (jax.nn.sigmoid(gate_b) * value_b * pmask[..., None]).astype(jnp.bfloat16)
    return (normed, left, right)


def sharded_plan(pair, token_mask, chains, chain_bias, proj_weight, gate_weight, out_weight):
    rows, cols, width = pair.shape
    row_start = lax.axis_index("row") * rows
    col_start = lax.axis_index("col") * cols
    chain_rows = lax.dynamic_slice_in_dim(chains, row_start, rows)
    chain_cols = lax.dynamic_slice_in_dim(chains, col_start, cols)
    mask_rows = lax.dynamic_slice_in_dim(token_mask, row_start, rows).astype(jnp.float32)
    mask_cols = lax.dynamic_slice_in_dim(token_mask, col_start, cols).astype(jnp.float32)
    same = (chain_rows[:, None] == chain_cols[None, :]).astype(jnp.float32)
    state = pair + same[..., None] * chain_bias
    pmask = mask_rows[:, None] * mask_cols[None, :]
    normed, left, right = project(state, pmask, proj_weight[0])
    left_rows, right_rows = (
        lax.all_gather(left, "col", axis=1, tiled=True),
        lax.all_gather(right, "col", axis=1, tiled=True),
    )
    every = jnp.einsum(
        "ikh,jkh->ijh",
        left_rows,
        lax.all_gather(right_rows, "row", axis=0, tiled=True),
        preferred_element_type=jnp.float32,
    )
    tri = lax.dynamic_slice_in_dim(every, col_start, cols, 1)
    state = finish(state, normed, tri, gate_weight[0], out_weight[0])
    normed, left, right = project(state, pmask, proj_weight[1])
    left_rows = lax.all_gather(left, "col", axis=1, tiled=True)
    left_cols = lax.all_to_all(left_rows, "row", split_axis=1, concat_axis=0, tiled=True)
    tri = jnp.einsum(
        "kih,kjh->ijh",
        left_cols,
        lax.all_gather(right, "row", axis=0, tiled=True),
        preferred_element_type=jnp.float32,
    )
    return finish(state, normed, tri, gate_weight[1], out_weight[1])


def gather_rows(block):
    n = lax.axis_size("row")
    me = lax.axis_index("row")
    parts = [block]
    for s in range(1, n):
        parts.append(lax.ppermute(block, "row", [(i, (i + s) % n) for i in range(n)]))
    stacked = jnp.stack(parts)
    order = lax.rem(me - jnp.arange(n) + n, n)
    return jnp.take(stacked, order, axis=0).reshape((-1,) + block.shape[1:])


def whole_crop_plan(pair, token_mask, chains, chain_bias, proj_weight, gate_weight, out_weight):
    rows, cols, width = pair.shape
    row_start = lax.axis_index("row") * rows
    col = lax.axis_index("col")
    col_start = col * cols
    mine = gather_rows(pair.astype(jnp.bfloat16))
    other = lax.ppermute(mine, "col", [(0, 1), (1, 0)])
    first = jnp.where(col == 0, mine, other)
    second = jnp.where(col == 0, other, mine)
    whole = jnp.concatenate([first, second], axis=1).astype(jnp.float32)
    whole = lax.dynamic_update_slice(whole, pair, (row_start, col_start, 0))
    same = (chains[:, None] == chains[None, :]).astype(jnp.float32)
    state = whole + same[..., None] * chain_bias
    mask = token_mask.astype(jnp.float32)
    pmask = mask[:, None] * mask[None, :]
    hidden2 = proj_weight.shape[2] // 2
    normed = layer_norm(state).astype(jnp.bfloat16)
    left = edge(normed, pmask, proj_weight[0, :, :hidden2])
    right = edge(normed, pmask, proj_weight[0, :, hidden2:])
    tri = jnp.einsum("ikh,jkh->ijh", left, right, preferred_element_type=jnp.float32)
    state = finish(state, normed, tri, gate_weight[0], out_weight[0])
    mine_rows = lax.dynamic_slice_in_dim(state, row_start, rows, 1)
    mine_cols = lax.dynamic_slice_in_dim(state, col_start, cols, 1)
    left = edge(layer_norm(mine_rows).astype(jnp.bfloat16), lax.dynamic_slice_in_dim(pmask, row_start, rows, 1), proj_weight[1, :, :hidden2])
    normed = layer_norm(mine_cols).astype(jnp.bfloat16)
    right = edge(normed, lax.dynamic_slice_in_dim(pmask, col_start, cols, 1), proj_weight[1, :, hidden2:])
    tri = jnp.einsum("kih,kjh->ijh", left, right, preferred_element_type=jnp.float32)
    own = lax.dynamic_slice_in_dim(mine_cols, row_start, rows, 0)
    return finish(own, lax.dynamic_slice_in_dim(normed, row_start, rows, 0), tri, gate_weight[1], out_weight[1])


def shards(pair, token_mask, *rest):
    tokens = token_mask.shape[0]
    plan = whole_crop_plan if tokens * tokens <= 4096 else sharded_plan
    return plan(pair, token_mask, *rest)


def solution(mesh):
    placed = (P(("group", "row"), "col", None), P("group"), P("group"), P(), P(), P(), P())
    return jax.shard_map(
        shards,
        mesh=mesh,
        in_specs=placed,
        out_specs=P(("group", "row"), "col", None),
        check_vma=False,
    )
```

```python
import jax
import jax.numpy as jnp
from jax import lax
from jax.sharding import PartitionSpec as P


def layer_norm(values):
    mean = jnp.mean(values, -1, keepdims=True)
    centred = values - mean
    var = jnp.mean(centred * centred, -1, keepdims=True)
    return centred * lax.rsqrt(var + 1e-05)


def flat_dot(values, weight):
    shape = values.shape
    result = jnp.dot(values.reshape(-1, shape[-1]), weight, preferred_element_type=jnp.float32)
    return result.reshape(shape[:-1] + (weight.shape[1],))


def edge(normed, mask, weight):
    proj = flat_dot(normed, weight)
    hidden = weight.shape[1] // 2
    return (jax.nn.sigmoid(proj[..., :hidden]) * proj[..., hidden:] * mask[..., None]).astype(jnp.bfloat16)


def finish(state, normed, tri, g_weight, o_weight):
    tnorm = layer_norm(tri).astype(jnp.bfloat16)
    gate = jax.nn.sigmoid(flat_dot(normed, g_weight))
    return state + gate * flat_dot(tnorm, o_weight)


def project(state, pmask, p_weight):
    normed = layer_norm(state).astype(jnp.bfloat16)
    proj = flat_dot(normed, p_weight)
    hidden = p_weight.shape[1] // 4
    gate_a = proj[..., :hidden]
    value_a = proj[..., hidden : 2 * hidden]
    gate_b = proj[..., 2 * hidden : 3 * hidden]
    value_b = proj[..., 3 * hidden :]
    left = (jax.nn.sigmoid(gate_a) * value_a * pmask[..., None]).astype(jnp.bfloat16)
    right = (jax.nn.sigmoid(gate_b) * value_b * pmask[..., None]).astype(jnp.bfloat16)
    return (normed, left, right)


def sharded_plan(pair, token_mask, chains, chain_bias, proj_weight, gate_weight, out_weight):
    rows, cols, width = pair.shape
    row_start = lax.axis_index("row") * rows
    col_start = lax.axis_index("col") * cols
    chain_rows = lax.dynamic_slice_in_dim(chains, row_start, rows)
    chain_cols = lax.dynamic_slice_in_dim(chains, col_start, cols)
    mask_rows = lax.dynamic_slice_in_dim(token_mask, row_start, rows).astype(jnp.float32)
    mask_cols = lax.dynamic_slice_in_dim(token_mask, col_start, cols).astype(jnp.float32)
    same = (chain_rows[:, None] == chain_cols[None, :]).astype(jnp.float32)
    state = pair + same[..., None] * chain_bias
    pmask = mask_rows[:, None] * mask_cols[None, :]
    normed, left, right = project(state, pmask, proj_weight[0])
    left_rows, right_rows = (
        lax.all_gather(left, "col", axis=1, tiled=True),
        lax.all_gather(right, "col", axis=1, tiled=True),
    )
    every = jnp.einsum(
        "ikh,jkh->ijh",
        left_rows,
        lax.all_gather(right_rows, "row", axis=0, tiled=True),
        preferred_element_type=jnp.float32,
    )
    tri = lax.dynamic_slice_in_dim(every, col_start, cols, 1)
    state = finish(state, normed, tri, gate_weight[0], out_weight[0])
    normed, left, right = project(state, pmask, proj_weight[1])
    left_rows = lax.all_gather(left, "col", axis=1, tiled=True)
    left_cols = lax.all_to_all(left_rows, "row", split_axis=1, concat_axis=0, tiled=True)
    tri = jnp.einsum(
        "kih,kjh->ijh",
        left_cols,
        lax.all_gather(right, "row", axis=0, tiled=True),
        preferred_element_type=jnp.float32,
    )
    return finish(state, normed, tri, gate_weight[1], out_weight[1])


def gather_rows(block):
    copies = jnp.broadcast_to(block, (lax.axis_size("row"),) + block.shape)
    return lax.all_to_all(copies, "row", split_axis=0, concat_axis=0, tiled=True).reshape((-1,) + block.shape[1:])


def whole_crop_plan(pair, token_mask, chains, chain_bias, proj_weight, gate_weight, out_weight):
    rows, cols, width = pair.shape
    row_start = lax.axis_index("row") * rows
    col = lax.axis_index("col")
    col_start = col * cols
    mine = gather_rows(pair)
    other = lax.ppermute(mine, "col", [(0, 1), (1, 0)])
    first = jnp.where(col == 0, mine, other)
    second = jnp.where(col == 0, other, mine)
    whole = jnp.concatenate([first, second], axis=1)
    same = (chains[:, None] == chains[None, :]).astype(jnp.float32)
    state = whole + same[..., None] * chain_bias
    mask = token_mask.astype(jnp.float32)
    pmask = mask[:, None] * mask[None, :]
    hidden2 = proj_weight.shape[2] // 2
    normed = layer_norm(state).astype(jnp.bfloat16)
    left = edge(normed, pmask, proj_weight[0, :, :hidden2])
    right = edge(normed, pmask, proj_weight[0, :, hidden2:])
    tri = jnp.einsum("ikh,jkh->ijh", left, right, preferred_element_type=jnp.float32)
    state = finish(state, normed, tri, gate_weight[0], out_weight[0])
    mine_rows = lax.dynamic_slice_in_dim(state, row_start, rows, 1)
    mine_cols = lax.dynamic_slice_in_dim(state, col_start, cols, 1)
    left = edge(layer_norm(mine_rows).astype(jnp.bfloat16), lax.dynamic_slice_in_dim(pmask, row_start, rows, 1), proj_weight[1, :, :hidden2])
    normed = layer_norm(mine_cols).astype(jnp.bfloat16)
    right = edge(normed, lax.dynamic_slice_in_dim(pmask, col_start, cols, 1), proj_weight[1, :, hidden2:])
    tri = jnp.einsum("kih,kjh->ijh", left, right, preferred_element_type=jnp.float32)
    own = lax.dynamic_slice_in_dim(mine_cols, row_start, rows, 0)
    return finish(own, lax.dynamic_slice_in_dim(normed, row_start, rows, 0), tri, gate_weight[1], out_weight[1])


def shards(pair, token_mask, *rest):
    tokens = token_mask.shape[0]
    plan = whole_crop_plan if tokens * tokens <= 4096 else sharded_plan
    return plan(pair, token_mask, *rest)


def solution(mesh):
    placed = (P(("group", "row"), "col", None), P("group"), P("group"), P(), P(), P(), P())
    return jax.shard_map(
        shards,
        mesh=mesh,
        in_specs=placed,
        out_specs=P(("group", "row"), "col", None),
        check_vma=False,
    )
```

```python
import functools
import jax
import jax.numpy as jnp
from jax import lax
from jax.experimental import pallas as pl
from jax.experimental.pallas import tpu as pltpu
from jax.sharding import PartitionSpec as P


def layer_norm(values):
    mean = jnp.mean(values, -1, keepdims=True)
    centred = values - mean
    var = jnp.mean(centred * centred, -1, keepdims=True)
    return centred * lax.rsqrt(var + 1e-05)


def flat_dot(values, weight):
    shape = values.shape
    result = jnp.dot(values.reshape(-1, shape[-1]), weight, preferred_element_type=jnp.float32)
    return result.reshape(shape[:-1] + (weight.shape[1],))


def project(state, pmask, p_weight):
    normed = layer_norm(state).astype(jnp.bfloat16)
    proj = flat_dot(normed, p_weight)
    hidden = p_weight.shape[1] // 4
    gate_a = proj[..., :hidden]
    value_a = proj[..., hidden : 2 * hidden]
    gate_b = proj[..., 2 * hidden : 3 * hidden]
    value_b = proj[..., 3 * hidden :]
    left = (jax.nn.sigmoid(gate_a) * value_a * pmask[..., None]).astype(jnp.bfloat16)
    right = (jax.nn.sigmoid(gate_b) * value_b * pmask[..., None]).astype(jnp.bfloat16)
    return (normed, left, right)


def finish(state, normed, tri, g_weight, o_weight):
    tnorm = layer_norm(tri).astype(jnp.bfloat16)
    gate = jax.nn.sigmoid(flat_dot(normed, g_weight))
    return state + gate * flat_dot(tnorm, o_weight)


def sharded_plan(pair, token_mask, chains, chain_bias, proj_weight, gate_weight, out_weight):
    rows, cols, width = pair.shape
    row_start = lax.axis_index("row") * rows
    col_start = lax.axis_index("col") * cols
    chain_rows = lax.dynamic_slice_in_dim(chains, row_start, rows)
    chain_cols = lax.dynamic_slice_in_dim(chains, col_start, cols)
    mask_rows = lax.dynamic_slice_in_dim(token_mask, row_start, rows).astype(jnp.float32)
    mask_cols = lax.dynamic_slice_in_dim(token_mask, col_start, cols).astype(jnp.float32)
    same = (chain_rows[:, None] == chain_cols[None, :]).astype(jnp.float32)
    state = pair + same[..., None] * chain_bias
    pmask = mask_rows[:, None] * mask_cols[None, :]
    normed, left, right = project(state, pmask, proj_weight[0])
    left_rows, right_rows = (
        lax.all_gather(left, "col", axis=1, tiled=True),
        lax.all_gather(right, "col", axis=1, tiled=True),
    )
    every = jnp.einsum(
        "ikh,jkh->ijh",
        left_rows,
        lax.all_gather(right_rows, "row", axis=0, tiled=True),
        preferred_element_type=jnp.float32,
    )
    tri = lax.dynamic_slice_in_dim(every, col_start, cols, 1)
    state = finish(state, normed, tri, gate_weight[0], out_weight[0])
    normed, left, right = project(state, pmask, proj_weight[1])
    left_rows = lax.all_gather(left, "col", axis=1, tiled=True)
    left_cols = lax.all_to_all(left_rows, "row", split_axis=1, concat_axis=0, tiled=True)
    tri = jnp.einsum(
        "kih,kjh->ijh",
        left_cols,
        lax.all_gather(right, "row", axis=0, tiled=True),
        preferred_element_type=jnp.float32,
    )
    return finish(state, normed, tri, gate_weight[1], out_weight[1])


def tile_norm(values):
    mean = jnp.mean(values, -1, keepdims=True)
    centred = values - mean
    var = jnp.mean(centred * centred, -1, keepdims=True)
    return centred * lax.rsqrt(var + 1e-05)


def gate_of(values):
    return 0.5 * jnp.tanh(0.5 * values) + 0.5


def dot(values, weight):
    return jnp.dot(values, weight, preferred_element_type=jnp.float32)


def rounded(values):
    return values.astype(jnp.bfloat16).astype(jnp.float32)


def crop_kernel(
    masks,
    chains_s,
    mask_s,
    mine,
    other,
    chains_v,
    mask_v,
    bias,
    proj_w,
    gate_w,
    out_w,
    updated,
    start,
    left,
    right,
    gates,
    tris,
    left1,
    right1,
):
    ranks, rows, cols, width = mine.shape
    tokens = ranks * rows
    me = lax.axis_index("row")
    col = lax.axis_index("col")
    chunk = min(4, ranks)
    bias_v = bias[...]
    hidden = proj_w.shape[2] // 4

    for half, source in enumerate((mine, other)):
        first = pl.multiple_of(jnp.where(col == half, 0, cols), cols)
        chain_cols = chains_v[pl.ds(first, cols), :]
        mask_cols = mask_v[pl.ds(first, cols), :]
        for base in range(0, ranks, chunk):
            states, pmasks = [], []
            for slot in range(base, base + chunk):
                for t in range(rows):
                    token = (me ^ masks[slot]) * rows + t
                    same = chain_cols == chains_s[token]
                    states.append(source[slot, t] + jnp.where(same, bias_v, 0.0))
                    pmasks.append(mask_cols * mask_s[token].astype(jnp.float32))
            state = jnp.concatenate(states, 0)
            pmask = jnp.concatenate(pmasks, 0)
            start[half, pl.ds(base * rows * cols, chunk * rows * cols), :] = state
            normed = tile_norm(state).astype(jnp.bfloat16)
            proj = dot(normed, proj_w[0])
            gates[half, pl.ds(base * rows * cols, chunk * rows * cols), :] = dot(normed, gate_w[0])
            lft = rounded(gate_of(proj[:, :hidden]) * proj[:, hidden : 2 * hidden] * pmask)
            rgt = rounded(gate_of(proj[:, 2 * hidden : 3 * hidden]) * proj[:, 3 * hidden :] * pmask)
            for n in range(chunk * rows):
                k = base * rows + n
                left[pl.ds(k * tokens + half * cols, cols), :] = lft[n * cols : (n + 1) * cols]
                slot, t = divmod(k, rows)
                token = (me ^ masks[slot]) * rows + t
                right[pl.ds(half * cols * tokens + token, cols, tokens), :] = rgt[n * cols : (n + 1) * cols]

    low = me * rows // 8 * 8
    groups = [col * cols + 8 * n for n in range(cols // 8)] + [low]
    groups = [pl.multiple_of(g, 8) for g in groups]
    count = len(groups)
    block = 8

    def tri_block(step, carry):
        k0 = step * block
        acc = [[None] * count for _ in range(block)]
        for l in range(tokens):
            cells = [right[pl.ds(pl.multiple_of(l * tokens + g, 8), 8), :] for g in groups]
            for k in range(block):
                row = left[pl.ds((k0 + k) * tokens + l, 1), :]
                for n in range(count):
                    term = row * cells[n]
                    acc[k][n] = term if l == 0 else acc[k][n] + term
        for n in range(count):
            for k in range(block):
                tris[n, pl.ds(pl.multiple_of((k0 + k) * 8, 8), 8), :] = acc[k][n]
        return carry

    lax.fori_loop(0, tokens // block, tri_block, 0)

    own_half = jnp.where(low // cols == col, 0, 1)
    low_off = lax.rem(low, cols)
    mask_left = mask_v[pl.ds(pl.multiple_of(low, 8), 8), :]
    mask_right = mask_v[pl.ds(pl.multiple_of(col * cols, cols), cols), :]

    def gather(source, n, k):
        if n < count - 1:
            return source[0, pl.ds(k * cols + 8 * n, 8), :]
        return source[own_half, pl.ds(pl.multiple_of(k * cols + low_off, 8), 8), :]

    def updated_state(n):
        tri = tris[n]
        tnorm = tile_norm(tri).astype(jnp.bfloat16)
        gate = gate_of(jnp.concatenate([gather(gates, n, k) for k in range(tokens)], 0))
        state = jnp.concatenate([gather(start, n, k) for k in range(tokens)], 0)
        return state + gate * dot(tnorm, out_w[0])

    row_masks = []
    for slot in range(ranks):
        for t in range(rows):
            row_masks.append(mask_s[(me ^ masks[slot]) * rows + t].astype(jnp.float32))

    normed = tile_norm(updated_state(count - 1)).astype(jnp.bfloat16)
    proj = dot(normed, proj_w[1, :, : 2 * hidden])
    edge = gate_of(proj[:, :hidden]) * proj[:, hidden:]
    pm = jnp.concatenate([mask_left * m for m in row_masks], 0)
    left1[...] = rounded(edge * pm)

    own_state, own_logits = [], []
    for n in range(count - 1):
        state = updated_state(n)
        normed = tile_norm(state).astype(jnp.bfloat16)
        own_state.append(state[: rows * 8])
        own_logits.append(dot(normed[: rows * 8], gate_w[1]))
        proj = dot(normed, proj_w[1, :, 2 * hidden :])
        edge = gate_of(proj[:, :hidden]) * proj[:, hidden:]
        pm = jnp.concatenate([mask_right[8 * n : 8 * n + 8] * m for m in row_masks], 0)
        right1[n] = rounded(edge * pm)

    shift = lax.rem(me * rows, 8)
    acc = [[None] * (count - 1) for _ in range(rows)]
    for k in range(tokens):
        cells = [right1[n, pl.ds(k * 8, 8), :] for n in range(count - 1)]
        for t in range(rows):
            row = left1[pl.ds(k * 8 + shift + t, 1), :]
            for n in range(count - 1):
                term = row * cells[n]
                acc[t][n] = term if k == 0 else acc[t][n] + term
    for n in range(count - 1):
        tri = jnp.concatenate([acc[t][n] for t in range(rows)], 0)
        tnorm = tile_norm(tri).astype(jnp.bfloat16)
        out = own_state[n] + gate_of(own_logits[n]) * dot(tnorm, out_w[1])
        for t in range(rows):
            updated[t, pl.ds(8 * n, 8), :] = out[8 * t : 8 * t + 8]


def exchange(block, bits):
    ranks = lax.axis_size("row")
    return lax.ppermute(block, "row", [(i, i ^ bits) for i in range(ranks)])


def whole_crop_plan(pair, token_mask, chains, chain_bias, proj_weight, gate_weight, out_weight):
    rows, cols, width = pair.shape
    ranks = lax.axis_size("row")
    tokens = token_mask.shape[0]
    hidden = proj_weight.shape[2] // 4
    top = ranks // 2
    two = jnp.stack([pair, exchange(pair, top)])
    masks = [0, top]
    parts = [two]
    for bits in list(range(top - 1, 0, -1)):
        parts.append(exchange(two, bits))
        masks += [bits, bits ^ top]
    mine = jnp.concatenate(parts, 0)
    other = lax.ppermute(mine, "col", [(0, 1), (1, 0)])
    chains_v = jnp.broadcast_to(chains[:, None], (tokens, width))
    mask_v = jnp.broadcast_to(token_mask.astype(jnp.float32)[:, None], (tokens, width))
    groups = cols // 8 + 1
    smem = pl.BlockSpec(memory_space=pltpu.SMEM)
    vmem = pl.BlockSpec(memory_space=pltpu.VMEM)
    return pl.pallas_call(
        functools.partial(crop_kernel, masks),
        out_shape=jax.ShapeDtypeStruct(pair.shape, jnp.float32),
        in_specs=[smem, smem] + [vmem] * 8,
        out_specs=vmem,
        scratch_shapes=[
            pltpu.VMEM((2, tokens * cols, width), jnp.float32),
            pltpu.VMEM((tokens * tokens, hidden), jnp.float32),
            pltpu.VMEM((tokens * tokens, hidden), jnp.float32),
            pltpu.VMEM((2, tokens * cols, width), jnp.float32),
            pltpu.VMEM((groups, tokens * 8, hidden), jnp.float32),
            pltpu.VMEM((tokens * 8, hidden), jnp.float32),
            pltpu.VMEM((groups - 1, tokens * 8, hidden), jnp.float32),
        ],
        compiler_params=pltpu.CompilerParams(vmem_limit_bytes=32 << 20),
        name="crop",
    )(chains, token_mask, mine, other, chains_v, mask_v, chain_bias[None, :], proj_weight, gate_weight, out_weight)


def shards(pair, token_mask, *rest):
    tokens = token_mask.shape[0]
    ranks = lax.axis_size("row")
    small = tokens * tokens * pair.shape[2] <= 1 << 18 and ranks & (ranks - 1) == 0 and tokens % 16 == 0
    plan = whole_crop_plan if small and lax.axis_size("col") == 2 else sharded_plan
    return plan(pair, token_mask, *rest)


def solution(mesh):
    placed = (P(("group", "row"), "col", None), P("group"), P("group"), P(), P(), P(), P())
    return jax.shard_map(
        shards,
        mesh=mesh,
        in_specs=placed,
        out_specs=P(("group", "row"), "col", None),
        check_vma=False,
    )
```

```python
import functools
import jax
import jax.numpy as jnp
from jax import lax
from jax.experimental import pallas as pl
from jax.experimental.pallas import tpu as pltpu
from jax.sharding import PartitionSpec as P


def layer_norm(values):
    mean = jnp.mean(values, -1, keepdims=True)
    centred = values - mean
    var = jnp.mean(centred * centred, -1, keepdims=True)
    return centred * lax.rsqrt(var + 1e-05)


def flat_dot(values, weight):
    shape = values.shape
    result = jnp.dot(values.reshape(-1, shape[-1]), weight, preferred_element_type=jnp.float32)
    return result.reshape(shape[:-1] + (weight.shape[1],))


def project(state, pmask, p_weight):
    normed = layer_norm(state).astype(jnp.bfloat16)
    proj = flat_dot(normed, p_weight)
    hidden = p_weight.shape[1] // 4
    gate_a = proj[..., :hidden]
    value_a = proj[..., hidden : 2 * hidden]
    gate_b = proj[..., 2 * hidden : 3 * hidden]
    value_b = proj[..., 3 * hidden :]
    left = (jax.nn.sigmoid(gate_a) * value_a * pmask[..., None]).astype(jnp.bfloat16)
    right = (jax.nn.sigmoid(gate_b) * value_b * pmask[..., None]).astype(jnp.bfloat16)
    return (normed, left, right)


def finish(state, normed, tri, g_weight, o_weight):
    tnorm = layer_norm(tri).astype(jnp.bfloat16)
    gate = jax.nn.sigmoid(flat_dot(normed, g_weight))
    return state + gate * flat_dot(tnorm, o_weight)


def sharded_plan(pair, token_mask, chains, chain_bias, proj_weight, gate_weight, out_weight):
    rows, cols, width = pair.shape
    row_start = lax.axis_index("row") * rows
    col_start = lax.axis_index("col") * cols
    chain_rows = lax.dynamic_slice_in_dim(chains, row_start, rows)
    chain_cols = lax.dynamic_slice_in_dim(chains, col_start, cols)
    mask_rows = lax.dynamic_slice_in_dim(token_mask, row_start, rows).astype(jnp.float32)
    mask_cols = lax.dynamic_slice_in_dim(token_mask, col_start, cols).astype(jnp.float32)
    same = (chain_rows[:, None] == chain_cols[None, :]).astype(jnp.float32)
    state = pair + same[..., None] * chain_bias
    pmask = mask_rows[:, None] * mask_cols[None, :]
    normed, left, right = project(state, pmask, proj_weight[0])
    left_rows, right_rows = (
        lax.all_gather(left, "col", axis=1, tiled=True),
        lax.all_gather(right, "col", axis=1, tiled=True),
    )
    every = jnp.einsum(
        "ikh,jkh->ijh",
        left_rows,
        lax.all_gather(right_rows, "row", axis=0, tiled=True),
        preferred_element_type=jnp.float32,
    )
    tri = lax.dynamic_slice_in_dim(every, col_start, cols, 1)
    state = finish(state, normed, tri, gate_weight[0], out_weight[0])
    normed, left, right = project(state, pmask, proj_weight[1])
    left_rows = lax.all_gather(left, "col", axis=1, tiled=True)
    left_cols = lax.all_to_all(left_rows, "row", split_axis=1, concat_axis=0, tiled=True)
    tri = jnp.einsum(
        "kih,kjh->ijh",
        left_cols,
        lax.all_gather(right, "row", axis=0, tiled=True),
        preferred_element_type=jnp.float32,
    )
    return finish(state, normed, tri, gate_weight[1], out_weight[1])


def tile_norm(values):
    mean = jnp.mean(values, -1, keepdims=True)
    centred = values - mean
    var = jnp.mean(centred * centred, -1, keepdims=True)
    return centred * lax.rsqrt(var + 1e-05)


def gate_of(values):
    return 0.5 * jnp.tanh(0.5 * values) + 0.5


def dot(values, weight):
    return jnp.dot(values, weight, preferred_element_type=jnp.float32)


def rounded(values):
    return values.astype(jnp.bfloat16).astype(jnp.float32)


def table(row, out):
    tokens, width = out.shape
    at = lax.broadcasted_iota(jnp.int32, (tokens, tokens), 0)
    lane = lax.broadcasted_iota(jnp.int32, (tokens, tokens), 1)
    spread = jnp.where(at == lane, jnp.broadcast_to(row[...].astype(jnp.float32), (tokens, tokens)), 0.0)
    out[...] = jnp.broadcast_to(jnp.sum(spread, -1, keepdims=True), (tokens, width))


def edges(masks, slots, half_start, source, chains, mask, bias, proj_w, gate_w, start, gates, left, right):
    rows, cols, width = source.shape[-3:]
    tokens = chains.shape[0]
    me = lax.axis_index("row")
    chunk = min(4, len(slots))
    bias_v = bias[...]
    hidden = proj_w.shape[2] // 4
    half_start = pl.multiple_of(half_start, cols)
    chain_cols = chains[pl.ds(half_start, cols), :]
    mask_cols = mask[pl.ds(half_start, cols), :]
    for at in range(0, len(slots), chunk):
        base, chunk_slots = slots[at], slots[at : at + chunk]
        states, pmasks = [], []
        for slot in chunk_slots:
            for t in range(rows):
                token = (me ^ masks[slot]) * rows + t
                same = chain_cols == chains[pl.ds(token, 1), :]
                cell = source[slot, t] if len(source.shape) == 4 else source[t]
                states.append(cell + jnp.where(same, bias_v, 0.0))
                pmasks.append(mask_cols * mask[pl.ds(token, 1), :])
        state = jnp.concatenate(states, 0)
        pmask = jnp.concatenate(pmasks, 0)
        count = len(chunk_slots) * rows
        span = pl.ds(base * rows * cols, count * cols)
        start[span, :] = state
        normed = tile_norm(state).astype(jnp.bfloat16)
        proj = dot(normed, proj_w[0])
        gates[span, :] = dot(normed, gate_w[0])
        left[span, :] = rounded(gate_of(proj[:, :hidden]) * proj[:, hidden : 2 * hidden] * pmask)
        rgt = rounded(gate_of(proj[:, 2 * hidden : 3 * hidden]) * proj[:, 3 * hidden :] * pmask)
        for n in range(count):
            slot, t = divmod(base * rows + n, rows)
            token = (me ^ masks[slot]) * rows + t
            right[pl.ds(token, cols, tokens), :] = rgt[n * cols : (n + 1) * cols]


def own_kernel(masks, *refs):
    pair, chains_row, mask_row, bias, proj_w, gate_w, out_w = refs[:7]
    bias_v, proj_v, gate_v, out_v, copied, chains, mask, start, gates, left, right, chains_v, mask_v, sems = refs[7:]
    loads = [
        pltpu.make_async_copy(source, target, sems.at[n])
        for n, (source, target) in enumerate(
            (
                (pair, copied),
                (chains_row, chains_v),
                (mask_row, mask_v),
                (bias, bias_v),
                (proj_w, proj_v),
                (gate_w, gate_v),
                (out_w, out_v),
            )
        )
    ]
    for load in loads:
        load.start()
    for load in loads:
        load.wait()
    table(chains_v, chains)
    table(mask_v, mask)
    half_start = lax.axis_index("col") * copied.shape[1]
    edges(masks, [0], half_start, copied, chains, mask, bias_v, proj_v, gate_v, start, gates, left, right)


def mine_kernel(masks, mine, chains, mask, bias, proj_w, gate_w, s_in, g_in, l_in, r_in, start, gates, left, right):
    half_start = lax.axis_index("col") * mine.shape[2]
    slots = list(range(1, mine.shape[0]))
    edges(masks, slots, half_start, mine, chains, mask, bias, proj_w, gate_w, start, gates, left, right)


def second_kernel(
    masks,
    other,
    chains,
    mask,
    bias,
    proj_w,
    gate_w,
    out_w,
    start_m,
    gates_m,
    left_m,
    right_m,
    updated,
    start_o,
    gates_o,
    left_o,
    right_o,
    tris,
    left1,
    right1,
):
    ranks, rows, cols, width = other.shape
    tokens = ranks * rows
    me = lax.axis_index("row")
    col = lax.axis_index("col")
    hidden = proj_w.shape[2] // 4
    edges(masks, list(range(ranks)), (1 - col) * cols, other, chains, mask, bias, proj_w, gate_w, start_o, gates_o, left_o, right_o)

    low = me * rows // 8 * 8
    groups = [col * cols + 8 * n for n in range(cols // 8)] + [low]
    groups = [pl.multiple_of(g, 8) for g in groups]
    count = len(groups)
    block = 8

    def tri_block(step, carry):
        k0 = step * block
        acc = [[None] * count for _ in range(block)]
        for half, (left, right) in enumerate(((left_m, right_m), (left_o, right_o))):
            for l in range(cols):
                cells = [right[pl.ds(pl.multiple_of(l * tokens + g, 8), 8), :] for g in groups]
                for k in range(block):
                    row = left[pl.ds((k0 + k) * cols + l, 1), :]
                    for n in range(count):
                        term = row * cells[n]
                        acc[k][n] = term if half + l == 0 else acc[k][n] + term
        for n in range(count):
            for k in range(block):
                tris[n, pl.ds(pl.multiple_of((k0 + k) * 8, 8), 8), :] = acc[k][n]
        return carry

    lax.fori_loop(0, tokens // block, tri_block, 0)

    low_mine = low // cols == col
    low_off = lax.rem(low, cols)
    mask_left = mask[pl.ds(pl.multiple_of(low, 8), 8), :]
    mask_right = mask[pl.ds(pl.multiple_of(col * cols, cols), cols), :]

    def gather(mine, other, n, k):
        if n < count - 1:
            return mine[pl.ds(k * cols + 8 * n, 8), :]
        span = pl.ds(pl.multiple_of(k * cols + low_off, 8), 8)
        return jnp.where(low_mine, mine[span, :], other[span, :])

    def updated_state(n):
        tri = tris[n]
        tnorm = tile_norm(tri).astype(jnp.bfloat16)
        gate = gate_of(jnp.concatenate([gather(gates_m, gates_o, n, k) for k in range(tokens)], 0))
        state = jnp.concatenate([gather(start_m, start_o, n, k) for k in range(tokens)], 0)
        return state + gate * dot(tnorm, out_w[0])

    row_masks = []
    for slot in range(ranks):
        for t in range(rows):
            row_masks.append(mask[pl.ds((me ^ masks[slot]) * rows + t, 1), :])

    normed = tile_norm(updated_state(count - 1)).astype(jnp.bfloat16)
    proj = dot(normed, proj_w[1, :, : 2 * hidden])
    edge = gate_of(proj[:, :hidden]) * proj[:, hidden:]
    pm = jnp.concatenate([mask_left * m for m in row_masks], 0)
    left1[...] = rounded(edge * pm)

    own_state, own_logits = [], []
    for n in range(count - 1):
        state = updated_state(n)
        normed = tile_norm(state).astype(jnp.bfloat16)
        own_state.append(state[: rows * 8])
        own_logits.append(dot(normed[: rows * 8], gate_w[1]))
        proj = dot(normed, proj_w[1, :, 2 * hidden :])
        edge = gate_of(proj[:, :hidden]) * proj[:, hidden:]
        pm = jnp.concatenate([mask_right[8 * n : 8 * n + 8] * m for m in row_masks], 0)
        right1[n] = rounded(edge * pm)

    shift = lax.rem(me * rows, 8)
    acc = [[None] * (count - 1) for _ in range(rows)]
    for k in range(tokens):
        cells = [right1[n, pl.ds(k * 8, 8), :] for n in range(count - 1)]
        for t in range(rows):
            row = left1[pl.ds(k * 8 + shift + t, 1), :]
            for n in range(count - 1):
                term = row * cells[n]
                acc[t][n] = term if k == 0 else acc[t][n] + term
    for n in range(count - 1):
        tri = jnp.concatenate([acc[t][n] for t in range(rows)], 0)
        tnorm = tile_norm(tri).astype(jnp.bfloat16)
        out = own_state[n] + gate_of(own_logits[n]) * dot(tnorm, out_w[1])
        for t in range(rows):
            updated[t, pl.ds(8 * n, 8), :] = out[8 * t : 8 * t + 8]


def exchange(block, bits):
    ranks = lax.axis_size("row")
    return lax.ppermute(block, "row", [(i, i ^ bits) for i in range(ranks)])


def call(body, inputs, outputs, scratch, name, flops, aliases={}, space=pltpu.VMEM):
    return pl.pallas_call(
        body,
        out_shape=outputs,
        in_specs=[pl.BlockSpec(memory_space=space)] * len(inputs),
        out_specs=[pl.BlockSpec(memory_space=pltpu.VMEM)] * len(outputs),
        scratch_shapes=scratch,
        compiler_params=pltpu.CompilerParams(vmem_limit_bytes=32 << 20),
        input_output_aliases=aliases,
        cost_estimate=pl.CostEstimate(flops=flops, bytes_accessed=1 << 21, transcendentals=0),
        name=name,
    )(*inputs)


def floats(*shapes):
    return [jax.ShapeDtypeStruct(shape, jnp.float32) for shape in shapes]


def like(*arrays):
    return [jax.ShapeDtypeStruct(array.shape, array.dtype) for array in arrays]


def whole_crop_plan(pair, token_mask, chains, chain_bias, proj_weight, gate_weight, out_weight):
    rows, cols, width = pair.shape
    ranks = lax.axis_size("row")
    tokens = token_mask.shape[0]
    hidden = proj_weight.shape[2] // 4
    bias = chain_bias[None, :]
    half = floats((tokens * cols, width), (tokens * cols, width), (tokens * cols, hidden), (tokens * cols, hidden))
    flops = 2 * tokens * cols * width * 5 * hidden
    top = ranks // 2
    masks = [0, top]
    for bits in range(top - 1, 0, -1):
        masks += [bits, bits ^ top]
    far = exchange(pair, top)
    own_inputs = (pair, chains[None, :], token_mask[None, :], bias, proj_weight, gate_weight, out_weight)
    own_inputs = [pltpu.with_memory_space_constraint(each, pltpu.HBM) for each in own_inputs]
    bias, proj_weight, gate_weight, out_weight, own, chains_t, mask_t, *partial = call(
        functools.partial(own_kernel, masks),
        own_inputs,
        like(bias, proj_weight, gate_weight, out_weight, pair) + floats((tokens, width), (tokens, width)) + half,
        [pltpu.VMEM((1, tokens), jnp.int32), pltpu.VMEM((1, tokens), jnp.int32), pltpu.SemaphoreType.DMA((7,))],
        "own",
        flops // ranks,
        space=pltpu.HBM,
    )
    two = jnp.stack([own, far])
    mine = jnp.concatenate([two] + [exchange(two, bits) for bits in range(top - 1, 0, -1)], 0)
    other = lax.ppermute(mine, "col", [(0, 1), (1, 0)])
    mine_edges = call(
        functools.partial(mine_kernel, masks),
        (mine, chains_t, mask_t, bias, proj_weight, gate_weight, *partial),
        half,
        [],
        "mine",
        flops,
        {6: 0, 7: 1, 8: 2, 9: 3},
    )
    groups = cols // 8 + 1
    extra = [(groups, tokens * 8, hidden), (tokens * 8, hidden), (groups - 1, tokens * 8, hidden)]
    return call(
        functools.partial(second_kernel, masks),
        (other, chains_t, mask_t, bias, proj_weight, gate_weight, out_weight, *mine_edges),
        floats(pair.shape),
        [pltpu.VMEM(each.shape, jnp.float32) for each in half + floats(*extra)],
        "crop",
        4 * flops,
    )[0]


def shards(pair, token_mask, *rest):
    tokens = token_mask.shape[0]
    ranks = lax.axis_size("row")
    small = tokens * tokens * pair.shape[2] <= 1 << 18 and ranks & (ranks - 1) == 0 and tokens % 16 == 0
    plan = whole_crop_plan if small and lax.axis_size("col") == 2 else sharded_plan
    return plan(pair, token_mask, *rest)


def solution(mesh):
    placed = (P(("group", "row"), "col", None), P("group"), P("group"), P(), P(), P(), P())
    return jax.shard_map(
        shards,
        mesh=mesh,
        in_specs=placed,
        out_specs=P(("group", "row"), "col", None),
        check_vma=False,
    )
```

```python
import functools
import jax
import jax.numpy as jnp
from jax import lax
from jax.experimental import pallas as pl
from jax.experimental.pallas import tpu as pltpu
from jax.sharding import PartitionSpec as P


def layer_norm(values):
    mean = jnp.mean(values, -1, keepdims=True)
    centred = values - mean
    var = jnp.mean(centred * centred, -1, keepdims=True)
    return centred * lax.rsqrt(var + 1e-05)


def flat_dot(values, weight):
    shape = values.shape
    result = jnp.dot(values.reshape(-1, shape[-1]), weight, preferred_element_type=jnp.float32)
    return result.reshape(shape[:-1] + (weight.shape[1],))


def project(state, pmask, p_weight):
    normed = layer_norm(state).astype(jnp.bfloat16)
    proj = flat_dot(normed, p_weight)
    hidden = p_weight.shape[1] // 4
    gate_a = proj[..., :hidden]
    value_a = proj[..., hidden : 2 * hidden]
    gate_b = proj[..., 2 * hidden : 3 * hidden]
    value_b = proj[..., 3 * hidden :]
    left = (jax.nn.sigmoid(gate_a) * value_a * pmask[..., None]).astype(jnp.bfloat16)
    right = (jax.nn.sigmoid(gate_b) * value_b * pmask[..., None]).astype(jnp.bfloat16)
    return (normed, left, right)


def finish(state, normed, tri, g_weight, o_weight):
    tnorm = layer_norm(tri).astype(jnp.bfloat16)
    gate = jax.nn.sigmoid(flat_dot(normed, g_weight))
    return state + gate * flat_dot(tnorm, o_weight)


def sharded_plan(pair, token_mask, chains, chain_bias, proj_weight, gate_weight, out_weight):
    rows, cols, width = pair.shape
    row_start = lax.axis_index("row") * rows
    col_start = lax.axis_index("col") * cols
    chain_rows = lax.dynamic_slice_in_dim(chains, row_start, rows)
    chain_cols = lax.dynamic_slice_in_dim(chains, col_start, cols)
    mask_rows = lax.dynamic_slice_in_dim(token_mask, row_start, rows).astype(jnp.float32)
    mask_cols = lax.dynamic_slice_in_dim(token_mask, col_start, cols).astype(jnp.float32)
    same = (chain_rows[:, None] == chain_cols[None, :]).astype(jnp.float32)
    state = pair + same[..., None] * chain_bias
    pmask = mask_rows[:, None] * mask_cols[None, :]
    normed, left, right = project(state, pmask, proj_weight[0])
    left_rows, right_rows = (
        lax.all_gather(left, "col", axis=1, tiled=True),
        lax.all_gather(right, "col", axis=1, tiled=True),
    )
    every = jnp.einsum(
        "ikh,jkh->ijh",
        left_rows,
        lax.all_gather(right_rows, "row", axis=0, tiled=True),
        preferred_element_type=jnp.float32,
    )
    tri = lax.dynamic_slice_in_dim(every, col_start, cols, 1)
    state = finish(state, normed, tri, gate_weight[0], out_weight[0])
    normed, left, right = project(state, pmask, proj_weight[1])
    left_rows = lax.all_gather(left, "col", axis=1, tiled=True)
    left_cols = lax.all_to_all(left_rows, "row", split_axis=1, concat_axis=0, tiled=True)
    tri = jnp.einsum(
        "kih,kjh->ijh",
        left_cols,
        lax.all_gather(right, "row", axis=0, tiled=True),
        preferred_element_type=jnp.float32,
    )
    return finish(state, normed, tri, gate_weight[1], out_weight[1])


def tile_norm(values):
    mean = jnp.mean(values, -1, keepdims=True)
    centred = values - mean
    var = jnp.mean(centred * centred, -1, keepdims=True)
    return centred * lax.rsqrt(var + 1e-05)


def gate_of(values):
    return 0.5 * jnp.tanh(0.5 * values) + 0.5


def dot(values, weight):
    return jnp.dot(values, weight, preferred_element_type=jnp.float32)


def rounded(values):
    return values.astype(jnp.bfloat16).astype(jnp.float32)


def table(row, out):
    tokens, width = out.shape
    at = lax.broadcasted_iota(jnp.int32, (tokens, tokens), 0)
    lane = lax.broadcasted_iota(jnp.int32, (tokens, tokens), 1)
    spread = jnp.where(at == lane, jnp.broadcast_to(row[...].astype(jnp.float32), (tokens, tokens)), 0.0)
    out[...] = jnp.broadcast_to(jnp.sum(spread, -1, keepdims=True), (tokens, width))


def edges(masks, slots, half_start, source, chains, mask, bias, proj_w, gate_w, start, gates, left, right):
    rows, cols, width = source.shape[-3:]
    tokens = chains.shape[0]
    me = lax.axis_index("row")
    chunk = min(4, len(slots))
    bias_v = bias[...]
    hidden = proj_w.shape[2] // 4
    half_start = pl.multiple_of(half_start, cols)
    chain_cols = chains[pl.ds(half_start, cols), :]
    mask_cols = mask[pl.ds(half_start, cols), :]
    for at in range(0, len(slots), chunk):
        base, chunk_slots = slots[at], slots[at : at + chunk]
        states, pmasks = [], []
        for slot in chunk_slots:
            for t in range(rows):
                token = (me ^ masks[slot]) * rows + t
                same = chain_cols == chains[pl.ds(token, 1), :]
                cell = source[slot, t] if len(source.shape) == 4 else source[t]
                states.append(cell + jnp.where(same, bias_v, 0.0))
                pmasks.append(mask_cols * mask[pl.ds(token, 1), :])
        state = jnp.concatenate(states, 0)
        pmask = jnp.concatenate(pmasks, 0)
        count = len(chunk_slots) * rows
        span = pl.ds(base * rows * cols, count * cols)
        start[span, :] = state
        normed = tile_norm(state).astype(jnp.bfloat16)
        proj = dot(normed, proj_w[0])
        gates[span, :] = dot(normed, gate_w[0])
        left[span, :] = rounded(gate_of(proj[:, :hidden]) * proj[:, hidden : 2 * hidden] * pmask)
        rgt = rounded(gate_of(proj[:, 2 * hidden : 3 * hidden]) * proj[:, 3 * hidden :] * pmask)
        for n in range(count):
            slot, t = divmod(base * rows + n, rows)
            token = (me ^ masks[slot]) * rows + t
            right[pl.ds(token, cols, tokens), :] = rgt[n * cols : (n + 1) * cols]


def own_kernel(masks, *refs):
    pair, chains_row, mask_row, bias, proj_w, gate_w, out_w = refs[:7]
    bias_v, proj_v, gate_v, out_v, copied, chains, mask, start, gates, left, right, chains_v, mask_v, sems = refs[7:]
    loads = [
        pltpu.make_async_copy(source, target, sems.at[n])
        for n, (source, target) in enumerate(
            (
                (pair, copied),
                (chains_row, chains_v),
                (mask_row, mask_v),
                (bias, bias_v),
                (proj_w, proj_v),
                (gate_w, gate_v),
                (out_w, out_v),
            )
        )
    ]
    for load in loads:
        load.start()
    for load in loads:
        load.wait()
    table(chains_v, chains)
    table(mask_v, mask)
    half_start = lax.axis_index("col") * copied.shape[1]
    edges(masks, [0], half_start, copied, chains, mask, bias_v, proj_v, gate_v, start, gates, left, right)


def mine_kernel(masks, mine, chains, mask, bias, proj_w, gate_w, s_in, g_in, l_in, r_in, start, gates, left, right):
    half_start = lax.axis_index("col") * mine.shape[2]
    slots = list(range(1, mine.shape[0]))
    edges(masks, slots, half_start, mine, chains, mask, bias, proj_w, gate_w, start, gates, left, right)


def second_kernel(
    masks,
    other,
    chains,
    mask,
    bias,
    proj_w,
    gate_w,
    out_w,
    start_m,
    gates_m,
    left_m,
    right_m,
    updated,
    start_o,
    gates_o,
    left_o,
    right_o,
    tris,
    left1,
    right1,
):
    ranks, rows, cols, width = other.shape
    tokens = ranks * rows
    me = lax.axis_index("row")
    col = lax.axis_index("col")
    hidden = proj_w.shape[2] // 4
    edges(masks, list(range(ranks)), (1 - col) * cols, other, chains, mask, bias, proj_w, gate_w, start_o, gates_o, left_o, right_o)

    low = me * rows // 8 * 8
    groups = [col * cols + 8 * n for n in range(cols // 8)] + [low]
    groups = [pl.multiple_of(g, 8) for g in groups]
    count = len(groups)
    block = 8

    def tri_block(step, carry):
        k0 = step * block
        acc = [[None] * count for _ in range(block)]
        for half, (left, right) in enumerate(((left_m, right_m), (left_o, right_o))):
            for l in range(cols):
                cells = [right[pl.ds(pl.multiple_of(l * tokens + g, 8), 8), :] for g in groups]
                for k in range(block):
                    row = left[pl.ds((k0 + k) * cols + l, 1), :]
                    for n in range(count):
                        term = row * cells[n]
                        acc[k][n] = term if half + l == 0 else acc[k][n] + term
        for n in range(count):
            for k in range(block):
                tris[n, pl.ds(pl.multiple_of((k0 + k) * 8, 8), 8), :] = acc[k][n]
        return carry

    lax.fori_loop(0, tokens // block, tri_block, 0)

    low_mine = low // cols == col
    low_off = lax.rem(low, cols)
    mask_left = mask[pl.ds(pl.multiple_of(low, 8), 8), :]
    mask_right = mask[pl.ds(pl.multiple_of(col * cols, cols), cols), :]

    def gather(mine, other, n, k):
        if n < count - 1:
            return mine[pl.ds(k * cols + 8 * n, 8), :]
        span = pl.ds(pl.multiple_of(k * cols + low_off, 8), 8)
        return jnp.where(low_mine, mine[span, :], other[span, :])

    def updated_state(n):
        tri = tris[n]
        tnorm = tile_norm(tri).astype(jnp.bfloat16)
        gate = gate_of(jnp.concatenate([gather(gates_m, gates_o, n, k) for k in range(tokens)], 0))
        state = jnp.concatenate([gather(start_m, start_o, n, k) for k in range(tokens)], 0)
        return state + gate * dot(tnorm, out_w[0])

    row_masks = []
    for slot in range(ranks):
        for t in range(rows):
            row_masks.append(mask[pl.ds((me ^ masks[slot]) * rows + t, 1), :])

    normed = tile_norm(updated_state(count - 1)).astype(jnp.bfloat16)
    proj = dot(normed, proj_w[1, :, : 2 * hidden])
    edge = gate_of(proj[:, :hidden]) * proj[:, hidden:]
    pm = jnp.concatenate([mask_left * m for m in row_masks], 0)
    left1[...] = rounded(edge * pm)

    own_state, own_logits = [], []
    for n in range(count - 1):
        state = updated_state(n)
        normed = tile_norm(state).astype(jnp.bfloat16)
        own_state.append(state[: rows * 8])
        own_logits.append(dot(normed[: rows * 8], gate_w[1]))
        proj = dot(normed, proj_w[1, :, 2 * hidden :])
        edge = gate_of(proj[:, :hidden]) * proj[:, hidden:]
        pm = jnp.concatenate([mask_right[8 * n : 8 * n + 8] * m for m in row_masks], 0)
        right1[n] = rounded(edge * pm)

    shift = lax.rem(me * rows, 8)
    acc = [[None] * (count - 1) for _ in range(rows)]
    for k in range(tokens):
        cells = [right1[n, pl.ds(k * 8, 8), :] for n in range(count - 1)]
        for t in range(rows):
            row = left1[pl.ds(k * 8 + shift + t, 1), :]
            for n in range(count - 1):
                term = row * cells[n]
                acc[t][n] = term if k == 0 else acc[t][n] + term
    for n in range(count - 1):
        tri = jnp.concatenate([acc[t][n] for t in range(rows)], 0)
        tnorm = tile_norm(tri).astype(jnp.bfloat16)
        out = own_state[n] + gate_of(own_logits[n]) * dot(tnorm, out_w[1])
        for t in range(rows):
            updated[t, pl.ds(8 * n, 8), :] = out[8 * t : 8 * t + 8]


def exchange(block, bits):
    ranks = lax.axis_size("row")
    return lax.ppermute(block, "row", [(i, i ^ bits) for i in range(ranks)])


def call(body, inputs, outputs, scratch, name, flops, aliases={}, space=pltpu.VMEM):
    return pl.pallas_call(
        body,
        out_shape=outputs,
        in_specs=[pl.BlockSpec(memory_space=space)] * len(inputs),
        out_specs=[pl.BlockSpec(memory_space=pltpu.VMEM)] * len(outputs),
        scratch_shapes=scratch,
        compiler_params=pltpu.CompilerParams(vmem_limit_bytes=32 << 20),
        input_output_aliases=aliases,
        cost_estimate=pl.CostEstimate(flops=flops, bytes_accessed=1 << 21, transcendentals=0),
        name=name,
    )(*inputs)


def floats(*shapes):
    return [jax.ShapeDtypeStruct(shape, jnp.float32) for shape in shapes]


def like(*arrays):
    return [jax.ShapeDtypeStruct(array.shape, array.dtype) for array in arrays]


def whole_crop_plan(pair, token_mask, chains, chain_bias, proj_weight, gate_weight, out_weight):
    rows, cols, width = pair.shape
    ranks = lax.axis_size("row")
    tokens = token_mask.shape[0]
    hidden = proj_weight.shape[2] // 4
    bias = chain_bias[None, :]
    half = floats((tokens * cols, width), (tokens * cols, width), (tokens * cols, hidden), (tokens * cols, hidden))
    flops = 2 * tokens * cols * width * 5 * hidden
    masks = [0] + sorted(range(1, ranks), key=lambda bits: -(bits ^ bits >> 1))
    own_inputs = (pair, chains[None, :], token_mask[None, :], bias, proj_weight, gate_weight, out_weight)
    own_inputs = [pltpu.with_memory_space_constraint(each, pltpu.HBM) for each in own_inputs]
    bias, proj_weight, gate_weight, out_weight, own, chains_t, mask_t, *partial = call(
        functools.partial(own_kernel, masks),
        own_inputs,
        like(bias, proj_weight, gate_weight, out_weight, pair) + floats((tokens, width), (tokens, width)) + half,
        [pltpu.VMEM((1, tokens), jnp.int32), pltpu.VMEM((1, tokens), jnp.int32), pltpu.SemaphoreType.DMA((7,))],
        "own",
        flops // ranks,
        space=pltpu.HBM,
    )
    mine = jnp.stack([own] + [exchange(pair, bits) for bits in masks[1:]])
    other = lax.ppermute(mine, "col", [(0, 1), (1, 0)])
    mine_edges = call(
        functools.partial(mine_kernel, masks),
        (mine, chains_t, mask_t, bias, proj_weight, gate_weight, *partial),
        half,
        [],
        "mine",
        flops,
        {6: 0, 7: 1, 8: 2, 9: 3},
    )
    groups = cols // 8 + 1
    extra = [(groups, tokens * 8, hidden), (tokens * 8, hidden), (groups - 1, tokens * 8, hidden)]
    return call(
        functools.partial(second_kernel, masks),
        (other, chains_t, mask_t, bias, proj_weight, gate_weight, out_weight, *mine_edges),
        floats(pair.shape),
        [pltpu.VMEM(each.shape, jnp.float32) for each in half + floats(*extra)],
        "crop",
        4 * flops,
    )[0]


def shards(pair, token_mask, *rest):
    tokens = token_mask.shape[0]
    ranks = lax.axis_size("row")
    small = tokens * tokens * pair.shape[2] <= 1 << 18 and ranks & (ranks - 1) == 0 and tokens % 16 == 0
    plan = whole_crop_plan if small and lax.axis_size("col") == 2 else sharded_plan
    return plan(pair, token_mask, *rest)


def solution(mesh):
    placed = (P(("group", "row"), "col", None), P("group"), P("group"), P(), P(), P(), P())
    return jax.shard_map(
        shards,
        mesh=mesh,
        in_specs=placed,
        out_specs=P(("group", "row"), "col", None),
        check_vma=False,
    )
```

```python
import functools
import jax
import jax.numpy as jnp
from jax import lax
from jax.experimental import pallas as pl
from jax.experimental.pallas import tpu as pltpu
from jax.sharding import PartitionSpec as P


def layer_norm(values):
    mean = jnp.mean(values, -1, keepdims=True)
    centred = values - mean
    var = jnp.mean(centred * centred, -1, keepdims=True)
    return centred * lax.rsqrt(var + 1e-05)


def flat_dot(values, weight):
    shape = values.shape
    result = jnp.dot(values.reshape(-1, shape[-1]), weight, preferred_element_type=jnp.float32)
    return result.reshape(shape[:-1] + (weight.shape[1],))


def project(state, pmask, p_weight):
    normed = layer_norm(state).astype(jnp.bfloat16)
    proj = flat_dot(normed, p_weight)
    hidden = p_weight.shape[1] // 4
    gate_a = proj[..., :hidden]
    value_a = proj[..., hidden : 2 * hidden]
    gate_b = proj[..., 2 * hidden : 3 * hidden]
    value_b = proj[..., 3 * hidden :]
    left = (jax.nn.sigmoid(gate_a) * value_a * pmask[..., None]).astype(jnp.bfloat16)
    right = (jax.nn.sigmoid(gate_b) * value_b * pmask[..., None]).astype(jnp.bfloat16)
    return (normed, left, right)


def finish(state, normed, tri, g_weight, o_weight):
    tnorm = layer_norm(tri).astype(jnp.bfloat16)
    gate = jax.nn.sigmoid(flat_dot(normed, g_weight))
    return state + gate * flat_dot(tnorm, o_weight)


def sharded_plan(pair, token_mask, chains, chain_bias, proj_weight, gate_weight, out_weight):
    rows, cols, width = pair.shape
    row_start = lax.axis_index("row") * rows
    col_start = lax.axis_index("col") * cols
    chain_rows = lax.dynamic_slice_in_dim(chains, row_start, rows)
    chain_cols = lax.dynamic_slice_in_dim(chains, col_start, cols)
    mask_rows = lax.dynamic_slice_in_dim(token_mask, row_start, rows).astype(jnp.float32)
    mask_cols = lax.dynamic_slice_in_dim(token_mask, col_start, cols).astype(jnp.float32)
    same = (chain_rows[:, None] == chain_cols[None, :]).astype(jnp.float32)
    state = pair + same[..., None] * chain_bias
    pmask = mask_rows[:, None] * mask_cols[None, :]
    normed, left, right = project(state, pmask, proj_weight[0])
    left_rows, right_rows = (
        lax.all_gather(left, "col", axis=1, tiled=True),
        lax.all_gather(right, "col", axis=1, tiled=True),
    )
    every = jnp.einsum(
        "ikh,jkh->ijh",
        left_rows,
        lax.all_gather(right_rows, "row", axis=0, tiled=True),
        preferred_element_type=jnp.float32,
    )
    tri = lax.dynamic_slice_in_dim(every, col_start, cols, 1)
    state = finish(state, normed, tri, gate_weight[0], out_weight[0])
    normed, left, right = project(state, pmask, proj_weight[1])
    left_rows = lax.all_gather(left, "col", axis=1, tiled=True)
    left_cols = lax.all_to_all(left_rows, "row", split_axis=1, concat_axis=0, tiled=True)
    tri = jnp.einsum(
        "kih,kjh->ijh",
        left_cols,
        lax.all_gather(right, "row", axis=0, tiled=True),
        preferred_element_type=jnp.float32,
    )
    return finish(state, normed, tri, gate_weight[1], out_weight[1])


def tile_norm(values):
    mean = jnp.mean(values, -1, keepdims=True)
    centred = values - mean
    var = jnp.mean(centred * centred, -1, keepdims=True)
    return centred * lax.rsqrt(var + 1e-05)


def gate_of(values):
    return 0.5 * jnp.tanh(0.5 * values) + 0.5


def dot(values, weight):
    return jnp.dot(values, weight, preferred_element_type=jnp.float32)


def rounded(values):
    return values.astype(jnp.bfloat16).astype(jnp.float32)


def table(row, out):
    tokens, width = out.shape
    at = lax.broadcasted_iota(jnp.int32, (tokens, tokens), 0)
    lane = lax.broadcasted_iota(jnp.int32, (tokens, tokens), 1)
    spread = jnp.where(at == lane, jnp.broadcast_to(row[...].astype(jnp.float32), (tokens, tokens)), 0.0)
    out[...] = jnp.broadcast_to(jnp.sum(spread, -1, keepdims=True), (tokens, width))


def pick(pair):
    return jnp.where(lax.axis_index("col") == 0, *pair)


def edges(masks, slots, halves, source, chains, mask, bias, proj_w, gate_w, start, gates, left, right):
    rows, cols, width = source(slots[0], 0).shape
    tokens = chains.shape[0]
    me = lax.axis_index("row")
    bias_v = bias[...]
    hidden = proj_w.shape[2] // 4
    for h in halves:
        col = lax.axis_index("col")
        first = pl.multiple_of((col if h == 0 else 1 - col) * cols, cols)
        chain_cols = chains[pl.ds(first, cols), :]
        mask_cols = mask[pl.ds(first, cols), :]
        states, pmasks = [], []
        for slot in slots:
            block = source(slot, h)
            for t in range(rows):
                token = (me ^ pick(masks[slot])) * rows + t
                same = chain_cols == chains[pl.ds(token, 1), :]
                states.append(block[t] + jnp.where(same, bias_v, 0.0))
                pmasks.append(mask_cols * mask[pl.ds(token, 1), :])
        state = jnp.concatenate(states, 0)
        pmask = jnp.concatenate(pmasks, 0)
        count = len(slots) * rows
        span = pl.ds(slots[0] * rows * cols, count * cols)
        start[h, span, :] = state
        normed = tile_norm(state).astype(jnp.bfloat16)
        proj = dot(normed, proj_w[0])
        gates[h, span, :] = dot(normed, gate_w[0])
        left[h, span, :] = rounded(gate_of(proj[:, :hidden]) * proj[:, hidden : 2 * hidden] * pmask)
        rgt = rounded(gate_of(proj[:, 2 * hidden : 3 * hidden]) * proj[:, 3 * hidden :] * pmask)
        for n in range(count):
            at, t = divmod(n, rows)
            token = (me ^ pick(masks[slots[at]])) * rows + t
            right[h, pl.ds(token, cols, tokens), :] = rgt[n * cols : (n + 1) * cols]


def prep_kernel(*refs):
    sources, targets, (chains, mask, chains_v, mask_v, sems) = refs[:6], refs[6:10], refs[10:]
    loads = []
    for n, (source, target) in enumerate(zip(sources, targets + (chains_v, mask_v))):
        loads.append(pltpu.make_async_copy(source, target, sems.at[n]))
    for load in loads:
        load.start()
    for load in loads:
        load.wait()
    table(chains_v, chains)
    table(mask_v, mask)


def mine_kernel(masks, *refs):
    blocks, rest = refs[: len(masks) // 2], refs[len(masks) // 2 :]

    def source(slot, half):
        return blocks[slot][half]

    edges(masks, list(range(len(blocks))), (0, 1), source, *rest)


def crop_kernel(
    masks,
    last,
    swapped,
    chains,
    mask,
    bias,
    proj_w,
    gate_w,
    out_w,
    start_in,
    gates_in,
    left_in,
    right_in,
    updated,
    start,
    gates,
    left,
    right,
    tris,
    left1,
    right1,
):
    ranks = len(masks)
    rows, cols, width = last.shape[1:]
    tokens = ranks * rows
    me = lax.axis_index("row")
    col = lax.axis_index("col")
    hidden = proj_w.shape[2] // 4

    def source(slot, half):
        there = swapped[slot - ranks // 2, 1 - half]
        return jnp.where(col == 1, last[half], there) if slot == ranks - 1 else there

    slots = list(range(ranks // 2, ranks))
    edges(masks, slots, (0, 1), source, chains, mask, bias, proj_w, gate_w, start, gates, left, right)

    low = me * rows // 8 * 8
    groups = [col * cols + 8 * n for n in range(cols // 8)] + [low]
    groups = [pl.multiple_of(g, 8) for g in groups]
    count = len(groups)
    block = 8

    def tri_block(step, carry):
        k0 = step * block
        acc = [[None] * count for _ in range(block)]
        for half in range(2):
            for l in range(cols):
                cells = [right[half, pl.ds(pl.multiple_of(l * tokens + g, 8), 8), :] for g in groups]
                for k in range(block):
                    row = left[half, pl.ds((k0 + k) * cols + l, 1), :]
                    for n in range(count):
                        term = row * cells[n]
                        acc[k][n] = term if half + l == 0 else acc[k][n] + term
        for n in range(count):
            for k in range(block):
                tris[n, pl.ds(pl.multiple_of((k0 + k) * 8, 8), 8), :] = acc[k][n]
        return carry

    lax.fori_loop(0, tokens // block, tri_block, 0)

    low_half = jnp.where(low // cols == col, 0, 1)
    low_off = lax.rem(low, cols)
    mask_left = mask[pl.ds(pl.multiple_of(low, 8), 8), :]
    mask_right = mask[pl.ds(pl.multiple_of(col * cols, cols), cols), :]

    def gather(values, n, k):
        if n < count - 1:
            return values[0, pl.ds(k * cols + 8 * n, 8), :]
        return values[low_half, pl.ds(pl.multiple_of(k * cols + low_off, 8), 8), :]

    def updated_state(n):
        tri = tris[n]
        tnorm = tile_norm(tri).astype(jnp.bfloat16)
        gate = gate_of(jnp.concatenate([gather(gates, n, k) for k in range(tokens)], 0))
        state = jnp.concatenate([gather(start, n, k) for k in range(tokens)], 0)
        return state + gate * dot(tnorm, out_w[0])

    row_masks = []
    for slot in range(ranks):
        for t in range(rows):
            row_masks.append(mask[pl.ds((me ^ pick(masks[slot])) * rows + t, 1), :])

    normed = tile_norm(updated_state(count - 1)).astype(jnp.bfloat16)
    proj = dot(normed, proj_w[1, :, : 2 * hidden])
    edge = gate_of(proj[:, :hidden]) * proj[:, hidden:]
    pm = jnp.concatenate([mask_left * m for m in row_masks], 0)
    left1[...] = rounded(edge * pm)

    own_state, own_logits = [], []
    for n in range(count - 1):
        state = updated_state(n)
        normed = tile_norm(state).astype(jnp.bfloat16)
        own_state.append(state[: rows * 8])
        own_logits.append(dot(normed[: rows * 8], gate_w[1]))
        proj = dot(normed, proj_w[1, :, 2 * hidden :])
        edge = gate_of(proj[:, :hidden]) * proj[:, hidden:]
        pm = jnp.concatenate([mask_right[8 * n : 8 * n + 8] * m for m in row_masks], 0)
        right1[n] = rounded(edge * pm)

    shift = lax.rem(me * rows, 8)
    acc = [[None] * (count - 1) for _ in range(rows)]
    for k in range(tokens):
        cells = [right1[n, pl.ds(k * 8, 8), :] for n in range(count - 1)]
        for t in range(rows):
            row = left1[pl.ds(k * 8 + shift + t, 1), :]
            for n in range(count - 1):
                term = row * cells[n]
                acc[t][n] = term if k == 0 else acc[t][n] + term
    for n in range(count - 1):
        tri = jnp.concatenate([acc[t][n] for t in range(rows)], 0)
        tnorm = tile_norm(tri).astype(jnp.bfloat16)
        out = own_state[n] + gate_of(own_logits[n]) * dot(tnorm, out_w[1])
        for t in range(rows):
            updated[t, pl.ds(8 * n, 8), :] = out[8 * t : 8 * t + 8]


def exchange(block, pair):
    ranks = lax.axis_size("row")
    hops = []
    for c, bits in enumerate(pair):
        hops += [(2 * i + c, 2 * (i ^ bits) + c) for i in range(ranks) if bits]
    return lax.ppermute(block, ("row", "col"), hops)


def call(body, inputs, outputs, scratch, name, flops, aliases={}, space=pltpu.VMEM):
    return pl.pallas_call(
        body,
        out_shape=outputs,
        in_specs=[pl.BlockSpec(memory_space=space)] * len(inputs),
        out_specs=[pl.BlockSpec(memory_space=pltpu.VMEM)] * len(outputs),
        scratch_shapes=scratch,
        compiler_params=pltpu.CompilerParams(vmem_limit_bytes=32 << 20),
        input_output_aliases=aliases,
        cost_estimate=pl.CostEstimate(flops=flops, bytes_accessed=1 << 21, transcendentals=0),
        name=name,
    )(*inputs)


def floats(*shapes):
    return [jax.ShapeDtypeStruct(shape, jnp.float32) for shape in shapes]


def like(*arrays):
    return [jax.ShapeDtypeStruct(array.shape, array.dtype) for array in arrays]


def whole_crop_plan(pair, token_mask, chains, chain_bias, proj_weight, gate_weight, out_weight):
    rows, cols, width = pair.shape
    ranks = lax.axis_size("row")
    tokens = token_mask.shape[0]
    hidden = proj_weight.shape[2] // 4
    bias = chain_bias[None, :]
    half = [(2, tokens * cols, width), (2, tokens * cols, width), (2, tokens * cols, hidden), (2, tokens * cols, hidden)]
    half = floats(*half)
    flops = 2 * tokens * cols * width * 5 * hidden
    peers = sorted(range(1, ranks), key=lambda bits: (bits & 1, bits))
    zero, one = peers[: ranks // 2 - 1], peers[ranks // 2 - 1 :]
    steps = list(zip(zero + [0], one))
    masks = [(0, 0)] + steps[:-1] + [(b, a) for a, b in steps[:-1]] + [(one[-1], one[-1])]
    chip = jnp.stack([pair, lax.ppermute(pair, "col", [(0, 1), (1, 0)])])
    got = [exchange(chip, step) for step in steps]
    swapped = lax.ppermute(jnp.stack(got), "col", [(0, 1), (1, 0)])
    loaded = (bias, proj_weight, gate_weight, out_weight, chains[None, :], token_mask[None, :])
    bias, proj_weight, gate_weight, out_weight, chains_t, mask_t = call(
        prep_kernel,
        [pltpu.with_memory_space_constraint(each, pltpu.HBM) for each in loaded],
        like(*loaded[:4]) + floats((tokens, width), (tokens, width)),
        [pltpu.VMEM((1, tokens), jnp.int32), pltpu.VMEM((1, tokens), jnp.int32), pltpu.SemaphoreType.DMA((6,))],
        "prep",
        flops // ranks,
        space=pltpu.HBM,
    )
    edge_inputs = (chains_t, mask_t, bias, proj_weight, gate_weight)
    partial = call(
        functools.partial(mine_kernel, masks),
        (chip, *got[:-1], *edge_inputs),
        half,
        [],
        "mine",
        flops,
    )
    groups = cols // 8 + 1
    extra = [(groups, tokens * 8, hidden), (tokens * 8, hidden), (groups - 1, tokens * 8, hidden)]
    return call(
        functools.partial(crop_kernel, masks),
        (got[-1], swapped, *edge_inputs, out_weight, *partial),
        floats(pair.shape) + half,
        [pltpu.VMEM(each.shape, jnp.float32) for each in floats(*extra)],
        "crop",
        4 * flops,
        {n + 8: n + 1 for n in range(4)},
    )[0]


def shards(pair, token_mask, *rest):
    tokens = token_mask.shape[0]
    ranks = lax.axis_size("row")
    small = tokens * tokens * pair.shape[2] <= 1 << 18 and ranks & (ranks - 1) == 0 and tokens % 16 == 0
    plan = whole_crop_plan if small and lax.axis_size("col") == 2 else sharded_plan
    return plan(pair, token_mask, *rest)


def solution(mesh):
    placed = (P(("group", "row"), "col", None), P("group"), P("group"), P(), P(), P(), P())
    return jax.shard_map(
        shards,
        mesh=mesh,
        in_specs=placed,
        out_specs=P(("group", "row"), "col", None),
        check_vma=False,
    )
```

```python
import functools
import jax
import jax.numpy as jnp
from jax import lax
from jax.experimental import pallas as pl
from jax.experimental.pallas import tpu as pltpu
from jax.sharding import PartitionSpec as P


def layer_norm(values):
    mean = jnp.mean(values, -1, keepdims=True)
    centred = values - mean
    var = jnp.mean(centred * centred, -1, keepdims=True)
    return centred * lax.rsqrt(var + 1e-05)


def flat_dot(values, weight):
    shape = values.shape
    result = jnp.dot(values.reshape(-1, shape[-1]), weight, preferred_element_type=jnp.float32)
    return result.reshape(shape[:-1] + (weight.shape[1],))


def project(state, pmask, p_weight):
    normed = layer_norm(state).astype(jnp.bfloat16)
    proj = flat_dot(normed, p_weight)
    hidden = p_weight.shape[1] // 4
    gate_a = proj[..., :hidden]
    value_a = proj[..., hidden : 2 * hidden]
    gate_b = proj[..., 2 * hidden : 3 * hidden]
    value_b = proj[..., 3 * hidden :]
    left = (jax.nn.sigmoid(gate_a) * value_a * pmask[..., None]).astype(jnp.bfloat16)
    right = (jax.nn.sigmoid(gate_b) * value_b * pmask[..., None]).astype(jnp.bfloat16)
    return (normed, left, right)


def finish(state, normed, tri, g_weight, o_weight):
    tnorm = layer_norm(tri).astype(jnp.bfloat16)
    gate = jax.nn.sigmoid(flat_dot(normed, g_weight))
    return state + gate * flat_dot(tnorm, o_weight)


def sharded_plan(pair, token_mask, chains, chain_bias, proj_weight, gate_weight, out_weight):
    rows, cols, width = pair.shape
    row_start = lax.axis_index("row") * rows
    col_start = lax.axis_index("col") * cols
    chain_rows = lax.dynamic_slice_in_dim(chains, row_start, rows)
    chain_cols = lax.dynamic_slice_in_dim(chains, col_start, cols)
    mask_rows = lax.dynamic_slice_in_dim(token_mask, row_start, rows).astype(jnp.float32)
    mask_cols = lax.dynamic_slice_in_dim(token_mask, col_start, cols).astype(jnp.float32)
    same = (chain_rows[:, None] == chain_cols[None, :]).astype(jnp.float32)
    state = pair + same[..., None] * chain_bias
    pmask = mask_rows[:, None] * mask_cols[None, :]
    normed, left, right = project(state, pmask, proj_weight[0])
    left_rows, right_rows = (
        lax.all_gather(left, "col", axis=1, tiled=True),
        lax.all_gather(right, "col", axis=1, tiled=True),
    )
    every = jnp.einsum(
        "ikh,jkh->ijh",
        left_rows,
        lax.all_gather(right_rows, "row", axis=0, tiled=True),
        preferred_element_type=jnp.float32,
    )
    tri = lax.dynamic_slice_in_dim(every, col_start, cols, 1)
    state = finish(state, normed, tri, gate_weight[0], out_weight[0])
    normed, left, right = project(state, pmask, proj_weight[1])
    left_rows = lax.all_gather(left, "col", axis=1, tiled=True)
    left_cols = lax.all_to_all(left_rows, "row", split_axis=1, concat_axis=0, tiled=True)
    tri = jnp.einsum(
        "kih,kjh->ijh",
        left_cols,
        lax.all_gather(right, "row", axis=0, tiled=True),
        preferred_element_type=jnp.float32,
    )
    return finish(state, normed, tri, gate_weight[1], out_weight[1])


def tile_norm(values):
    mean = jnp.mean(values, -1, keepdims=True)
    centred = values - mean
    var = jnp.mean(centred * centred, -1, keepdims=True)
    return centred * lax.rsqrt(var + 1e-05)


def gate_of(values):
    return 0.5 * jnp.tanh(0.5 * values) + 0.5


def dot(values, weight):
    return jnp.dot(values, weight, preferred_element_type=jnp.float32)


def rounded(values):
    return values.astype(jnp.bfloat16).astype(jnp.float32)


def table(row, out):
    tokens, width = out.shape
    at = lax.broadcasted_iota(jnp.int32, (tokens, tokens), 0)
    lane = lax.broadcasted_iota(jnp.int32, (tokens, tokens), 1)
    spread = jnp.where(at == lane, jnp.broadcast_to(row[...].astype(jnp.float32), (tokens, tokens)), 0.0)
    out[...] = jnp.broadcast_to(jnp.sum(spread, -1, keepdims=True), (tokens, width))


def pick(pair):
    return jnp.where(lax.axis_index("col") == 0, *pair)


def edges(masks, slots, halves, source, chains, mask, bias, proj_w, gate_w, start, gates, left, right):
    rows, cols, width = source(slots[0], 0).shape
    tokens = chains.shape[0]
    me = lax.axis_index("row")
    bias_v = bias[...]
    hidden = proj_w.shape[2] // 4
    for h in halves:
        col = lax.axis_index("col")
        first = pl.multiple_of((col if h == 0 else 1 - col) * cols, cols)
        chain_cols = chains[pl.ds(first, cols), :]
        mask_cols = mask[pl.ds(first, cols), :]
        states, pmasks = [], []
        for slot in slots:
            block = source(slot, h)
            for t in range(rows):
                token = (me ^ pick(masks[slot])) * rows + t
                same = chain_cols == chains[pl.ds(token, 1), :]
                states.append(block[t] + jnp.where(same, bias_v, 0.0))
                pmasks.append(mask_cols * mask[pl.ds(token, 1), :])
        state = jnp.concatenate(states, 0)
        pmask = jnp.concatenate(pmasks, 0)
        count = len(slots) * rows
        span = pl.ds(slots[0] * rows * cols, count * cols)
        start[h, span, :] = state
        normed = tile_norm(state).astype(jnp.bfloat16)
        proj = dot(normed, proj_w[0])
        gates[h, span, :] = dot(normed, gate_w[0])
        left[h, span, :] = rounded(gate_of(proj[:, :hidden]) * proj[:, hidden : 2 * hidden] * pmask)
        rgt = rounded(gate_of(proj[:, 2 * hidden : 3 * hidden]) * proj[:, 3 * hidden :] * pmask)
        for n in range(count):
            at, t = divmod(n, rows)
            token = (me ^ pick(masks[slots[at]])) * rows + t
            right[h, pl.ds(token, cols, tokens), :] = rgt[n * cols : (n + 1) * cols]


def prep_kernel(*refs):
    sources, targets, (chains, mask, chains_v, mask_v, sems) = refs[:7], refs[7:12], refs[12:]
    loads = []
    for n, (source, target) in enumerate(zip(sources, targets + (chains_v, mask_v))):
        loads.append(pltpu.make_async_copy(source, target, sems.at[n]))
    for load in loads:
        load.start()
    for load in loads:
        load.wait()
    table(chains_v, chains)
    table(mask_v, mask)


def mine_kernel(masks, *refs):
    two, more, *rest = refs

    def source(slot, half):
        return two[slot, half] if slot < 2 else more[slot - 2, half]

    edges(masks, list(range(4)), (0, 1), source, *rest)


def crop_kernel(
    masks,
    last,
    swapped,
    chains,
    mask,
    bias,
    proj_w,
    gate_w,
    out_w,
    start_in,
    gates_in,
    left_in,
    right_in,
    updated,
    start,
    gates,
    left,
    right,
    tris,
    left1,
    right1,
):
    ranks = len(masks)
    rows, cols, width = last.shape[2:]
    tokens = ranks * rows
    me = lax.axis_index("row")
    col = lax.axis_index("col")
    hidden = proj_w.shape[2] // 4

    def source(slot, half):
        at = slot - ranks // 2
        there = swapped[at, 1 - half]
        return there if at < 2 else jnp.where(col == 1, last[at - 2, half], there)

    slots = list(range(ranks // 2, ranks))
    edges(masks, slots, (0, 1), source, chains, mask, bias, proj_w, gate_w, start, gates, left, right)

    low = me * rows // 8 * 8
    groups = [col * cols + 8 * n for n in range(cols // 8)] + [low]
    groups = [pl.multiple_of(g, 8) for g in groups]
    count = len(groups)
    block = 8

    def tri_block(step, carry):
        k0 = step * block
        acc = [[None] * count for _ in range(block)]
        for half in range(2):
            for l in range(cols):
                cells = [right[half, pl.ds(pl.multiple_of(l * tokens + g, 8), 8), :] for g in groups]
                for k in range(block):
                    row = left[half, pl.ds((k0 + k) * cols + l, 1), :]
                    for n in range(count):
                        term = row * cells[n]
                        acc[k][n] = term if half + l == 0 else acc[k][n] + term
        for n in range(count):
            for k in range(block):
                tris[n, pl.ds(pl.multiple_of((k0 + k) * 8, 8), 8), :] = acc[k][n]
        return carry

    lax.fori_loop(0, tokens // block, tri_block, 0)

    low_half = jnp.where(low // cols == col, 0, 1)
    low_off = lax.rem(low, cols)
    mask_left = mask[pl.ds(pl.multiple_of(low, 8), 8), :]
    mask_right = mask[pl.ds(pl.multiple_of(col * cols, cols), cols), :]

    def gather(values, n, k):
        if n < count - 1:
            return values[0, pl.ds(k * cols + 8 * n, 8), :]
        return values[low_half, pl.ds(pl.multiple_of(k * cols + low_off, 8), 8), :]

    def updated_state(n):
        tri = tris[n]
        tnorm = tile_norm(tri).astype(jnp.bfloat16)
        gate = gate_of(jnp.concatenate([gather(gates, n, k) for k in range(tokens)], 0))
        state = jnp.concatenate([gather(start, n, k) for k in range(tokens)], 0)
        return state + gate * dot(tnorm, out_w[0])

    row_masks = []
    for slot in range(ranks):
        for t in range(rows):
            row_masks.append(mask[pl.ds((me ^ pick(masks[slot])) * rows + t, 1), :])

    normed = tile_norm(updated_state(count - 1)).astype(jnp.bfloat16)
    proj = dot(normed, proj_w[1, :, : 2 * hidden])
    edge = gate_of(proj[:, :hidden]) * proj[:, hidden:]
    pm = jnp.concatenate([mask_left * m for m in row_masks], 0)
    left1[...] = rounded(edge * pm)

    own_state, own_logits = [], []
    for n in range(count - 1):
        state = updated_state(n)
        normed = tile_norm(state).astype(jnp.bfloat16)
        own_state.append(state[: rows * 8])
        own_logits.append(dot(normed[: rows * 8], gate_w[1]))
        proj = dot(normed, proj_w[1, :, 2 * hidden :])
        edge = gate_of(proj[:, :hidden]) * proj[:, hidden:]
        pm = jnp.concatenate([mask_right[8 * n : 8 * n + 8] * m for m in row_masks], 0)
        right1[n] = rounded(edge * pm)

    shift = lax.rem(me * rows, 8)
    acc = [[None] * (count - 1) for _ in range(rows)]
    for k in range(tokens):
        cells = [right1[n, pl.ds(k * 8, 8), :] for n in range(count - 1)]
        for t in range(rows):
            row = left1[pl.ds(k * 8 + shift + t, 1), :]
            for n in range(count - 1):
                term = row * cells[n]
                acc[t][n] = term if k == 0 else acc[t][n] + term
    for n in range(count - 1):
        tri = jnp.concatenate([acc[t][n] for t in range(rows)], 0)
        tnorm = tile_norm(tri).astype(jnp.bfloat16)
        out = own_state[n] + gate_of(own_logits[n]) * dot(tnorm, out_w[1])
        for t in range(rows):
            updated[t, pl.ds(8 * n, 8), :] = out[8 * t : 8 * t + 8]


def exchange(block, pair):
    ranks = lax.axis_size("row")
    hops = []
    for c, bits in enumerate(pair):
        hops += [(2 * i + c, 2 * (i ^ bits) + c) for i in range(ranks) if bits]
    return lax.ppermute(block, ("row", "col"), hops)


def call(body, inputs, outputs, scratch, name, flops, aliases={}, space=pltpu.VMEM):
    return pl.pallas_call(
        body,
        out_shape=outputs,
        in_specs=[pl.BlockSpec(memory_space=space)] * len(inputs),
        out_specs=[pl.BlockSpec(memory_space=pltpu.VMEM)] * len(outputs),
        scratch_shapes=scratch,
        compiler_params=pltpu.CompilerParams(vmem_limit_bytes=32 << 20),
        input_output_aliases=aliases,
        cost_estimate=pl.CostEstimate(flops=flops, bytes_accessed=1 << 21, transcendentals=0),
        name=name,
    )(*inputs)


def floats(*shapes):
    return [jax.ShapeDtypeStruct(shape, jnp.float32) for shape in shapes]


def like(*arrays):
    return [jax.ShapeDtypeStruct(array.shape, array.dtype) for array in arrays]


def whole_crop_plan(pair, token_mask, chains, chain_bias, proj_weight, gate_weight, out_weight):
    rows, cols, width = pair.shape
    ranks = lax.axis_size("row")
    tokens = token_mask.shape[0]
    hidden = proj_weight.shape[2] // 4
    bias = chain_bias[None, :]
    half = [(2, tokens * cols, width), (2, tokens * cols, width), (2, tokens * cols, hidden), (2, tokens * cols, hidden)]
    half = floats(*half)
    flops = 2 * tokens * cols * width * 5 * hidden
    y, z1, z2 = 1, 2, 4
    masks = [(0, 0), (y, z2), (z2, z1), (z2 | y, z2 | z1), (z1, y), (z2 | z1, z2 | y), (z1 | y,) * 2, (z2 | z1 | y,) * 2]
    partner = lax.ppermute(pair, "col", [(0, 1), (1, 0)])
    loaded = (pair, bias, proj_weight, gate_weight, out_weight, chains[None, :], token_mask[None, :])
    own, bias, proj_weight, gate_weight, out_weight, chains_t, mask_t = call(
        prep_kernel,
        [pltpu.with_memory_space_constraint(each, pltpu.HBM) for each in loaded],
        like(*loaded[:5]) + floats((tokens, width), (tokens, width)),
        [pltpu.VMEM((1, tokens), jnp.int32), pltpu.VMEM((1, tokens), jnp.int32), pltpu.SemaphoreType.DMA((7,))],
        "prep",
        flops // ranks,
        space=pltpu.HBM,
    )
    chip = jnp.stack([own, partner])
    first = exchange(chip, (y, z2))
    two = jnp.stack([chip, first])
    more = exchange(two, (z2, z1))
    last = exchange(two, (0, z1 | y))
    head = jnp.where(lax.axis_index("col") == 0, first, more[0])
    swapped = lax.ppermute(jnp.concatenate([head[None], more[1:], last]), "col", [(0, 1), (1, 0)])
    edge_inputs = (chains_t, mask_t, bias, proj_weight, gate_weight)
    partial = call(functools.partial(mine_kernel, masks), (two, more, *edge_inputs), half, [], "mine", flops)
    groups = cols // 8 + 1
    extra = [(groups, tokens * 8, hidden), (tokens * 8, hidden), (groups - 1, tokens * 8, hidden)]
    return call(
        functools.partial(crop_kernel, masks),
        (last, swapped, *edge_inputs, out_weight, *partial),
        floats(pair.shape) + half,
        [pltpu.VMEM(each.shape, jnp.float32) for each in floats(*extra)],
        "crop",
        4 * flops,
        {n + 8: n + 1 for n in range(4)},
    )[0]


def shards(pair, token_mask, *rest):
    tokens = token_mask.shape[0]
    ranks = lax.axis_size("row")
    small = tokens * tokens * pair.shape[2] <= 1 << 18 and ranks == 8 and pair.shape[1] % 8 == 0
    plan = whole_crop_plan if small and lax.axis_size("col") == 2 else sharded_plan
    return plan(pair, token_mask, *rest)


def solution(mesh):
    placed = (P(("group", "row"), "col", None), P("group"), P("group"), P(), P(), P(), P())
    return jax.shard_map(
        shards,
        mesh=mesh,
        in_specs=placed,
        out_specs=P(("group", "row"), "col", None),
        check_vma=False,
    )
```

```python
import functools
import jax
import jax.numpy as jnp
from jax import lax
from jax.experimental import pallas as pl
from jax.experimental.pallas import tpu as pltpu
from jax.sharding import PartitionSpec as P


def layer_norm(values):
    mean = jnp.mean(values, -1, keepdims=True)
    centred = values - mean
    var = jnp.mean(centred * centred, -1, keepdims=True)
    return centred * lax.rsqrt(var + 1e-05)


def flat_dot(values, weight):
    shape = values.shape
    result = jnp.dot(values.reshape(-1, shape[-1]), weight, preferred_element_type=jnp.float32)
    return result.reshape(shape[:-1] + (weight.shape[1],))


def project(state, pmask, p_weight):
    normed = layer_norm(state).astype(jnp.bfloat16)
    proj = flat_dot(normed, p_weight)
    hidden = p_weight.shape[1] // 4
    gate_a = proj[..., :hidden]
    value_a = proj[..., hidden : 2 * hidden]
    gate_b = proj[..., 2 * hidden : 3 * hidden]
    value_b = proj[..., 3 * hidden :]
    left = (jax.nn.sigmoid(gate_a) * value_a * pmask[..., None]).astype(jnp.bfloat16)
    right = (jax.nn.sigmoid(gate_b) * value_b * pmask[..., None]).astype(jnp.bfloat16)
    return (normed, left, right)


def finish(state, normed, tri, g_weight, o_weight):
    tnorm = layer_norm(tri).astype(jnp.bfloat16)
    gate = jax.nn.sigmoid(flat_dot(normed, g_weight))
    return state + gate * flat_dot(tnorm, o_weight)


def sharded_plan(pair, token_mask, chains, chain_bias, proj_weight, gate_weight, out_weight):
    rows, cols, width = pair.shape
    row_start = lax.axis_index("row") * rows
    col_start = lax.axis_index("col") * cols
    chain_rows = lax.dynamic_slice_in_dim(chains, row_start, rows)
    chain_cols = lax.dynamic_slice_in_dim(chains, col_start, cols)
    mask_rows = lax.dynamic_slice_in_dim(token_mask, row_start, rows).astype(jnp.float32)
    mask_cols = lax.dynamic_slice_in_dim(token_mask, col_start, cols).astype(jnp.float32)
    same = (chain_rows[:, None] == chain_cols[None, :]).astype(jnp.float32)
    state = pair + same[..., None] * chain_bias
    pmask = mask_rows[:, None] * mask_cols[None, :]
    normed, left, right = project(state, pmask, proj_weight[0])
    left_rows, right_rows = (
        lax.all_gather(left, "col", axis=1, tiled=True),
        lax.all_gather(right, "col", axis=1, tiled=True),
    )
    every = jnp.einsum(
        "ikh,jkh->ijh",
        left_rows,
        lax.all_gather(right_rows, "row", axis=0, tiled=True),
        preferred_element_type=jnp.float32,
    )
    tri = lax.dynamic_slice_in_dim(every, col_start, cols, 1)
    state = finish(state, normed, tri, gate_weight[0], out_weight[0])
    normed, left, right = project(state, pmask, proj_weight[1])
    left_rows = lax.all_gather(left, "col", axis=1, tiled=True)
    left_cols = lax.all_to_all(left_rows, "row", split_axis=1, concat_axis=0, tiled=True)
    tri = jnp.einsum(
        "kih,kjh->ijh",
        left_cols,
        lax.all_gather(right, "row", axis=0, tiled=True),
        preferred_element_type=jnp.float32,
    )
    return finish(state, normed, tri, gate_weight[1], out_weight[1])


def tile_norm(values):
    mean = jnp.mean(values, -1, keepdims=True)
    centred = values - mean
    var = jnp.mean(centred * centred, -1, keepdims=True)
    return centred * lax.rsqrt(var + 1e-05)


def gate_of(values):
    return 0.5 * jnp.tanh(0.5 * values) + 0.5


def dot(values, weight):
    return jnp.dot(values, weight, preferred_element_type=jnp.float32)


def rounded(values):
    return values.astype(jnp.bfloat16).astype(jnp.float32)


def table(row, out):
    tokens, width = out.shape
    at = lax.broadcasted_iota(jnp.int32, (tokens, tokens), 0)
    lane = lax.broadcasted_iota(jnp.int32, (tokens, tokens), 1)
    spread = jnp.where(at == lane, jnp.broadcast_to(row[...].astype(jnp.float32), (tokens, tokens)), 0.0)
    out[...] = jnp.broadcast_to(jnp.sum(spread, -1, keepdims=True), (tokens, width))


def edges(masks, items, chains, mask, bias, proj_w, gate_w, start, gates, left, right):
    rows, cols, width = items[0][2].shape
    tokens = chains.shape[0]
    me = lax.axis_index("row")
    col = lax.axis_index("col")
    bias_v = bias[...]
    hidden = proj_w.shape[2] // 4
    for half in range(2):
        batch = [(slot, block) for slot, h, block in items if h == half]
        if not batch:
            continue
        first = pl.multiple_of((col if half == 0 else 1 - col) * cols, cols)
        chain_cols = chains[pl.ds(first, cols), :]
        mask_cols = mask[pl.ds(first, cols), :]
        states, pmasks = [], []
        for slot, block in batch:
            for t in range(rows):
                token = (me ^ masks[slot]) * rows + t
                same = chain_cols == chains[pl.ds(token, 1), :]
                states.append(block[t] + jnp.where(same, bias_v, 0.0))
                pmasks.append(mask_cols * mask[pl.ds(token, 1), :])
        state = jnp.concatenate(states, 0)
        pmask = jnp.concatenate(pmasks, 0)
        normed = tile_norm(state).astype(jnp.bfloat16)
        proj = dot(normed, proj_w[0])
        gate = dot(normed, gate_w[0])
        lft = rounded(gate_of(proj[:, :hidden]) * proj[:, hidden : 2 * hidden] * pmask)
        rgt = rounded(gate_of(proj[:, 2 * hidden : 3 * hidden]) * proj[:, 3 * hidden :] * pmask)
        size = rows * cols
        for n, (slot, _) in enumerate(batch):
            span, part = pl.ds(slot * size, size), slice(n * size, (n + 1) * size)
            start[half, span, :] = state[part]
            gates[half, span, :] = gate[part]
            left[half, span, :] = lft[part]
            for t in range(rows):
                token = (me ^ masks[slot]) * rows + t
                at = n * size + t * cols
                right[half, pl.ds(token, cols, tokens), :] = rgt[at : at + cols]


def own_kernel(masks, *refs):
    sources, rest = refs[:7], refs[7:]
    pair, bias, proj_w, gate_w, out_w, chains, mask, start, gates, left, right, chains_v, mask_v, sems = rest
    loads = []
    for n, (source, target) in enumerate(zip(sources, (pair, bias, proj_w, gate_w, out_w, chains_v, mask_v))):
        loads.append(pltpu.make_async_copy(source, target, sems.at[n]))
    for load in loads:
        load.start()
    for load in loads:
        load.wait()
    table(chains_v, chains)
    table(mask_v, mask)
    edges(masks, [(0, 0, pair[...])], chains, mask, bias, proj_w, gate_w, start, gates, left, right)


def mine_kernel(masks, halves, mine, chains, mask, bias, proj_w, gate_w, s_in, g_in, l_in, r_in, *outs):
    items = [(slot, halves[slot], mine[slot]) for slot in range(1, len(masks))]
    edges(masks, items, chains, mask, bias, proj_w, gate_w, *outs)


def crop_kernel(
    masks,
    halves,
    other,
    chains,
    mask,
    bias,
    proj_w,
    gate_w,
    out_w,
    start_in,
    gates_in,
    left_in,
    right_in,
    updated,
    start,
    gates,
    left,
    right,
    tris,
    left1,
    right1,
):
    ranks, rows, cols, width = other.shape
    tokens = ranks * rows
    me = lax.axis_index("row")
    col = lax.axis_index("col")
    hidden = proj_w.shape[2] // 4
    items = [(slot, 1 - halves[slot], other[slot]) for slot in range(ranks)]
    edges(masks, items, chains, mask, bias, proj_w, gate_w, start, gates, left, right)

    low = me * rows // 8 * 8
    groups = [col * cols + 8 * n for n in range(cols // 8)] + [low]
    groups = [pl.multiple_of(g, 8) for g in groups]
    count = len(groups)
    block = 8

    def tri_block(step, carry):
        k0 = step * block
        acc = [[None] * count for _ in range(block)]
        for half in range(2):
            for l in range(cols):
                cells = [right[half, pl.ds(pl.multiple_of(l * tokens + g, 8), 8), :] for g in groups]
                for k in range(block):
                    row = left[half, pl.ds((k0 + k) * cols + l, 1), :]
                    for n in range(count):
                        term = row * cells[n]
                        acc[k][n] = term if half + l == 0 else acc[k][n] + term
        for n in range(count):
            for k in range(block):
                tris[n, pl.ds(pl.multiple_of((k0 + k) * 8, 8), 8), :] = acc[k][n]
        return carry

    lax.fori_loop(0, tokens // block, tri_block, 0)

    low_half = jnp.where(low // cols == col, 0, 1)
    low_off = lax.rem(low, cols)
    mask_left = mask[pl.ds(pl.multiple_of(low, 8), 8), :]
    mask_right = mask[pl.ds(pl.multiple_of(col * cols, cols), cols), :]

    def gather(values, n, k):
        if n < count - 1:
            return values[0, pl.ds(k * cols + 8 * n, 8), :]
        return values[low_half, pl.ds(pl.multiple_of(k * cols + low_off, 8), 8), :]

    def updated_state(n):
        tri = tris[n]
        tnorm = tile_norm(tri).astype(jnp.bfloat16)
        gate = gate_of(jnp.concatenate([gather(gates, n, k) for k in range(tokens)], 0))
        state = jnp.concatenate([gather(start, n, k) for k in range(tokens)], 0)
        return state + gate * dot(tnorm, out_w[0])

    row_masks = []
    for slot in range(ranks):
        for t in range(rows):
            row_masks.append(mask[pl.ds((me ^ masks[slot]) * rows + t, 1), :])

    normed = tile_norm(updated_state(count - 1)).astype(jnp.bfloat16)
    proj = dot(normed, proj_w[1, :, : 2 * hidden])
    edge = gate_of(proj[:, :hidden]) * proj[:, hidden:]
    pm = jnp.concatenate([mask_left * m for m in row_masks], 0)
    left1[...] = rounded(edge * pm)

    own_state, own_logits = [], []
    for n in range(count - 1):
        state = updated_state(n)
        normed = tile_norm(state).astype(jnp.bfloat16)
        own_state.append(state[: rows * 8])
        own_logits.append(dot(normed[: rows * 8], gate_w[1]))
        proj = dot(normed, proj_w[1, :, 2 * hidden :])
        edge = gate_of(proj[:, :hidden]) * proj[:, hidden:]
        pm = jnp.concatenate([mask_right[8 * n : 8 * n + 8] * m for m in row_masks], 0)
        right1[n] = rounded(edge * pm)

    shift = lax.rem(me * rows, 8)
    acc = [[None] * (count - 1) for _ in range(rows)]
    for k in range(tokens):
        cells = [right1[n, pl.ds(k * 8, 8), :] for n in range(count - 1)]
        for t in range(rows):
            row = left1[pl.ds(k * 8 + shift + t, 1), :]
            for n in range(count - 1):
                term = row * cells[n]
                acc[t][n] = term if k == 0 else acc[t][n] + term
    for n in range(count - 1):
        tri = jnp.concatenate([acc[t][n] for t in range(rows)], 0)
        tnorm = tile_norm(tri).astype(jnp.bfloat16)
        out = own_state[n] + gate_of(own_logits[n]) * dot(tnorm, out_w[1])
        for t in range(rows):
            updated[t, pl.ds(8 * n, 8), :] = out[8 * t : 8 * t + 8]


def exchange(block, bits):
    ranks = lax.axis_size("row")
    hops = [(2 * i + c, 2 * (i ^ bits) + 1 - c) for i in range(ranks) for c in range(2)]
    return lax.ppermute(block, ("row", "col"), hops)


def call(body, inputs, outputs, scratch, name, flops, aliases={}, space=pltpu.VMEM):
    return pl.pallas_call(
        body,
        out_shape=outputs,
        in_specs=[pl.BlockSpec(memory_space=space)] * len(inputs),
        out_specs=[pl.BlockSpec(memory_space=pltpu.VMEM)] * len(outputs),
        scratch_shapes=scratch,
        compiler_params=pltpu.CompilerParams(vmem_limit_bytes=32 << 20),
        input_output_aliases=aliases,
        cost_estimate=pl.CostEstimate(flops=flops, bytes_accessed=1 << 21, transcendentals=0),
        name=name,
    )(*inputs)


def floats(*shapes):
    return [jax.ShapeDtypeStruct(shape, jnp.float32) for shape in shapes]


def like(*arrays):
    return [jax.ShapeDtypeStruct(array.shape, array.dtype) for array in arrays]


def whole_crop_plan(pair, token_mask, chains, chain_bias, proj_weight, gate_weight, out_weight):
    rows, cols, width = pair.shape
    ranks = lax.axis_size("row")
    tokens = token_mask.shape[0]
    hidden = proj_weight.shape[2] // 4
    bias = chain_bias[None, :]
    half = [(2, tokens * cols, width), (2, tokens * cols, width), (2, tokens * cols, hidden), (2, tokens * cols, hidden)]
    half = floats(*half)
    flops = 2 * tokens * cols * width * 5 * hidden
    top = ranks // 2
    masks, halves = [0, top], [0, 1]
    for bits in range(top - 1, 0, -1):
        masks += [bits, bits ^ top]
        halves += [1, 0]
    far = exchange(pair, top)
    loaded = (pair, bias, proj_weight, gate_weight, out_weight, chains[None, :], token_mask[None, :])
    own, bias, proj_weight, gate_weight, out_weight, chains_t, mask_t, *partial = call(
        functools.partial(own_kernel, masks),
        [pltpu.with_memory_space_constraint(each, pltpu.HBM) for each in loaded],
        like(*loaded[:5]) + floats((tokens, width), (tokens, width)) + half,
        [pltpu.VMEM((1, tokens), jnp.int32), pltpu.VMEM((1, tokens), jnp.int32), pltpu.SemaphoreType.DMA((7,))],
        "own",
        flops // ranks,
        space=pltpu.HBM,
    )
    two = jnp.stack([own, far])
    mine = jnp.concatenate([two] + [exchange(two, bits) for bits in range(top - 1, 0, -1)], 0)
    other = lax.ppermute(mine, "col", [(0, 1), (1, 0)])
    edge_inputs = (chains_t, mask_t, bias, proj_weight, gate_weight)
    partial = call(
        functools.partial(mine_kernel, masks, halves),
        (mine, *edge_inputs, *partial),
        half,
        [],
        "mine",
        flops,
        {n + 6: n for n in range(4)},
    )
    groups = cols // 8 + 1
    extra = [(groups, tokens * 8, hidden), (tokens * 8, hidden), (groups - 1, tokens * 8, hidden)]
    return call(
        functools.partial(crop_kernel, masks, halves),
        (other, *edge_inputs, out_weight, *partial),
        floats(pair.shape) + half,
        [pltpu.VMEM(each.shape, jnp.float32) for each in floats(*extra)],
        "crop",
        4 * flops,
        {n + 7: n + 1 for n in range(4)},
    )[0]


def shards(pair, token_mask, *rest):
    tokens = token_mask.shape[0]
    ranks = lax.axis_size("row")
    small = tokens * tokens * pair.shape[2] <= 1 << 18 and ranks & (ranks - 1) == 0 and pair.shape[1] % 8 == 0
    plan = whole_crop_plan if small and lax.axis_size("col") == 2 else sharded_plan
    return plan(pair, token_mask, *rest)


def solution(mesh):
    placed = (P(("group", "row"), "col", None), P("group"), P("group"), P(), P(), P(), P())
    return jax.shard_map(
        shards,
        mesh=mesh,
        in_specs=placed,
        out_specs=P(("group", "row"), "col", None),
        check_vma=False,
    )
```

```python
import functools
import jax
import jax.numpy as jnp
from jax import lax
from jax.experimental import pallas as pl
from jax.experimental.pallas import tpu as pltpu
from jax.sharding import PartitionSpec as P


def layer_norm(values):
    mean = jnp.mean(values, -1, keepdims=True)
    centred = values - mean
    var = jnp.mean(centred * centred, -1, keepdims=True)
    return centred * lax.rsqrt(var + 1e-05)


def flat_dot(values, weight):
    shape = values.shape
    result = jnp.dot(values.reshape(-1, shape[-1]), weight, preferred_element_type=jnp.float32)
    return result.reshape(shape[:-1] + (weight.shape[1],))


def project(state, pmask, p_weight):
    normed = layer_norm(state).astype(jnp.bfloat16)
    proj = flat_dot(normed, p_weight)
    hidden = p_weight.shape[1] // 4
    gate_a = proj[..., :hidden]
    value_a = proj[..., hidden : 2 * hidden]
    gate_b = proj[..., 2 * hidden : 3 * hidden]
    value_b = proj[..., 3 * hidden :]
    left = (jax.nn.sigmoid(gate_a) * value_a * pmask[..., None]).astype(jnp.bfloat16)
    right = (jax.nn.sigmoid(gate_b) * value_b * pmask[..., None]).astype(jnp.bfloat16)
    return (normed, left, right)


def finish(state, normed, tri, g_weight, o_weight):
    tnorm = layer_norm(tri).astype(jnp.bfloat16)
    gate = jax.nn.sigmoid(flat_dot(normed, g_weight))
    return state + gate * flat_dot(tnorm, o_weight)


def sharded_plan(pair, token_mask, chains, chain_bias, proj_weight, gate_weight, out_weight):
    rows, cols, width = pair.shape
    row_start = lax.axis_index("row") * rows
    col_start = lax.axis_index("col") * cols
    chain_rows = lax.dynamic_slice_in_dim(chains, row_start, rows)
    chain_cols = lax.dynamic_slice_in_dim(chains, col_start, cols)
    mask_rows = lax.dynamic_slice_in_dim(token_mask, row_start, rows).astype(jnp.float32)
    mask_cols = lax.dynamic_slice_in_dim(token_mask, col_start, cols).astype(jnp.float32)
    same = (chain_rows[:, None] == chain_cols[None, :]).astype(jnp.float32)
    state = pair + same[..., None] * chain_bias
    pmask = mask_rows[:, None] * mask_cols[None, :]
    normed, left, right = project(state, pmask, proj_weight[0])
    left_rows, right_rows = (
        lax.all_gather(left, "col", axis=1, tiled=True),
        lax.all_gather(right, "col", axis=1, tiled=True),
    )
    every = jnp.einsum(
        "ikh,jkh->ijh",
        left_rows,
        lax.all_gather(right_rows, "row", axis=0, tiled=True),
        preferred_element_type=jnp.float32,
    )
    tri = lax.dynamic_slice_in_dim(every, col_start, cols, 1)
    state = finish(state, normed, tri, gate_weight[0], out_weight[0])
    normed, left, right = project(state, pmask, proj_weight[1])
    left_rows = lax.all_gather(left, "col", axis=1, tiled=True)
    left_cols = lax.all_to_all(left_rows, "row", split_axis=1, concat_axis=0, tiled=True)
    tri = jnp.einsum(
        "kih,kjh->ijh",
        left_cols,
        lax.all_gather(right, "row", axis=0, tiled=True),
        preferred_element_type=jnp.float32,
    )
    return finish(state, normed, tri, gate_weight[1], out_weight[1])


def tile_norm(values):
    mean = jnp.mean(values, -1, keepdims=True)
    centred = values - mean
    var = jnp.mean(centred * centred, -1, keepdims=True)
    return centred * lax.rsqrt(var + 1e-05)


def gate_of(values):
    return 0.5 * jnp.tanh(0.5 * values) + 0.5


def dot(values, weight):
    return jnp.dot(values, weight, preferred_element_type=jnp.float32)


def rounded(values):
    return values.astype(jnp.bfloat16).astype(jnp.float32)


def table(row, out):
    tokens, width = out.shape
    at = lax.broadcasted_iota(jnp.int32, (tokens, tokens), 0)
    lane = lax.broadcasted_iota(jnp.int32, (tokens, tokens), 1)
    spread = jnp.where(at == lane, jnp.broadcast_to(row[...].astype(jnp.float32), (tokens, tokens)), 0.0)
    out[...] = jnp.broadcast_to(jnp.sum(spread, -1, keepdims=True), (tokens, width))


def edges(masks, items, chains, mask, bias, proj_w, gate_w, start, gates, left, right):
    rows, cols, width = items[0][2].shape
    tokens = chains.shape[0]
    me = lax.axis_index("row")
    col = lax.axis_index("col")
    bias_v = bias[...]
    hidden = proj_w.shape[2] // 4
    for half in range(2):
        batch = [(slot, block) for slot, h, block in items if h == half]
        if not batch:
            continue
        first = pl.multiple_of((col if half == 0 else 1 - col) * cols, cols)
        chain_cols = chains[pl.ds(first, cols), :]
        mask_cols = mask[pl.ds(first, cols), :]
        states, pmasks = [], []
        for slot, block in batch:
            for t in range(rows):
                token = (me ^ masks[slot]) * rows + t
                same = chain_cols == chains[pl.ds(token, 1), :]
                states.append(block[t] + jnp.where(same, bias_v, 0.0))
                pmasks.append(mask_cols * mask[pl.ds(token, 1), :])
        state = jnp.concatenate(states, 0)
        pmask = jnp.concatenate(pmasks, 0)
        normed = tile_norm(state).astype(jnp.bfloat16)
        proj = dot(normed, proj_w[0])
        gate = dot(normed, gate_w[0])
        lft = rounded(gate_of(proj[:, :hidden]) * proj[:, hidden : 2 * hidden] * pmask)
        rgt = rounded(gate_of(proj[:, 2 * hidden : 3 * hidden]) * proj[:, 3 * hidden :] * pmask)
        size = rows * cols
        for n, (slot, _) in enumerate(batch):
            span, part = pl.ds(slot * size, size), slice(n * size, (n + 1) * size)
            start[half, span, :] = state[part]
            gates[half, span, :] = gate[part]
            left[half, span, :] = lft[part]
            for t in range(rows):
                token = (me ^ masks[slot]) * rows + t
                at = n * size + t * cols
                right[half, pl.ds(token, cols, tokens), :] = rgt[at : at + cols]


def own_kernel(masks, *refs):
    sources, rest = refs[:7], refs[7:]
    pair, bias, proj_w, gate_w, out_w, chains, mask, start, gates, left, right, chains_v, mask_v, sems = rest
    loads = []
    for n, (source, target) in enumerate(zip(sources, (pair, bias, proj_w, gate_w, out_w, chains_v, mask_v))):
        loads.append(pltpu.make_async_copy(source, target, sems.at[n]))
    for load in loads:
        load.start()
    for load in loads:
        load.wait()
    table(chains_v, chains)
    table(mask_v, mask)
    edges(masks, [(0, 0, pair[...])], chains, mask, bias, proj_w, gate_w, start, gates, left, right)


def mine_kernel(masks, halves, mine, chains, mask, bias, proj_w, gate_w, s_in, g_in, l_in, r_in, *outs):
    items = [(slot, halves[slot], mine[slot]) for slot in range(1, len(masks))]
    edges(masks, items, chains, mask, bias, proj_w, gate_w, *outs)


def crop_kernel(
    masks,
    halves,
    other,
    chains,
    mask,
    bias,
    proj_w,
    gate_w,
    out_w,
    start_in,
    gates_in,
    left_in,
    right_in,
    updated,
    start,
    gates,
    left,
    right,
    tris,
    left1,
    right1,
):
    ranks, rows, cols, width = other.shape
    tokens = ranks * rows
    me = lax.axis_index("row")
    col = lax.axis_index("col")
    hidden = proj_w.shape[2] // 4
    items = [(slot, 1 - halves[slot], other[slot]) for slot in range(ranks)]
    edges(masks, items, chains, mask, bias, proj_w, gate_w, start, gates, left, right)

    low = me * rows // 8 * 8
    groups = [col * cols + 8 * n for n in range(cols // 8)] + [low]
    groups = [pl.multiple_of(g, 8) for g in groups]
    count = len(groups)
    block = 8

    def tri_block(step, carry):
        k0 = step * block
        acc = [[None] * count for _ in range(block)]
        for half in range(2):
            for l in range(cols):
                cells = [right[half, pl.ds(pl.multiple_of(l * tokens + g, 8), 8), :] for g in groups]
                for k in range(block):
                    row = left[half, pl.ds((k0 + k) * cols + l, 1), :]
                    for n in range(count):
                        term = row * cells[n]
                        acc[k][n] = term if half + l == 0 else acc[k][n] + term
        for n in range(count):
            for k in range(block):
                tris[n, pl.ds(pl.multiple_of((k0 + k) * 8, 8), 8), :] = acc[k][n]
        return carry

    lax.fori_loop(0, tokens // block, tri_block, 0)

    low_half = jnp.where(low // cols == col, 0, 1)
    low_off = lax.rem(low, cols)
    mask_left = mask[pl.ds(pl.multiple_of(low, 8), 8), :]
    mask_right = mask[pl.ds(pl.multiple_of(col * cols, cols), cols), :]

    def gather(values, n, k):
        if n < count - 1:
            return values[0, pl.ds(k * cols + 8 * n, 8), :]
        return values[low_half, pl.ds(pl.multiple_of(k * cols + low_off, 8), 8), :]

    def updated_state(n):
        tri = tris[n]
        tnorm = tile_norm(tri).astype(jnp.bfloat16)
        gate = gate_of(jnp.concatenate([gather(gates, n, k) for k in range(tokens)], 0))
        state = jnp.concatenate([gather(start, n, k) for k in range(tokens)], 0)
        return state + gate * dot(tnorm, out_w[0])

    row_masks = []
    for slot in range(ranks):
        for t in range(rows):
            row_masks.append(mask[pl.ds((me ^ masks[slot]) * rows + t, 1), :])

    normed = tile_norm(updated_state(count - 1)).astype(jnp.bfloat16)
    proj = dot(normed, proj_w[1, :, : 2 * hidden])
    edge = gate_of(proj[:, :hidden]) * proj[:, hidden:]
    pm = jnp.concatenate([mask_left * m for m in row_masks], 0)
    left1[...] = rounded(edge * pm)

    own_state, own_logits = [], []
    for n in range(count - 1):
        state = updated_state(n)
        normed = tile_norm(state).astype(jnp.bfloat16)
        own_state.append(state[: rows * 8])
        own_logits.append(dot(normed[: rows * 8], gate_w[1]))
        proj = dot(normed, proj_w[1, :, 2 * hidden :])
        edge = gate_of(proj[:, :hidden]) * proj[:, hidden:]
        pm = jnp.concatenate([mask_right[8 * n : 8 * n + 8] * m for m in row_masks], 0)
        right1[n] = rounded(edge * pm)

    shift = lax.rem(me * rows, 8)
    acc = [[None] * (count - 1) for _ in range(rows)]
    for k in range(tokens):
        cells = [right1[n, pl.ds(k * 8, 8), :] for n in range(count - 1)]
        for t in range(rows):
            row = left1[pl.ds(k * 8 + shift + t, 1), :]
            for n in range(count - 1):
                term = row * cells[n]
                acc[t][n] = term if k == 0 else acc[t][n] + term
    for n in range(count - 1):
        tri = jnp.concatenate([acc[t][n] for t in range(rows)], 0)
        tnorm = tile_norm(tri).astype(jnp.bfloat16)
        out = own_state[n] + gate_of(own_logits[n]) * dot(tnorm, out_w[1])
        for t in range(rows):
            updated[t, pl.ds(8 * n, 8), :] = out[8 * t : 8 * t + 8]


def exchange(block, bits):
    ranks = lax.axis_size("row")
    hops = [(2 * i + c, 2 * (i ^ bits) + 1 - c) for i in range(ranks) for c in range(2)]
    return lax.ppermute(block, ("row", "col"), hops)


def call(body, inputs, outputs, scratch, name, flops, aliases={}, space=pltpu.VMEM):
    return pl.pallas_call(
        body,
        out_shape=outputs,
        in_specs=[pl.BlockSpec(memory_space=space)] * len(inputs),
        out_specs=[pl.BlockSpec(memory_space=pltpu.VMEM)] * len(outputs),
        scratch_shapes=scratch,
        compiler_params=pltpu.CompilerParams(vmem_limit_bytes=32 << 20),
        input_output_aliases=aliases,
        cost_estimate=pl.CostEstimate(flops=flops, bytes_accessed=1 << 21, transcendentals=0),
        name=name,
    )(*inputs)


def floats(*shapes):
    return [jax.ShapeDtypeStruct(shape, jnp.float32) for shape in shapes]


def like(*arrays):
    return [jax.ShapeDtypeStruct(array.shape, array.dtype) for array in arrays]


def whole_crop_plan(pair, token_mask, chains, chain_bias, proj_weight, gate_weight, out_weight):
    rows, cols, width = pair.shape
    ranks = lax.axis_size("row")
    tokens = token_mask.shape[0]
    hidden = proj_weight.shape[2] // 4
    bias = chain_bias[None, :]
    half = [(2, tokens * cols, width), (2, tokens * cols, width), (2, tokens * cols, hidden), (2, tokens * cols, hidden)]
    half = floats(*half)
    flops = 2 * tokens * cols * width * 5 * hidden
    top = ranks // 2
    masks, halves = [0, top], [0, 1]
    for bits in range(1, top):
        masks += [bits, bits ^ top]
        halves += [1, 0]
    far = exchange(pair, top)
    loaded = (pair, bias, proj_weight, gate_weight, out_weight, chains[None, :], token_mask[None, :])
    own, bias, proj_weight, gate_weight, out_weight, chains_t, mask_t, *partial = call(
        functools.partial(own_kernel, masks),
        [pltpu.with_memory_space_constraint(each, pltpu.HBM) for each in loaded],
        like(*loaded[:5]) + floats((tokens, width), (tokens, width)) + half,
        [pltpu.VMEM((1, tokens), jnp.int32), pltpu.VMEM((1, tokens), jnp.int32), pltpu.SemaphoreType.DMA((7,))],
        "own",
        flops // ranks,
        space=pltpu.HBM,
    )
    two = jnp.stack([own, far])
    mine = jnp.concatenate([two] + [exchange(two, bits) for bits in range(1, top)], 0)
    other = lax.ppermute(mine, "col", [(0, 1), (1, 0)])
    edge_inputs = (chains_t, mask_t, bias, proj_weight, gate_weight)
    partial = call(
        functools.partial(mine_kernel, masks, halves),
        (mine, *edge_inputs, *partial),
        half,
        [],
        "mine",
        flops,
        {n + 6: n for n in range(4)},
    )
    groups = cols // 8 + 1
    extra = [(groups, tokens * 8, hidden), (tokens * 8, hidden), (groups - 1, tokens * 8, hidden)]
    return call(
        functools.partial(crop_kernel, masks, halves),
        (other, *edge_inputs, out_weight, *partial),
        floats(pair.shape) + half,
        [pltpu.VMEM(each.shape, jnp.float32) for each in floats(*extra)],
        "crop",
        4 * flops,
        {n + 7: n + 1 for n in range(4)},
    )[0]


def shards(pair, token_mask, *rest):
    tokens = token_mask.shape[0]
    ranks = lax.axis_size("row")
    small = tokens * tokens * pair.shape[2] <= 1 << 18 and ranks & (ranks - 1) == 0 and pair.shape[1] % 8 == 0
    plan = whole_crop_plan if small and lax.axis_size("col") == 2 else sharded_plan
    return plan(pair, token_mask, *rest)


def solution(mesh):
    placed = (P(("group", "row"), "col", None), P("group"), P("group"), P(), P(), P(), P())
    return jax.shard_map(
        shards,
        mesh=mesh,
        in_specs=placed,
        out_specs=P(("group", "row"), "col", None),
        check_vma=False,
    )
```

```python
import functools
import jax
import jax.numpy as jnp
from jax import lax
from jax.experimental import pallas as pl
from jax.experimental.pallas import tpu as pltpu
from jax.sharding import PartitionSpec as P


def layer_norm(values):
    mean = jnp.mean(values, -1, keepdims=True)
    centred = values - mean
    var = jnp.mean(centred * centred, -1, keepdims=True)
    return centred * lax.rsqrt(var + 1e-05)


def flat_dot(values, weight):
    shape = values.shape
    result = jnp.dot(values.reshape(-1, shape[-1]), weight, preferred_element_type=jnp.float32)
    return result.reshape(shape[:-1] + (weight.shape[1],))


def project(state, pmask, p_weight):
    normed = layer_norm(state).astype(jnp.bfloat16)
    proj = flat_dot(normed, p_weight)
    hidden = p_weight.shape[1] // 4
    gate_a = proj[..., :hidden]
    value_a = proj[..., hidden : 2 * hidden]
    gate_b = proj[..., 2 * hidden : 3 * hidden]
    value_b = proj[..., 3 * hidden :]
    left = (jax.nn.sigmoid(gate_a) * value_a * pmask[..., None]).astype(jnp.bfloat16)
    right = (jax.nn.sigmoid(gate_b) * value_b * pmask[..., None]).astype(jnp.bfloat16)
    return (normed, left, right)


def finish(state, normed, tri, g_weight, o_weight):
    tnorm = layer_norm(tri).astype(jnp.bfloat16)
    gate = jax.nn.sigmoid(flat_dot(normed, g_weight))
    return state + gate * flat_dot(tnorm, o_weight)


def sharded_plan(pair, token_mask, chains, chain_bias, proj_weight, gate_weight, out_weight):
    rows, cols, width = pair.shape
    row_start = lax.axis_index("row") * rows
    col_start = lax.axis_index("col") * cols
    chain_rows = lax.dynamic_slice_in_dim(chains, row_start, rows)
    chain_cols = lax.dynamic_slice_in_dim(chains, col_start, cols)
    mask_rows = lax.dynamic_slice_in_dim(token_mask, row_start, rows).astype(jnp.float32)
    mask_cols = lax.dynamic_slice_in_dim(token_mask, col_start, cols).astype(jnp.float32)
    same = (chain_rows[:, None] == chain_cols[None, :]).astype(jnp.float32)
    state = pair + same[..., None] * chain_bias
    pmask = mask_rows[:, None] * mask_cols[None, :]
    normed, left, right = project(state, pmask, proj_weight[0])
    left_rows, right_rows = (
        lax.all_gather(left, "col", axis=1, tiled=True),
        lax.all_gather(right, "col", axis=1, tiled=True),
    )
    every = jnp.einsum(
        "ikh,jkh->ijh",
        left_rows,
        lax.all_gather(right_rows, "row", axis=0, tiled=True),
        preferred_element_type=jnp.float32,
    )
    tri = lax.dynamic_slice_in_dim(every, col_start, cols, 1)
    state = finish(state, normed, tri, gate_weight[0], out_weight[0])
    normed, left, right = project(state, pmask, proj_weight[1])
    left_rows = lax.all_gather(left, "col", axis=1, tiled=True)
    left_cols = lax.all_to_all(left_rows, "row", split_axis=1, concat_axis=0, tiled=True)
    tri = jnp.einsum(
        "kih,kjh->ijh",
        left_cols,
        lax.all_gather(right, "row", axis=0, tiled=True),
        preferred_element_type=jnp.float32,
    )
    return finish(state, normed, tri, gate_weight[1], out_weight[1])


def lane_mean(values):
    width = values.shape[-1]
    high = values.astype(jnp.bfloat16)
    low = (values - high.astype(jnp.float32)).astype(jnp.bfloat16)
    share = jnp.full((2 * width, width), 1 / width, jnp.bfloat16)
    return dot(jnp.concatenate([high, low], -1), share)


def tile_norm(values):
    centred = values - lane_mean(values)
    return centred * lax.rsqrt(lane_mean(centred * centred) + 1e-05)


def gate_of(values):
    return 0.5 * jnp.tanh(0.5 * values) + 0.5


def dot(values, weight):
    return jnp.dot(values, weight, preferred_element_type=jnp.float32)


def rounded(values):
    return values.astype(jnp.bfloat16).astype(jnp.float32)


def table(row, out):
    tokens, width = out.shape
    at = lax.broadcasted_iota(jnp.int32, (tokens, tokens), 0)
    lane = lax.broadcasted_iota(jnp.int32, (tokens, tokens), 1)
    spread = jnp.where(at == lane, jnp.broadcast_to(row[...].astype(jnp.float32), (tokens, tokens)), 0.0)
    out[...] = jnp.broadcast_to(jnp.sum(spread, -1, keepdims=True), (tokens, width))


def edges(masks, items, chains, mask, bias, proj_w, gate_w, start, gates, left, right):
    rows, cols, width = items[0][2].shape
    tokens = chains.shape[0]
    me = lax.axis_index("row")
    col = lax.axis_index("col")
    bias_v = bias[...]
    hidden = proj_w.shape[2] // 4
    for half in range(2):
        batch = [(slot, block) for slot, h, block in items if h == half]
        if not batch:
            continue
        first = pl.multiple_of((col if half == 0 else 1 - col) * cols, cols)
        chain_cols = chains[pl.ds(first, cols), :]
        mask_cols = mask[pl.ds(first, cols), :]
        states, pmasks = [], []
        for slot, block in batch:
            for t in range(rows):
                token = (me ^ masks[slot]) * rows + t
                same = chain_cols == chains[pl.ds(token, 1), :]
                states.append(block[t] + jnp.where(same, bias_v, 0.0))
                pmasks.append(mask_cols * mask[pl.ds(token, 1), :])
        state = jnp.concatenate(states, 0)
        pmask = jnp.concatenate(pmasks, 0)
        normed = tile_norm(state).astype(jnp.bfloat16)
        proj = dot(normed, proj_w[0])
        gate = dot(normed, gate_w[0])
        lft = rounded(gate_of(proj[:, :hidden]) * proj[:, hidden : 2 * hidden] * pmask)
        rgt = rounded(gate_of(proj[:, 2 * hidden : 3 * hidden]) * proj[:, 3 * hidden :] * pmask)
        size = rows * cols
        for n, (slot, _) in enumerate(batch):
            span, part = pl.ds(slot * size, size), slice(n * size, (n + 1) * size)
            start[half, span, :] = state[part]
            gates[half, span, :] = gate[part]
            left[half, span, :] = lft[part]
            for t in range(rows):
                token = (me ^ masks[slot]) * rows + t
                at = n * size + t * cols
                right[half, pl.ds(token, cols, tokens), :] = rgt[at : at + cols]


def own_kernel(masks, *refs):
    sources, rest = refs[:7], refs[7:]
    pair, bias, proj_w, gate_w, out_w, chains, mask, start, gates, left, right, chains_v, mask_v, sems = rest
    loads = []
    for n, (source, target) in enumerate(zip(sources, (pair, bias, proj_w, gate_w, out_w, chains_v, mask_v))):
        loads.append(pltpu.make_async_copy(source, target, sems.at[n]))
    for load in loads:
        load.start()
    for load in loads:
        load.wait()
    table(chains_v, chains)
    table(mask_v, mask)
    edges(masks, [(0, 0, pair[...])], chains, mask, bias, proj_w, gate_w, start, gates, left, right)


def mine_kernel(masks, halves, mine, chains, mask, bias, proj_w, gate_w, s_in, g_in, l_in, r_in, *outs):
    items = [(slot, halves[slot], mine[slot]) for slot in range(1, len(masks))]
    edges(masks, items, chains, mask, bias, proj_w, gate_w, *outs)


def crop_kernel(
    masks,
    halves,
    other,
    chains,
    mask,
    bias,
    proj_w,
    gate_w,
    out_w,
    start_in,
    gates_in,
    left_in,
    right_in,
    updated,
    start,
    gates,
    left,
    right,
    tris,
    left1,
    right1,
):
    ranks, rows, cols, width = other.shape
    tokens = ranks * rows
    me = lax.axis_index("row")
    col = lax.axis_index("col")
    hidden = proj_w.shape[2] // 4
    items = [(slot, 1 - halves[slot], other[slot]) for slot in range(ranks)]
    edges(masks, items, chains, mask, bias, proj_w, gate_w, start, gates, left, right)

    low = me * rows // 8 * 8
    groups = [col * cols + 8 * n for n in range(cols // 8)] + [low]
    groups = [pl.multiple_of(g, 8) for g in groups]
    count = len(groups)
    block = 8

    def tri_block(step, carry):
        k0 = step * block
        acc = [[None] * count for _ in range(block)]
        for half in range(2):
            for l in range(cols):
                cells = [right[half, pl.ds(pl.multiple_of(l * tokens + g, 8), 8), :] for g in groups]
                for k in range(block):
                    row = left[half, pl.ds((k0 + k) * cols + l, 1), :]
                    for n in range(count):
                        term = row * cells[n]
                        acc[k][n] = term if half + l == 0 else acc[k][n] + term
        for n in range(count):
            for k in range(block):
                tris[n, pl.ds(pl.multiple_of((k0 + k) * 8, 8), 8), :] = acc[k][n]
        return carry

    lax.fori_loop(0, tokens // block, tri_block, 0)

    low_half = jnp.where(low // cols == col, 0, 1)
    low_off = lax.rem(low, cols)
    mask_left = mask[pl.ds(pl.multiple_of(low, 8), 8), :]
    mask_right = mask[pl.ds(pl.multiple_of(col * cols, cols), cols), :]

    def gather(values, n, k):
        if n < count - 1:
            return values[0, pl.ds(k * cols + 8 * n, 8), :]
        return values[low_half, pl.ds(pl.multiple_of(k * cols + low_off, 8), 8), :]

    def updated_state(n):
        tri = tris[n]
        tnorm = tile_norm(tri).astype(jnp.bfloat16)
        gate = gate_of(jnp.concatenate([gather(gates, n, k) for k in range(tokens)], 0))
        state = jnp.concatenate([gather(start, n, k) for k in range(tokens)], 0)
        return state + gate * dot(tnorm, out_w[0])

    row_masks = []
    for slot in range(ranks):
        for t in range(rows):
            row_masks.append(mask[pl.ds((me ^ masks[slot]) * rows + t, 1), :])

    normed = tile_norm(updated_state(count - 1)).astype(jnp.bfloat16)
    proj = dot(normed, proj_w[1, :, : 2 * hidden])
    edge = gate_of(proj[:, :hidden]) * proj[:, hidden:]
    pm = jnp.concatenate([mask_left * m for m in row_masks], 0)
    left1[...] = rounded(edge * pm)

    own_state, own_logits = [], []
    for n in range(count - 1):
        state = updated_state(n)
        normed = tile_norm(state).astype(jnp.bfloat16)
        own_state.append(state[: rows * 8])
        own_logits.append(dot(normed[: rows * 8], gate_w[1]))
        proj = dot(normed, proj_w[1, :, 2 * hidden :])
        edge = gate_of(proj[:, :hidden]) * proj[:, hidden:]
        pm = jnp.concatenate([mask_right[8 * n : 8 * n + 8] * m for m in row_masks], 0)
        right1[n] = rounded(edge * pm)

    shift = lax.rem(me * rows, 8)
    acc = [[None] * (count - 1) for _ in range(rows)]
    for k in range(tokens):
        cells = [right1[n, pl.ds(k * 8, 8), :] for n in range(count - 1)]
        for t in range(rows):
            row = left1[pl.ds(k * 8 + shift + t, 1), :]
            for n in range(count - 1):
                term = row * cells[n]
                acc[t][n] = term if k == 0 else acc[t][n] + term
    for n in range(count - 1):
        tri = jnp.concatenate([acc[t][n] for t in range(rows)], 0)
        tnorm = tile_norm(tri).astype(jnp.bfloat16)
        out = own_state[n] + gate_of(own_logits[n]) * dot(tnorm, out_w[1])
        for t in range(rows):
            updated[t, pl.ds(8 * n, 8), :] = out[8 * t : 8 * t + 8]


def exchange(block, bits):
    ranks = lax.axis_size("row")
    hops = [(2 * i + c, 2 * (i ^ bits) + 1 - c) for i in range(ranks) for c in range(2)]
    return lax.ppermute(block, ("row", "col"), hops)


def call(body, inputs, outputs, scratch, name, flops, aliases={}, space=pltpu.VMEM):
    return pl.pallas_call(
        body,
        out_shape=outputs,
        in_specs=[pl.BlockSpec(memory_space=space)] * len(inputs),
        out_specs=[pl.BlockSpec(memory_space=pltpu.VMEM)] * len(outputs),
        scratch_shapes=scratch,
        compiler_params=pltpu.CompilerParams(vmem_limit_bytes=32 << 20),
        input_output_aliases=aliases,
        cost_estimate=pl.CostEstimate(flops=flops, bytes_accessed=1 << 21, transcendentals=0),
        name=name,
    )(*inputs)


def floats(*shapes):
    return [jax.ShapeDtypeStruct(shape, jnp.float32) for shape in shapes]


def like(*arrays):
    return [jax.ShapeDtypeStruct(array.shape, array.dtype) for array in arrays]


def whole_crop_plan(pair, token_mask, chains, chain_bias, proj_weight, gate_weight, out_weight):
    rows, cols, width = pair.shape
    ranks = lax.axis_size("row")
    tokens = token_mask.shape[0]
    hidden = proj_weight.shape[2] // 4
    bias = chain_bias[None, :]
    half = [(2, tokens * cols, width), (2, tokens * cols, width), (2, tokens * cols, hidden), (2, tokens * cols, hidden)]
    half = floats(*half)
    flops = 2 * tokens * cols * width * 5 * hidden
    top = ranks // 2
    masks, halves = [0, top], [0, 1]
    for bits in range(1, top):
        masks += [bits, bits ^ top]
        halves += [1, 0]
    far = exchange(pair, top)
    loaded = (pair, bias, proj_weight, gate_weight, out_weight, chains[None, :], token_mask[None, :])
    own, bias, proj_weight, gate_weight, out_weight, chains_t, mask_t, *partial = call(
        functools.partial(own_kernel, masks),
        [pltpu.with_memory_space_constraint(each, pltpu.HBM) for each in loaded],
        like(*loaded[:5]) + floats((tokens, width), (tokens, width)) + half,
        [pltpu.VMEM((1, tokens), jnp.int32), pltpu.VMEM((1, tokens), jnp.int32), pltpu.SemaphoreType.DMA((7,))],
        "own",
        flops // ranks,
        space=pltpu.HBM,
    )
    two = jnp.stack([own, far])
    mine = jnp.concatenate([two] + [exchange(two, bits) for bits in range(1, top)], 0)
    other = lax.ppermute(mine, "col", [(0, 1), (1, 0)])
    edge_inputs = (chains_t, mask_t, bias, proj_weight, gate_weight)
    partial = call(
        functools.partial(mine_kernel, masks, halves),
        (mine, *edge_inputs, *partial),
        half,
        [],
        "mine",
        flops,
        {n + 6: n for n in range(4)},
    )
    groups = cols // 8 + 1
    extra = [(groups, tokens * 8, hidden), (tokens * 8, hidden), (groups - 1, tokens * 8, hidden)]
    return call(
        functools.partial(crop_kernel, masks, halves),
        (other, *edge_inputs, out_weight, *partial),
        floats(pair.shape) + half,
        [pltpu.VMEM(each.shape, jnp.float32) for each in floats(*extra)],
        "crop",
        4 * flops,
        {n + 7: n + 1 for n in range(4)},
    )[0]


def shards(pair, token_mask, *rest):
    tokens = token_mask.shape[0]
    ranks = lax.axis_size("row")
    small = tokens * tokens * pair.shape[2] <= 1 << 18 and ranks & (ranks - 1) == 0 and pair.shape[1] % 8 == 0
    plan = whole_crop_plan if small and lax.axis_size("col") == 2 else sharded_plan
    return plan(pair, token_mask, *rest)


def solution(mesh):
    placed = (P(("group", "row"), "col", None), P("group"), P("group"), P(), P(), P(), P())
    return jax.shard_map(
        shards,
        mesh=mesh,
        in_specs=placed,
        out_specs=P(("group", "row"), "col", None),
        check_vma=False,
    )
```

```python
import functools
import jax
import jax.numpy as jnp
from jax import lax
from jax.experimental import pallas as pl
from jax.experimental.pallas import tpu as pltpu
from jax.sharding import PartitionSpec as P


def layer_norm(values):
    mean = jnp.mean(values, -1, keepdims=True)
    centred = values - mean
    var = jnp.mean(centred * centred, -1, keepdims=True)
    return centred * lax.rsqrt(var + 1e-05)


def flat_dot(values, weight):
    shape = values.shape
    result = jnp.dot(values.reshape(-1, shape[-1]), weight, preferred_element_type=jnp.float32)
    return result.reshape(shape[:-1] + (weight.shape[1],))


def project(state, pmask, p_weight):
    normed = layer_norm(state).astype(jnp.bfloat16)
    proj = flat_dot(normed, p_weight)
    hidden = p_weight.shape[1] // 4
    gate_a = proj[..., :hidden]
    value_a = proj[..., hidden : 2 * hidden]
    gate_b = proj[..., 2 * hidden : 3 * hidden]
    value_b = proj[..., 3 * hidden :]
    left = (jax.nn.sigmoid(gate_a) * value_a * pmask[..., None]).astype(jnp.bfloat16)
    right = (jax.nn.sigmoid(gate_b) * value_b * pmask[..., None]).astype(jnp.bfloat16)
    return (normed, left, right)


def finish(state, normed, tri, g_weight, o_weight):
    tnorm = layer_norm(tri).astype(jnp.bfloat16)
    gate = jax.nn.sigmoid(flat_dot(normed, g_weight))
    return state + gate * flat_dot(tnorm, o_weight)


def sharded_plan(pair, token_mask, chains, chain_bias, proj_weight, gate_weight, out_weight):
    rows, cols, width = pair.shape
    row_start = lax.axis_index("row") * rows
    col_start = lax.axis_index("col") * cols
    chain_rows = lax.dynamic_slice_in_dim(chains, row_start, rows)
    chain_cols = lax.dynamic_slice_in_dim(chains, col_start, cols)
    mask_rows = lax.dynamic_slice_in_dim(token_mask, row_start, rows).astype(jnp.float32)
    mask_cols = lax.dynamic_slice_in_dim(token_mask, col_start, cols).astype(jnp.float32)
    same = (chain_rows[:, None] == chain_cols[None, :]).astype(jnp.float32)
    state = pair + same[..., None] * chain_bias
    pmask = mask_rows[:, None] * mask_cols[None, :]
    normed, left, right = project(state, pmask, proj_weight[0])
    left_rows, right_rows = (
        lax.all_gather(left, "col", axis=1, tiled=True),
        lax.all_gather(right, "col", axis=1, tiled=True),
    )
    every = jnp.einsum(
        "ikh,jkh->ijh",
        left_rows,
        lax.all_gather(right_rows, "row", axis=0, tiled=True),
        preferred_element_type=jnp.float32,
    )
    tri = lax.dynamic_slice_in_dim(every, col_start, cols, 1)
    state = finish(state, normed, tri, gate_weight[0], out_weight[0])
    normed, left, right = project(state, pmask, proj_weight[1])
    left_rows = lax.all_gather(left, "col", axis=1, tiled=True)
    left_cols = lax.all_to_all(left_rows, "row", split_axis=1, concat_axis=0, tiled=True)
    tri = jnp.einsum(
        "kih,kjh->ijh",
        left_cols,
        lax.all_gather(right, "row", axis=0, tiled=True),
        preferred_element_type=jnp.float32,
    )
    return finish(state, normed, tri, gate_weight[1], out_weight[1])


def tile_norm(values):
    mean = jnp.mean(values, -1, keepdims=True)
    centred = values - mean
    var = jnp.mean(centred * centred, -1, keepdims=True)
    return centred * lax.rsqrt(var + 1e-05)


def gate_of(values):
    return 0.5 * jnp.tanh(0.5 * values) + 0.5


def dot(values, weight):
    return jnp.dot(values, weight, preferred_element_type=jnp.float32)


def rounded(values):
    return values.astype(jnp.bfloat16).astype(jnp.float32)


def table(row, out):
    tokens, width = out.shape
    at = lax.broadcasted_iota(jnp.int32, (tokens, tokens), 0)
    lane = lax.broadcasted_iota(jnp.int32, (tokens, tokens), 1)
    spread = jnp.where(at == lane, jnp.broadcast_to(row[...].astype(jnp.float32), (tokens, tokens)), 0.0)
    out[...] = jnp.broadcast_to(jnp.sum(spread, -1, keepdims=True), (tokens, width))


def edges(masks, items, chains, mask, bias, weights, start, gates, left, right):
    rows, cols, width = items[0][2].shape
    tokens = chains.shape[0]
    me = lax.axis_index("row")
    col = lax.axis_index("col")
    bias_v = bias[...]
    hidden = left.shape[-1]
    firsts = [pl.multiple_of(each * cols, cols) for each in (col, 1 - col)]
    chain_cols = [chains[pl.ds(first, cols), :] for first in firsts]
    mask_cols = [mask[pl.ds(first, cols), :] for first in firsts]
    states, pmasks = [], []
    for slot, half, block in items:
        for t in range(rows):
            token = (me ^ masks[slot]) * rows + t
            same = chain_cols[half] == chains[pl.ds(token, 1), :]
            states.append(block[t] + jnp.where(same, bias_v, 0.0))
            pmasks.append(mask_cols[half] * mask[pl.ds(token, 1), :])
    state = jnp.concatenate(states, 0)
    pmask = jnp.concatenate(pmasks, 0)
    proj = dot(tile_norm(state).astype(jnp.bfloat16), weights[0])
    lft = rounded(gate_of(proj[:, :hidden]) * proj[:, hidden : 2 * hidden] * pmask)
    rgt = rounded(gate_of(proj[:, 2 * hidden : 3 * hidden]) * proj[:, 3 * hidden : 4 * hidden] * pmask)
    size = rows * cols
    for n, (slot, half, _) in enumerate(items):
        span, part = pl.ds(slot * size, size), slice(n * size, (n + 1) * size)
        start[half, span, :] = state[part]
        gates[half, span, :] = proj[part, 4 * hidden :]
        left[half, span, :] = lft[part]
        for t in range(rows):
            token = (me ^ masks[slot]) * rows + t
            at = n * size + t * cols
            right[half, pl.ds(token, cols, tokens), :] = rgt[at : at + cols]


def own_kernel(masks, *refs):
    sources, rest = refs[:7], refs[7:]
    pair, bias, weights, out_w, chains, mask, start, gates, left, right, chains_v, mask_v, sems = rest
    split = sources[2].shape[-1]
    proj_w, gate_w = weights.at[:, :, pl.ds(0, split)], weights.at[:, :, pl.ds(split, weights.shape[-1] - split)]
    loads = []
    for n, (source, target) in enumerate(zip(sources, (pair, bias, proj_w, gate_w, out_w, chains_v, mask_v))):
        loads.append(pltpu.make_async_copy(source, target, sems.at[n]))
    for load in loads:
        load.start()
    for load in loads:
        load.wait()
    table(chains_v, chains)
    table(mask_v, mask)
    edges(masks, [(0, 0, pair[...])], chains, mask, bias, weights, start, gates, left, right)


def mine_kernel(masks, halves, mine, chains, mask, bias, weights, s_in, g_in, l_in, r_in, *outs):
    items = [(slot, halves[slot], mine[slot]) for slot in range(1, len(masks))]
    edges(masks, items, chains, mask, bias, weights, *outs)


def crop_kernel(
    masks,
    halves,
    other,
    chains,
    mask,
    bias,
    weights,
    out_w,
    start_in,
    gates_in,
    left_in,
    right_in,
    updated,
    start,
    gates,
    left,
    right,
    tris,
    left1,
    right1,
):
    ranks, rows, cols, width = other.shape
    tokens = ranks * rows
    me = lax.axis_index("row")
    col = lax.axis_index("col")
    hidden = left.shape[-1]
    items = [(slot, 1 - halves[slot], other[slot]) for slot in range(ranks)]
    edges(masks, items, chains, mask, bias, weights, start, gates, left, right)

    low = me * rows // 8 * 8
    groups = [col * cols + 8 * n for n in range(cols // 8)] + [low]
    groups = [pl.multiple_of(g, 8) for g in groups]
    count = len(groups)
    block = 8

    def tri_block(step, carry):
        k0 = step * block
        acc = [[None] * count for _ in range(block)]
        for half in range(2):
            for l in range(cols):
                cells = [right[half, pl.ds(pl.multiple_of(l * tokens + g, 8), 8), :] for g in groups]
                for k in range(block):
                    row = left[half, pl.ds((k0 + k) * cols + l, 1), :]
                    for n in range(count):
                        term = row * cells[n]
                        acc[k][n] = term if half + l == 0 else acc[k][n] + term
        for n in range(count):
            for k in range(block):
                tris[pl.ds(pl.multiple_of((n * tokens + k0 + k) * 8, 8), 8), :] = acc[k][n]
        return carry

    lax.fori_loop(0, tokens // block, tri_block, 0)

    low_half = jnp.where(low // cols == col, 0, 1)
    low_off = lax.rem(low, cols)
    mask_left = mask[pl.ds(pl.multiple_of(low, 8), 8), :]
    mask_right = mask[pl.ds(pl.multiple_of(col * cols, cols), cols), :]

    def gather(values, n, k):
        if n < count - 1:
            return values[0, pl.ds(k * cols + 8 * n, 8), :]
        return values[low_half, pl.ds(pl.multiple_of(k * cols + low_off, 8), 8), :]

    row_masks = []
    for slot in range(ranks):
        for t in range(rows):
            row_masks.append(mask[pl.ds((me ^ masks[slot]) * rows + t, 1), :])

    cells = [(n, k) for n in range(count) for k in range(tokens)]
    tnorm = tile_norm(tris[...]).astype(jnp.bfloat16)
    gate = gate_of(jnp.concatenate([gather(gates, n, k) for n, k in cells], 0))
    state = jnp.concatenate([gather(start, n, k) for n, k in cells], 0)
    state = state + gate * dot(tnorm, out_w[0])
    normed = tile_norm(state).astype(jnp.bfloat16)
    edge_rows = (count - 1) * tokens * 8
    proj_r = dot(normed[:edge_rows], weights[1, :, 2 * hidden : 4 * hidden])
    proj_l = dot(normed[edge_rows:], weights[1, :, : 2 * hidden])
    own = [slice(n * tokens * 8, n * tokens * 8 + rows * 8) for n in range(count - 1)]
    own_state = jnp.concatenate([state[part] for part in own], 0)
    own_logit = dot(jnp.concatenate([normed[part] for part in own], 0), weights[1, :, 4 * hidden :])
    pm = jnp.concatenate([mask_left * m for m in row_masks], 0)
    left1[...] = rounded(gate_of(proj_l[:, :hidden]) * proj_l[:, hidden:] * pm)
    pm = jnp.concatenate([mask_right[8 * n : 8 * n + 8] * m for n in range(count - 1) for m in row_masks], 0)
    right1[...] = rounded(gate_of(proj_r[:, :hidden]) * proj_r[:, hidden:] * pm)

    shift = lax.rem(me * rows, 8)
    acc = [[None] * rows for _ in range(count - 1)]
    for k in range(tokens):
        for n in range(count - 1):
            cell = right1[pl.ds((n * tokens + k) * 8, 8), :]
            for t in range(rows):
                term = left1[pl.ds(k * 8 + shift + t, 1), :] * cell
                acc[n][t] = term if k == 0 else acc[n][t] + term
    tri = jnp.concatenate([acc[n][t] for n in range(count - 1) for t in range(rows)], 0)
    tnorm = tile_norm(tri).astype(jnp.bfloat16)
    out = own_state + gate_of(own_logit) * dot(tnorm, out_w[1])
    for n in range(count - 1):
        for t in range(rows):
            at = (n * rows + t) * 8
            updated[t, pl.ds(8 * n, 8), :] = out[at : at + 8]


def exchange(block, bits):
    ranks = lax.axis_size("row")
    hops = [(2 * i + c, 2 * (i ^ bits) + 1 - c) for i in range(ranks) for c in range(2)]
    return lax.ppermute(block, ("row", "col"), hops)


def call(body, inputs, outputs, scratch, name, flops, aliases={}, space=pltpu.VMEM):
    return pl.pallas_call(
        body,
        out_shape=outputs,
        in_specs=[pl.BlockSpec(memory_space=space)] * len(inputs),
        out_specs=[pl.BlockSpec(memory_space=pltpu.VMEM)] * len(outputs),
        scratch_shapes=scratch,
        compiler_params=pltpu.CompilerParams(vmem_limit_bytes=32 << 20),
        input_output_aliases=aliases,
        cost_estimate=pl.CostEstimate(flops=flops, bytes_accessed=1 << 21, transcendentals=0),
        name=name,
    )(*inputs)


def floats(*shapes):
    return [jax.ShapeDtypeStruct(shape, jnp.float32) for shape in shapes]


def like(*arrays):
    return [jax.ShapeDtypeStruct(array.shape, array.dtype) for array in arrays]


def whole_crop_plan(pair, token_mask, chains, chain_bias, proj_weight, gate_weight, out_weight):
    rows, cols, width = pair.shape
    ranks = lax.axis_size("row")
    tokens = token_mask.shape[0]
    hidden = proj_weight.shape[2] // 4
    bias = chain_bias[None, :]
    half = [(2, tokens * cols, width), (2, tokens * cols, width), (2, tokens * cols, hidden), (2, tokens * cols, hidden)]
    half = floats(*half)
    flops = 2 * tokens * cols * width * 5 * hidden
    top = ranks // 2
    masks, halves = [0, top], [0, 1]
    for bits in range(1, top):
        masks += [bits, bits ^ top]
        halves += [1, 0]
    far = exchange(pair, top)
    loaded = (pair, bias, proj_weight, gate_weight, out_weight, chains[None, :], token_mask[None, :])
    joined = jax.ShapeDtypeStruct((2, width, 4 * hidden + width), proj_weight.dtype)
    own, bias, weights, out_weight, chains_t, mask_t, *partial = call(
        functools.partial(own_kernel, masks),
        [pltpu.with_memory_space_constraint(each, pltpu.HBM) for each in loaded],
        like(pair, bias) + [joined] + like(out_weight) + floats((tokens, width), (tokens, width)) + half,
        [pltpu.VMEM((1, tokens), jnp.int32), pltpu.VMEM((1, tokens), jnp.int32), pltpu.SemaphoreType.DMA((7,))],
        "own",
        flops // ranks,
        space=pltpu.HBM,
    )
    two = jnp.stack([own, far])
    mine = jnp.concatenate([two] + [exchange(two, bits) for bits in range(1, top)], 0)
    other = lax.ppermute(mine, "col", [(0, 1), (1, 0)])
    edge_inputs = (chains_t, mask_t, bias, weights)
    partial = call(
        functools.partial(mine_kernel, masks, halves),
        (mine, *edge_inputs, *partial),
        half,
        [],
        "mine",
        flops,
        {n + 5: n for n in range(4)},
    )
    groups = cols // 8 + 1
    extra = [(groups * tokens * 8, hidden), (tokens * 8, hidden), ((groups - 1) * tokens * 8, hidden)]
    return call(
        functools.partial(crop_kernel, masks, halves),
        (other, *edge_inputs, out_weight, *partial),
        floats(pair.shape) + half,
        [pltpu.VMEM(each.shape, jnp.float32) for each in floats(*extra)],
        "crop",
        4 * flops,
        {n + 6: n + 1 for n in range(4)},
    )[0]


def shards(pair, token_mask, *rest):
    tokens = token_mask.shape[0]
    ranks = lax.axis_size("row")
    small = tokens * tokens * pair.shape[2] <= 1 << 18 and ranks & (ranks - 1) == 0 and pair.shape[1] % 8 == 0
    plan = whole_crop_plan if small and lax.axis_size("col") == 2 else sharded_plan
    return plan(pair, token_mask, *rest)


def solution(mesh):
    placed = (P(("group", "row"), "col", None), P("group"), P("group"), P(), P(), P(), P())
    return jax.shard_map(
        shards,
        mesh=mesh,
        in_specs=placed,
        out_specs=P(("group", "row"), "col", None),
        check_vma=False,
    )
```

```python
import functools
import jax
import jax.numpy as jnp
from jax import lax
from jax.experimental import pallas as pl
from jax.experimental.pallas import tpu as pltpu
from jax.sharding import PartitionSpec as P


def layer_norm(values):
    mean = jnp.mean(values, -1, keepdims=True)
    centred = values - mean
    var = jnp.mean(centred * centred, -1, keepdims=True)
    return centred * lax.rsqrt(var + 1e-05)


def flat_dot(values, weight):
    shape = values.shape
    result = jnp.dot(values.reshape(-1, shape[-1]), weight, preferred_element_type=jnp.float32)
    return result.reshape(shape[:-1] + (weight.shape[1],))


def project(state, pmask, p_weight):
    normed = layer_norm(state).astype(jnp.bfloat16)
    proj = flat_dot(normed, p_weight)
    hidden = p_weight.shape[1] // 4
    gate_a = proj[..., :hidden]
    value_a = proj[..., hidden : 2 * hidden]
    gate_b = proj[..., 2 * hidden : 3 * hidden]
    value_b = proj[..., 3 * hidden :]
    left = (jax.nn.sigmoid(gate_a) * value_a * pmask[..., None]).astype(jnp.bfloat16)
    right = (jax.nn.sigmoid(gate_b) * value_b * pmask[..., None]).astype(jnp.bfloat16)
    return (normed, left, right)


def finish(state, normed, tri, g_weight, o_weight):
    tnorm = layer_norm(tri).astype(jnp.bfloat16)
    gate = jax.nn.sigmoid(flat_dot(normed, g_weight))
    return state + gate * flat_dot(tnorm, o_weight)


def sharded_plan(pair, token_mask, chains, chain_bias, proj_weight, gate_weight, out_weight):
    rows, cols, width = pair.shape
    row_start = lax.axis_index("row") * rows
    col_start = lax.axis_index("col") * cols
    chain_rows = lax.dynamic_slice_in_dim(chains, row_start, rows)
    chain_cols = lax.dynamic_slice_in_dim(chains, col_start, cols)
    mask_rows = lax.dynamic_slice_in_dim(token_mask, row_start, rows).astype(jnp.float32)
    mask_cols = lax.dynamic_slice_in_dim(token_mask, col_start, cols).astype(jnp.float32)
    same = (chain_rows[:, None] == chain_cols[None, :]).astype(jnp.float32)
    state = pair + same[..., None] * chain_bias
    pmask = mask_rows[:, None] * mask_cols[None, :]
    normed, left, right = project(state, pmask, proj_weight[0])
    left_rows, right_rows = (
        lax.all_gather(left, "col", axis=1, tiled=True),
        lax.all_gather(right, "col", axis=1, tiled=True),
    )
    every = jnp.einsum(
        "ikh,jkh->ijh",
        left_rows,
        lax.all_gather(right_rows, "row", axis=0, tiled=True),
        preferred_element_type=jnp.float32,
    )
    tri = lax.dynamic_slice_in_dim(every, col_start, cols, 1)
    state = finish(state, normed, tri, gate_weight[0], out_weight[0])
    normed, left, right = project(state, pmask, proj_weight[1])
    left_rows = lax.all_gather(left, "col", axis=1, tiled=True)
    left_cols = lax.all_to_all(left_rows, "row", split_axis=1, concat_axis=0, tiled=True)
    tri = jnp.einsum(
        "kih,kjh->ijh",
        left_cols,
        lax.all_gather(right, "row", axis=0, tiled=True),
        preferred_element_type=jnp.float32,
    )
    return finish(state, normed, tri, gate_weight[1], out_weight[1])


def tile_norm(values):
    mean = jnp.mean(values, -1, keepdims=True)
    centred = values - mean
    var = jnp.mean(centred * centred, -1, keepdims=True)
    return centred * lax.rsqrt(var + 1e-05)


def gate_of(values):
    return 0.5 * jnp.tanh(0.5 * values) + 0.5


def dot(values, weight):
    return jnp.dot(values, weight, preferred_element_type=jnp.float32)


def rounded(values):
    return values.astype(jnp.bfloat16).astype(jnp.float32)


def table(row, out):
    tokens, width = out.shape
    at = lax.broadcasted_iota(jnp.int32, (tokens, tokens), 0)
    lane = lax.broadcasted_iota(jnp.int32, (tokens, tokens), 1)
    spread = jnp.where(at == lane, jnp.broadcast_to(row[...].astype(jnp.float32), (tokens, tokens)), 0.0)
    out[...] = jnp.broadcast_to(jnp.sum(spread, -1, keepdims=True), (tokens, width))


def edges(masks, items, chains, mask, bias, weights, start, gates, left, right):
    rows, cols, width = items[0][2].shape
    tokens = chains.shape[0]
    me = lax.axis_index("row")
    col = lax.axis_index("col")
    bias_v = bias[...]
    hidden = left.shape[-1]
    firsts = [pl.multiple_of(each * cols, cols) for each in (col, 1 - col)]
    chain_cols = [chains[pl.ds(first, cols), :] for first in firsts]
    mask_cols = [mask[pl.ds(first, cols), :] for first in firsts]
    states, pmasks = [], []
    for slot, half, block in items:
        for t in range(rows):
            token = (me ^ masks[slot]) * rows + t
            same = chain_cols[half] == chains[pl.ds(token, 1), :]
            states.append(block[t] + jnp.where(same, bias_v, 0.0))
            pmasks.append(mask_cols[half] * mask[pl.ds(token, 1), :])
    state = jnp.concatenate(states, 0)
    pmask = jnp.concatenate(pmasks, 0)
    proj = dot(tile_norm(state).astype(jnp.bfloat16), weights[0])
    lft = rounded(gate_of(proj[:, :hidden]) * proj[:, hidden : 2 * hidden] * pmask)
    rgt = rounded(gate_of(proj[:, 2 * hidden : 3 * hidden]) * proj[:, 3 * hidden : 4 * hidden] * pmask)
    size = rows * cols
    for n, (slot, half, _) in enumerate(items):
        span, part = pl.ds(slot * size, size), slice(n * size, (n + 1) * size)
        start[half, span, :] = state[part]
        gates[half, span, :] = proj[part, 4 * hidden :]
        for t in range(rows):
            token = (me ^ masks[slot]) * rows + t
            at = n * size + t * cols
            left[half, slot * rows + t] = lft[at : at + cols]
            right[half, pl.ds(token, cols, tokens), :] = rgt[at : at + cols]


def own_kernel(masks, *refs):
    sources, rest = refs[:7], refs[7:]
    pair, bias, weights, out_w, chains, mask, start, gates, left, right, chains_v, mask_v, sems = rest
    split = sources[2].shape[-1]
    proj_w, gate_w = weights.at[:, :, pl.ds(0, split)], weights.at[:, :, pl.ds(split, weights.shape[-1] - split)]
    loads = []
    for n, (source, target) in enumerate(zip(sources, (pair, bias, proj_w, gate_w, out_w, chains_v, mask_v))):
        loads.append(pltpu.make_async_copy(source, target, sems.at[n]))
    for load in loads:
        load.start()
    for load in loads:
        load.wait()
    table(chains_v, chains)
    table(mask_v, mask)
    edges(masks, [(0, 0, pair[...])], chains, mask, bias, weights, start, gates, left, right)


def mine_kernel(masks, halves, mine, chains, mask, bias, weights, s_in, g_in, l_in, r_in, *outs):
    items = [(slot, halves[slot], mine[slot]) for slot in range(1, len(masks))]
    edges(masks, items, chains, mask, bias, weights, *outs)


def crop_kernel(
    masks,
    halves,
    other,
    chains,
    mask,
    bias,
    weights,
    out_w,
    start_in,
    gates_in,
    left_in,
    right_in,
    updated,
    start,
    gates,
    left,
    right,
    tris,
    left1,
    right1,
):
    ranks, rows, cols, width = other.shape
    tokens = ranks * rows
    me = lax.axis_index("row")
    col = lax.axis_index("col")
    hidden = left.shape[-1]
    items = [(slot, 1 - halves[slot], other[slot]) for slot in range(ranks)]
    edges(masks, items, chains, mask, bias, weights, start, gates, left, right)

    low = me * rows // 8 * 8
    groups = [col * cols + 8 * n for n in range(cols // 8)] + [low]
    groups = [pl.multiple_of(g, 8) for g in groups]
    count = len(groups)
    block = 8

    def tri_block(step, carry):
        k0 = step * block
        acc = [[None] * count for _ in range(block)]
        for half in range(2):
            for l in range(cols):
                cells = [right[half, pl.ds(pl.multiple_of(l * tokens + g, 8), 8), :] for g in groups]
                for k in range(block):
                    row = left[half, k0 + k, pl.ds(l, 1), :]
                    for n in range(count):
                        term = row * cells[n]
                        acc[k][n] = term if half + l == 0 else acc[k][n] + term
        for n in range(count):
            for k in range(block):
                tris[pl.ds(pl.multiple_of((n * tokens + k0 + k) * 8, 8), 8), :] = acc[k][n]
        return carry

    lax.fori_loop(0, tokens // block, tri_block, 0)

    low_half = jnp.where(low // cols == col, 0, 1)
    low_off = lax.rem(low, cols)
    mask_left = mask[pl.ds(pl.multiple_of(low, 8), 8), :]
    mask_right = mask[pl.ds(pl.multiple_of(col * cols, cols), cols), :]

    def gather(values, n, k):
        if n < count - 1:
            return values[0, pl.ds(k * cols + 8 * n, 8), :]
        return values[low_half, pl.ds(pl.multiple_of(k * cols + low_off, 8), 8), :]

    row_masks = []
    for slot in range(ranks):
        for t in range(rows):
            row_masks.append(mask[pl.ds((me ^ masks[slot]) * rows + t, 1), :])

    cells = [(n, k) for n in range(count) for k in range(tokens)]
    tnorm = tile_norm(tris[...]).astype(jnp.bfloat16)
    gate = gate_of(jnp.concatenate([gather(gates, n, k) for n, k in cells], 0))
    state = jnp.concatenate([gather(start, n, k) for n, k in cells], 0)
    state = state + gate * dot(tnorm, out_w[0])
    normed = tile_norm(state).astype(jnp.bfloat16)
    edge_rows = (count - 1) * tokens * 8
    proj_r = dot(normed[:edge_rows], weights[1, :, 2 * hidden : 4 * hidden])
    proj_l = dot(normed[edge_rows:], weights[1, :, : 2 * hidden])
    own = [slice(n * tokens * 8, n * tokens * 8 + rows * 8) for n in range(count - 1)]
    own_state = jnp.concatenate([state[part] for part in own], 0)
    own_logit = dot(jnp.concatenate([normed[part] for part in own], 0), weights[1, :, 4 * hidden :])
    pm = jnp.concatenate([mask_left * m for m in row_masks], 0)
    left1[...] = rounded(gate_of(proj_l[:, :hidden]) * proj_l[:, hidden:] * pm)
    pm = jnp.concatenate([mask_right[8 * n : 8 * n + 8] * m for n in range(count - 1) for m in row_masks], 0)
    right1[...] = rounded(gate_of(proj_r[:, :hidden]) * proj_r[:, hidden:] * pm)

    shift = lax.rem(me * rows, 8)
    acc = [[None] * rows for _ in range(count - 1)]
    for k in range(tokens):
        for n in range(count - 1):
            cell = right1[pl.ds((n * tokens + k) * 8, 8), :]
            for t in range(rows):
                term = left1[pl.ds(k * 8 + shift + t, 1), :] * cell
                acc[n][t] = term if k == 0 else acc[n][t] + term
    tri = jnp.concatenate([acc[n][t] for n in range(count - 1) for t in range(rows)], 0)
    tnorm = tile_norm(tri).astype(jnp.bfloat16)
    out = own_state + gate_of(own_logit) * dot(tnorm, out_w[1])
    for n in range(count - 1):
        for t in range(rows):
            at = (n * rows + t) * 8
            updated[t, pl.ds(8 * n, 8), :] = out[at : at + 8]


def exchange(block, bits):
    ranks = lax.axis_size("row")
    hops = [(2 * i + c, 2 * (i ^ bits) + 1 - c) for i in range(ranks) for c in range(2)]
    return lax.ppermute(block, ("row", "col"), hops)


def call(body, inputs, outputs, scratch, name, flops, aliases={}, space=pltpu.VMEM):
    return pl.pallas_call(
        body,
        out_shape=outputs,
        in_specs=[pl.BlockSpec(memory_space=space)] * len(inputs),
        out_specs=[pl.BlockSpec(memory_space=pltpu.VMEM)] * len(outputs),
        scratch_shapes=scratch,
        compiler_params=pltpu.CompilerParams(vmem_limit_bytes=32 << 20),
        input_output_aliases=aliases,
        cost_estimate=pl.CostEstimate(flops=flops, bytes_accessed=1 << 21, transcendentals=0),
        name=name,
    )(*inputs)


def floats(*shapes):
    return [jax.ShapeDtypeStruct(shape, jnp.float32) for shape in shapes]


def like(*arrays):
    return [jax.ShapeDtypeStruct(array.shape, array.dtype) for array in arrays]


def whole_crop_plan(pair, token_mask, chains, chain_bias, proj_weight, gate_weight, out_weight):
    rows, cols, width = pair.shape
    ranks = lax.axis_size("row")
    tokens = token_mask.shape[0]
    hidden = proj_weight.shape[2] // 4
    bias = chain_bias[None, :]
    half = [(2, tokens * cols, width), (2, tokens * cols, width), (2, tokens, cols, hidden), (2, tokens * cols, hidden)]
    half = floats(*half)
    flops = 2 * tokens * cols * width * 5 * hidden
    top = ranks // 2
    masks, halves = [0, top], [0, 1]
    for bits in range(1, top):
        masks += [bits, bits ^ top]
        halves += [1, 0]
    far = exchange(pair, top)
    loaded = (pair, bias, proj_weight, gate_weight, out_weight, chains[None, :], token_mask[None, :])
    joined = jax.ShapeDtypeStruct((2, width, 4 * hidden + width), proj_weight.dtype)
    own, bias, weights, out_weight, chains_t, mask_t, *partial = call(
        functools.partial(own_kernel, masks),
        [pltpu.with_memory_space_constraint(each, pltpu.HBM) for each in loaded],
        like(pair, bias) + [joined] + like(out_weight) + floats((tokens, width), (tokens, width)) + half,
        [pltpu.VMEM((1, tokens), jnp.int32), pltpu.VMEM((1, tokens), jnp.int32), pltpu.SemaphoreType.DMA((7,))],
        "own",
        flops // ranks,
        space=pltpu.HBM,
    )
    two = jnp.stack([own, far])
    mine = jnp.concatenate([two] + [exchange(two, bits) for bits in range(1, top)], 0)
    other = lax.ppermute(mine, "col", [(0, 1), (1, 0)])
    edge_inputs = (chains_t, mask_t, bias, weights)
    partial = call(
        functools.partial(mine_kernel, masks, halves),
        (mine, *edge_inputs, *partial),
        half,
        [],
        "mine",
        flops,
        {n + 5: n for n in range(4)},
    )
    groups = cols // 8 + 1
    extra = [(groups * tokens * 8, hidden), (tokens * 8, hidden), ((groups - 1) * tokens * 8, hidden)]
    return call(
        functools.partial(crop_kernel, masks, halves),
        (other, *edge_inputs, out_weight, *partial),
        floats(pair.shape) + half,
        [pltpu.VMEM(each.shape, jnp.float32) for each in floats(*extra)],
        "crop",
        4 * flops,
        {n + 6: n + 1 for n in range(4)},
    )[0]


def shards(pair, token_mask, *rest):
    tokens = token_mask.shape[0]
    ranks = lax.axis_size("row")
    small = tokens * tokens * pair.shape[2] <= 1 << 18 and ranks & (ranks - 1) == 0 and pair.shape[1] % 8 == 0
    plan = whole_crop_plan if small and lax.axis_size("col") == 2 else sharded_plan
    return plan(pair, token_mask, *rest)


def solution(mesh):
    placed = (P(("group", "row"), "col", None), P("group"), P("group"), P(), P(), P(), P())
    return jax.shard_map(
        shards,
        mesh=mesh,
        in_specs=placed,
        out_specs=P(("group", "row"), "col", None),
        check_vma=False,
    )
```

```python
import functools
import jax
import jax.numpy as jnp
from jax import lax
from jax.experimental import pallas as pl
from jax.experimental.pallas import tpu as pltpu
from jax.sharding import PartitionSpec as P


def layer_norm(values):
    mean = jnp.mean(values, -1, keepdims=True)
    centred = values - mean
    var = jnp.mean(centred * centred, -1, keepdims=True)
    return centred * lax.rsqrt(var + 1e-05)


def flat_dot(values, weight):
    shape = values.shape
    result = jnp.dot(values.reshape(-1, shape[-1]), weight, preferred_element_type=jnp.float32)
    return result.reshape(shape[:-1] + (weight.shape[1],))


def project(state, pmask, p_weight):
    normed = layer_norm(state).astype(jnp.bfloat16)
    proj = flat_dot(normed, p_weight)
    hidden = p_weight.shape[1] // 4
    gate_a = proj[..., :hidden]
    value_a = proj[..., hidden : 2 * hidden]
    gate_b = proj[..., 2 * hidden : 3 * hidden]
    value_b = proj[..., 3 * hidden :]
    left = (jax.nn.sigmoid(gate_a) * value_a * pmask[..., None]).astype(jnp.bfloat16)
    right = (jax.nn.sigmoid(gate_b) * value_b * pmask[..., None]).astype(jnp.bfloat16)
    return (normed, left, right)


def finish(state, normed, tri, g_weight, o_weight):
    tnorm = layer_norm(tri).astype(jnp.bfloat16)
    gate = jax.nn.sigmoid(flat_dot(normed, g_weight))
    return state + gate * flat_dot(tnorm, o_weight)


def sharded_plan(pair, token_mask, chains, chain_bias, proj_weight, gate_weight, out_weight):
    rows, cols, width = pair.shape
    row_start = lax.axis_index("row") * rows
    col_start = lax.axis_index("col") * cols
    chain_rows = lax.dynamic_slice_in_dim(chains, row_start, rows)
    chain_cols = lax.dynamic_slice_in_dim(chains, col_start, cols)
    mask_rows = lax.dynamic_slice_in_dim(token_mask, row_start, rows).astype(jnp.float32)
    mask_cols = lax.dynamic_slice_in_dim(token_mask, col_start, cols).astype(jnp.float32)
    same = (chain_rows[:, None] == chain_cols[None, :]).astype(jnp.float32)
    state = pair + same[..., None] * chain_bias
    pmask = mask_rows[:, None] * mask_cols[None, :]
    normed, left, right = project(state, pmask, proj_weight[0])
    left_rows, right_rows = (
        lax.all_gather(left, "col", axis=1, tiled=True),
        lax.all_gather(right, "col", axis=1, tiled=True),
    )
    every = jnp.einsum(
        "ikh,jkh->ijh",
        left_rows,
        lax.all_gather(right_rows, "row", axis=0, tiled=True),
        preferred_element_type=jnp.float32,
    )
    tri = lax.dynamic_slice_in_dim(every, col_start, cols, 1)
    state = finish(state, normed, tri, gate_weight[0], out_weight[0])
    normed, left, right = project(state, pmask, proj_weight[1])
    left_rows = lax.all_gather(left, "col", axis=1, tiled=True)
    left_cols = lax.all_to_all(left_rows, "row", split_axis=1, concat_axis=0, tiled=True)
    tri = jnp.einsum(
        "kih,kjh->ijh",
        left_cols,
        lax.all_gather(right, "row", axis=0, tiled=True),
        preferred_element_type=jnp.float32,
    )
    return finish(state, normed, tri, gate_weight[1], out_weight[1])


def tile_norm(values):
    mean = jnp.mean(values, -1, keepdims=True)
    centred = values - mean
    var = jnp.mean(centred * centred, -1, keepdims=True)
    return centred * lax.rsqrt(var + 1e-05)


def gate_of(values):
    return 0.5 * jnp.tanh(0.5 * values) + 0.5


def dot(values, weight):
    return jnp.dot(values, weight, preferred_element_type=jnp.float32)


def rounded(values):
    return values.astype(jnp.bfloat16).astype(jnp.float32)


def table(row, out):
    tokens, width = out.shape
    at = lax.broadcasted_iota(jnp.int32, (tokens, tokens), 0)
    lane = lax.broadcasted_iota(jnp.int32, (tokens, tokens), 1)
    spread = jnp.where(at == lane, jnp.broadcast_to(row[...].astype(jnp.float32), (tokens, tokens)), 0.0)
    out[...] = jnp.broadcast_to(jnp.sum(spread, -1, keepdims=True), (tokens, width))


def edges(masks, items, chains, mask, bias, weights, start, gates, left, right):
    rows, cols, width = items[0][2].shape
    tokens = chains.shape[0]
    me = lax.axis_index("row")
    col = lax.axis_index("col")
    bias_v = bias[...]
    hidden = left.shape[-1]
    firsts = [pl.multiple_of(each * cols, cols) for each in (col, 1 - col)]
    chain_cols = [chains[pl.ds(first, cols), :] for first in firsts]
    mask_cols = [mask[pl.ds(first, cols), :] for first in firsts]
    states, pmasks = [], []
    for slot, half, block in items:
        for t in range(rows):
            token = (me ^ masks[slot]) * rows + t
            same = chain_cols[half] == chains[pl.ds(token, 1), :]
            states.append(block[t] + jnp.where(same, bias_v, 0.0))
            pmasks.append(mask_cols[half] * mask[pl.ds(token, 1), :])
    state = jnp.concatenate(states, 0)
    pmask = jnp.concatenate(pmasks, 0)
    proj = dot(tile_norm(state).astype(jnp.bfloat16), weights[0])
    lft = rounded(gate_of(proj[:, :hidden]) * proj[:, hidden : 2 * hidden] * pmask)
    rgt = rounded(gate_of(proj[:, 2 * hidden : 3 * hidden]) * proj[:, 3 * hidden : 4 * hidden] * pmask)
    size = rows * cols
    for n, (slot, half, _) in enumerate(items):
        span, part = pl.ds(slot * size, size), slice(n * size, (n + 1) * size)
        start[half, span, :] = state[part]
        gates[half, span, :] = proj[part, 4 * hidden :]
        for t in range(rows):
            token = (me ^ masks[slot]) * rows + t
            at = n * size + t * cols
            left[half, slot * rows + t] = lft[at : at + cols]
            right[half, pl.ds(token, cols, tokens), :] = rgt[at : at + cols]


def prep_kernel(*refs):
    sources, rest = refs[:7], refs[7:]
    pair, bias, weights, out_w, chains, mask, chains_v, mask_v, sems = rest
    split = sources[2].shape[-1]
    proj_w, gate_w = weights.at[:, :, pl.ds(0, split)], weights.at[:, :, pl.ds(split, weights.shape[-1] - split)]
    loads = []
    for n, (source, target) in enumerate(zip(sources, (pair, bias, proj_w, gate_w, out_w, chains_v, mask_v))):
        loads.append(pltpu.make_async_copy(source, target, sems.at[n]))
    for load in loads:
        load.start()
    for load in loads:
        load.wait()
    table(chains_v, chains)
    table(mask_v, mask)


def mine_kernel(masks, halves, mine, chains, mask, bias, weights, *outs):
    items = [(slot, halves[slot], mine[slot]) for slot in range(len(masks))]
    edges(masks, items, chains, mask, bias, weights, *outs)


def crop_kernel(
    masks,
    halves,
    other,
    chains,
    mask,
    bias,
    weights,
    out_w,
    start_in,
    gates_in,
    left_in,
    right_in,
    updated,
    start,
    gates,
    left,
    right,
    tris,
    left1,
    right1,
):
    ranks, rows, cols, width = other.shape
    tokens = ranks * rows
    me = lax.axis_index("row")
    col = lax.axis_index("col")
    hidden = left.shape[-1]
    items = [(slot, 1 - halves[slot], other[slot]) for slot in range(ranks)]
    edges(masks, items, chains, mask, bias, weights, start, gates, left, right)

    low = me * rows // 8 * 8
    groups = [col * cols + 8 * n for n in range(cols // 8)] + [low]
    groups = [pl.multiple_of(g, 8) for g in groups]
    count = len(groups)
    block = 8

    def tri_block(step, carry):
        k0 = step * block
        acc = [[None] * count for _ in range(block)]
        for half in range(2):
            for l in range(cols):
                cells = [right[half, pl.ds(pl.multiple_of(l * tokens + g, 8), 8), :] for g in groups]
                for k in range(block):
                    row = left[half, k0 + k, pl.ds(l, 1), :]
                    for n in range(count):
                        term = row * cells[n]
                        acc[k][n] = term if half + l == 0 else acc[k][n] + term
        for n in range(count):
            for k in range(block):
                tris[pl.ds(pl.multiple_of((n * tokens + k0 + k) * 8, 8), 8), :] = acc[k][n]
        return carry

    lax.fori_loop(0, tokens // block, tri_block, 0)

    low_half = jnp.where(low // cols == col, 0, 1)
    low_off = lax.rem(low, cols)
    mask_left = mask[pl.ds(pl.multiple_of(low, 8), 8), :]
    mask_right = mask[pl.ds(pl.multiple_of(col * cols, cols), cols), :]

    def gather(values, n, k):
        if n < count - 1:
            return values[0, pl.ds(k * cols + 8 * n, 8), :]
        return values[low_half, pl.ds(pl.multiple_of(k * cols + low_off, 8), 8), :]

    row_masks = []
    for slot in range(ranks):
        for t in range(rows):
            row_masks.append(mask[pl.ds((me ^ masks[slot]) * rows + t, 1), :])

    cells = [(n, k) for n in range(count) for k in range(tokens)]
    tnorm = tile_norm(tris[...]).astype(jnp.bfloat16)
    gate = gate_of(jnp.concatenate([gather(gates, n, k) for n, k in cells], 0))
    state = jnp.concatenate([gather(start, n, k) for n, k in cells], 0)
    state = state + gate * dot(tnorm, out_w[0])
    normed = tile_norm(state).astype(jnp.bfloat16)
    edge_rows = (count - 1) * tokens * 8
    proj_r = dot(normed[:edge_rows], weights[1, :, 2 * hidden : 4 * hidden])
    proj_l = dot(normed[edge_rows:], weights[1, :, : 2 * hidden])
    own = [slice(n * tokens * 8, n * tokens * 8 + rows * 8) for n in range(count - 1)]
    own_state = jnp.concatenate([state[part] for part in own], 0)
    own_logit = dot(jnp.concatenate([normed[part] for part in own], 0), weights[1, :, 4 * hidden :])
    pm = jnp.concatenate([mask_left * m for m in row_masks], 0)
    left1[...] = rounded(gate_of(proj_l[:, :hidden]) * proj_l[:, hidden:] * pm)
    pm = jnp.concatenate([mask_right[8 * n : 8 * n + 8] * m for n in range(count - 1) for m in row_masks], 0)
    right1[...] = rounded(gate_of(proj_r[:, :hidden]) * proj_r[:, hidden:] * pm)

    shift = lax.rem(me * rows, 8)
    acc = [[None] * rows for _ in range(count - 1)]
    for k in range(tokens):
        for n in range(count - 1):
            cell = right1[pl.ds((n * tokens + k) * 8, 8), :]
            for t in range(rows):
                term = left1[pl.ds(k * 8 + shift + t, 1), :] * cell
                acc[n][t] = term if k == 0 else acc[n][t] + term
    tri = jnp.concatenate([acc[n][t] for n in range(count - 1) for t in range(rows)], 0)
    tnorm = tile_norm(tri).astype(jnp.bfloat16)
    out = own_state + gate_of(own_logit) * dot(tnorm, out_w[1])
    for n in range(count - 1):
        for t in range(rows):
            at = (n * rows + t) * 8
            updated[t, pl.ds(8 * n, 8), :] = out[at : at + 8]


def exchange(block, bits):
    ranks = lax.axis_size("row")
    hops = [(2 * i + c, 2 * (i ^ bits) + 1 - c) for i in range(ranks) for c in range(2)]
    return lax.ppermute(block, ("row", "col"), hops)


def call(body, inputs, outputs, scratch, name, flops, aliases={}, space=pltpu.VMEM):
    return pl.pallas_call(
        body,
        out_shape=outputs,
        in_specs=[pl.BlockSpec(memory_space=space)] * len(inputs),
        out_specs=[pl.BlockSpec(memory_space=pltpu.VMEM)] * len(outputs),
        scratch_shapes=scratch,
        compiler_params=pltpu.CompilerParams(vmem_limit_bytes=32 << 20),
        input_output_aliases=aliases,
        cost_estimate=pl.CostEstimate(flops=flops, bytes_accessed=1 << 21, transcendentals=0),
        name=name,
    )(*inputs)


def floats(*shapes):
    return [jax.ShapeDtypeStruct(shape, jnp.float32) for shape in shapes]


def like(*arrays):
    return [jax.ShapeDtypeStruct(array.shape, array.dtype) for array in arrays]


def whole_crop_plan(pair, token_mask, chains, chain_bias, proj_weight, gate_weight, out_weight):
    rows, cols, width = pair.shape
    ranks = lax.axis_size("row")
    tokens = token_mask.shape[0]
    hidden = proj_weight.shape[2] // 4
    bias = chain_bias[None, :]
    half = [(2, tokens * cols, width), (2, tokens * cols, width), (2, tokens, cols, hidden), (2, tokens * cols, hidden)]
    half = floats(*half)
    flops = 2 * tokens * cols * width * 5 * hidden
    top = ranks // 2
    masks, halves = [0, top], [0, 1]
    for bits in range(1, top):
        masks += [bits, bits ^ top]
        halves += [1, 0]
    far = exchange(pair, top)
    loaded = (pair, bias, proj_weight, gate_weight, out_weight, chains[None, :], token_mask[None, :])
    joined = jax.ShapeDtypeStruct((2, width, 4 * hidden + width), proj_weight.dtype)
    own, bias, weights, out_weight, chains_t, mask_t = call(
        prep_kernel,
        [pltpu.with_memory_space_constraint(each, pltpu.HBM) for each in loaded],
        like(pair, bias) + [joined] + like(out_weight) + floats((tokens, width), (tokens, width)),
        [pltpu.VMEM((1, tokens), jnp.int32), pltpu.VMEM((1, tokens), jnp.int32), pltpu.SemaphoreType.DMA((7,))],
        "prep",
        flops // ranks,
        space=pltpu.HBM,
    )
    near = [bits for bits in range(1, top) if bits & (bits - 1) == 0]
    sent = {bits: exchange(own, bits) for bits in near}
    two = jnp.stack([own, far])
    parts = [own[None], far[None]]
    for bits in range(1, top):
        if bits in sent:
            parts += [sent[bits][None], exchange(far, bits)[None]]
        else:
            parts.append(exchange(two, bits))
    mine = jnp.concatenate(parts, 0)
    other = lax.ppermute(mine, "col", [(0, 1), (1, 0)])
    edge_inputs = (chains_t, mask_t, bias, weights)
    partial = call(
        functools.partial(mine_kernel, masks, halves),
        (mine, *edge_inputs),
        half,
        [],
        "mine",
        flops,
    )
    groups = cols // 8 + 1
    extra = [(groups * tokens * 8, hidden), (tokens * 8, hidden), ((groups - 1) * tokens * 8, hidden)]
    return call(
        functools.partial(crop_kernel, masks, halves),
        (other, *edge_inputs, out_weight, *partial),
        floats(pair.shape) + half,
        [pltpu.VMEM(each.shape, jnp.float32) for each in floats(*extra)],
        "crop",
        4 * flops,
        {n + 6: n + 1 for n in range(4)},
    )[0]


def shards(pair, token_mask, *rest):
    tokens = token_mask.shape[0]
    ranks = lax.axis_size("row")
    small = tokens * tokens * pair.shape[2] <= 1 << 18 and ranks & (ranks - 1) == 0 and pair.shape[1] % 8 == 0
    plan = whole_crop_plan if small and lax.axis_size("col") == 2 else sharded_plan
    return plan(pair, token_mask, *rest)


def solution(mesh):
    placed = (P(("group", "row"), "col", None), P("group"), P("group"), P(), P(), P(), P())
    return jax.shard_map(
        shards,
        mesh=mesh,
        in_specs=placed,
        out_specs=P(("group", "row"), "col", None),
        check_vma=False,
    )
```

```python
import functools
import jax
import jax.numpy as jnp
from jax import lax
from jax.experimental import pallas as pl
from jax.experimental.pallas import tpu as pltpu
from jax.sharding import PartitionSpec as P


def layer_norm(values):
    mean = jnp.mean(values, -1, keepdims=True)
    centred = values - mean
    var = jnp.mean(centred * centred, -1, keepdims=True)
    return centred * lax.rsqrt(var + 1e-05)


def flat_dot(values, weight):
    shape = values.shape
    result = jnp.dot(values.reshape(-1, shape[-1]), weight, preferred_element_type=jnp.float32)
    return result.reshape(shape[:-1] + (weight.shape[1],))


def project(state, pmask, p_weight):
    normed = layer_norm(state).astype(jnp.bfloat16)
    proj = flat_dot(normed, p_weight)
    hidden = p_weight.shape[1] // 4
    gate_a = proj[..., :hidden]
    value_a = proj[..., hidden : 2 * hidden]
    gate_b = proj[..., 2 * hidden : 3 * hidden]
    value_b = proj[..., 3 * hidden :]
    left = (jax.nn.sigmoid(gate_a) * value_a * pmask[..., None]).astype(jnp.bfloat16)
    right = (jax.nn.sigmoid(gate_b) * value_b * pmask[..., None]).astype(jnp.bfloat16)
    return (normed, left, right)


def finish(state, normed, tri, g_weight, o_weight):
    tnorm = layer_norm(tri).astype(jnp.bfloat16)
    gate = jax.nn.sigmoid(flat_dot(normed, g_weight))
    return state + gate * flat_dot(tnorm, o_weight)


def sharded_plan(pair, token_mask, chains, chain_bias, proj_weight, gate_weight, out_weight):
    rows, cols, width = pair.shape
    row_start = lax.axis_index("row") * rows
    col_start = lax.axis_index("col") * cols
    chain_rows = lax.dynamic_slice_in_dim(chains, row_start, rows)
    chain_cols = lax.dynamic_slice_in_dim(chains, col_start, cols)
    mask_rows = lax.dynamic_slice_in_dim(token_mask, row_start, rows).astype(jnp.float32)
    mask_cols = lax.dynamic_slice_in_dim(token_mask, col_start, cols).astype(jnp.float32)
    same = (chain_rows[:, None] == chain_cols[None, :]).astype(jnp.float32)
    state = pair + same[..., None] * chain_bias
    pmask = mask_rows[:, None] * mask_cols[None, :]
    normed, left, right = project(state, pmask, proj_weight[0])
    left_rows, right_rows = (
        lax.all_gather(left, "col", axis=1, tiled=True),
        lax.all_gather(right, "col", axis=1, tiled=True),
    )
    every = jnp.einsum(
        "ikh,jkh->ijh",
        left_rows,
        lax.all_gather(right_rows, "row", axis=0, tiled=True),
        preferred_element_type=jnp.float32,
    )
    tri = lax.dynamic_slice_in_dim(every, col_start, cols, 1)
    state = finish(state, normed, tri, gate_weight[0], out_weight[0])
    normed, left, right = project(state, pmask, proj_weight[1])
    left_rows = lax.all_gather(left, "col", axis=1, tiled=True)
    left_cols = lax.all_to_all(left_rows, "row", split_axis=1, concat_axis=0, tiled=True)
    tri = jnp.einsum(
        "kih,kjh->ijh",
        left_cols,
        lax.all_gather(right, "row", axis=0, tiled=True),
        preferred_element_type=jnp.float32,
    )
    return finish(state, normed, tri, gate_weight[1], out_weight[1])


def tile_norm(values):
    mean = jnp.mean(values, -1, keepdims=True)
    centred = values - mean
    var = jnp.mean(centred * centred, -1, keepdims=True)
    return centred * lax.rsqrt(var + 1e-05)


def gate_of(values):
    return 0.5 * jnp.tanh(0.5 * values) + 0.5


def dot(values, weight):
    return jnp.dot(values, weight, preferred_element_type=jnp.float32)


def rounded(values):
    return values.astype(jnp.bfloat16).astype(jnp.float32)


def table(row, out):
    tokens, width = out.shape
    at = lax.broadcasted_iota(jnp.int32, (tokens, tokens), 0)
    lane = lax.broadcasted_iota(jnp.int32, (tokens, tokens), 1)
    spread = jnp.where(at == lane, jnp.broadcast_to(row[...].astype(jnp.float32), (tokens, tokens)), 0.0)
    out[...] = jnp.broadcast_to(jnp.sum(spread, -1, keepdims=True), (tokens, width))


def edges(masks, items, chains, mask, bias, weights, start, gates, left, right):
    rows, cols, width = items[0][2].shape
    tokens = chains.shape[0]
    me = lax.axis_index("row")
    col = lax.axis_index("col")
    bias_v = bias[...]
    hidden = left.shape[-1]
    firsts = [pl.multiple_of(each * cols, cols) for each in (col, 1 - col)]
    chain_cols = [chains[pl.ds(first, cols), :] for first in firsts]
    mask_cols = [mask[pl.ds(first, cols), :] for first in firsts]
    states, pmasks = [], []
    for slot, half, block in items:
        for t in range(rows):
            token = (me ^ masks[slot]) * rows + t
            same = chain_cols[half] == chains[pl.ds(token, 1), :]
            states.append(block[t] + jnp.where(same, bias_v, 0.0))
            pmasks.append(mask_cols[half] * mask[pl.ds(token, 1), :])
    state = jnp.concatenate(states, 0)
    pmask = jnp.concatenate(pmasks, 0)
    proj = dot(tile_norm(state).astype(jnp.bfloat16), weights[0])
    lft = rounded(gate_of(proj[:, :hidden]) * proj[:, hidden : 2 * hidden] * pmask)
    rgt = rounded(gate_of(proj[:, 2 * hidden : 3 * hidden]) * proj[:, 3 * hidden : 4 * hidden] * pmask)
    size = rows * cols
    for n, (slot, half, _) in enumerate(items):
        span, part = pl.ds(slot * size, size), slice(n * size, (n + 1) * size)
        start[half, span, :] = state[part]
        gates[half, span, :] = proj[part, 4 * hidden :]
        for t in range(rows):
            token = (me ^ masks[slot]) * rows + t
            at = n * size + t * cols
            left[half, slot * rows + t] = lft[at : at + cols]
            right[half, pl.ds(token, cols, tokens), :] = rgt[at : at + cols]


def prep_kernel(masks, halves, early, *refs):
    blocks, refs = refs[: len(early)], refs[len(early) :]
    sources, rest = refs[:7], refs[7:]
    pair, bias, weights, out_w, chains, mask, start, gates, left, right, chains_v, mask_v, sems = rest
    split = sources[2].shape[-1]
    proj_w, gate_w = weights.at[:, :, pl.ds(0, split)], weights.at[:, :, pl.ds(split, weights.shape[-1] - split)]
    loads = []
    for n, (source, target) in enumerate(zip(sources, (pair, bias, proj_w, gate_w, out_w, chains_v, mask_v))):
        loads.append(pltpu.make_async_copy(source, target, sems.at[n]))
    for load in loads:
        load.start()
    for load in loads:
        load.wait()
    table(chains_v, chains)
    table(mask_v, mask)
    items = [(len(masks) - 1, halves[-1], pair[...])] + [(slot, halves[slot], block[...]) for slot, block in zip(early, blocks)]
    edges(masks, items, chains, mask, bias, weights, start, gates, left, right)


def mine_kernel(masks, halves, early, mine, chains, mask, bias, weights, s_in, g_in, l_in, r_in, *outs):
    items = [(slot, halves[slot], mine[slot]) for slot in range(len(masks) - 1) if slot not in early]
    edges(masks, items, chains, mask, bias, weights, *outs)


def crop_kernel(
    masks,
    halves,
    other,
    chains,
    mask,
    bias,
    weights,
    out_w,
    start_in,
    gates_in,
    left_in,
    right_in,
    updated,
    start,
    gates,
    left,
    right,
    tris,
    left1,
    right1,
):
    ranks, rows, cols, width = other.shape
    tokens = ranks * rows
    me = lax.axis_index("row")
    col = lax.axis_index("col")
    hidden = left.shape[-1]
    items = [(slot, 1 - halves[slot], other[slot]) for slot in range(ranks)]
    edges(masks, items, chains, mask, bias, weights, start, gates, left, right)

    low = me * rows // 8 * 8
    groups = [col * cols + 8 * n for n in range(cols // 8)] + [low]
    groups = [pl.multiple_of(g, 8) for g in groups]
    count = len(groups)
    block = 8

    def tri_block(step, carry):
        k0 = step * block
        acc = [[None] * count for _ in range(block)]
        for half in range(2):
            for l in range(cols):
                cells = [right[half, pl.ds(pl.multiple_of(l * tokens + g, 8), 8), :] for g in groups]
                for k in range(block):
                    row = left[half, k0 + k, pl.ds(l, 1), :]
                    for n in range(count):
                        term = row * cells[n]
                        acc[k][n] = term if half + l == 0 else acc[k][n] + term
        for n in range(count):
            for k in range(block):
                tris[pl.ds(pl.multiple_of((n * tokens + k0 + k) * 8, 8), 8), :] = acc[k][n]
        return carry

    lax.fori_loop(0, tokens // block, tri_block, 0)

    low_half = jnp.where(low // cols == col, 0, 1)
    low_off = lax.rem(low, cols)
    mask_left = mask[pl.ds(pl.multiple_of(low, 8), 8), :]
    mask_right = mask[pl.ds(pl.multiple_of(col * cols, cols), cols), :]

    def gather(values, n, k):
        if n < count - 1:
            return values[0, pl.ds(k * cols + 8 * n, 8), :]
        return values[low_half, pl.ds(pl.multiple_of(k * cols + low_off, 8), 8), :]

    row_masks = []
    for slot in range(ranks):
        for t in range(rows):
            row_masks.append(mask[pl.ds((me ^ masks[slot]) * rows + t, 1), :])

    cells = [(n, k) for n in range(count) for k in range(tokens)]
    tnorm = tile_norm(tris[...]).astype(jnp.bfloat16)
    gate = gate_of(jnp.concatenate([gather(gates, n, k) for n, k in cells], 0))
    state = jnp.concatenate([gather(start, n, k) for n, k in cells], 0)
    state = state + gate * dot(tnorm, out_w[0])
    normed = tile_norm(state).astype(jnp.bfloat16)
    edge_rows = (count - 1) * tokens * 8
    proj_r = dot(normed[:edge_rows], weights[1, :, 2 * hidden : 4 * hidden])
    proj_l = dot(normed[edge_rows:], weights[1, :, : 2 * hidden])
    ends = [(n + 1) * tokens * 8 for n in range(count - 1)]
    own = [slice(end - rows * 8, end) for end in ends]
    own_state = jnp.concatenate([state[part] for part in own], 0)
    own_logit = dot(jnp.concatenate([normed[part] for part in own], 0), weights[1, :, 4 * hidden :])
    pm = jnp.concatenate([mask_left * m for m in row_masks], 0)
    left1[...] = rounded(gate_of(proj_l[:, :hidden]) * proj_l[:, hidden:] * pm)
    pm = jnp.concatenate([mask_right[8 * n : 8 * n + 8] * m for n in range(count - 1) for m in row_masks], 0)
    right1[...] = rounded(gate_of(proj_r[:, :hidden]) * proj_r[:, hidden:] * pm)

    shift = lax.rem(me * rows, 8)
    acc = [[None] * rows for _ in range(count - 1)]
    for k in range(tokens):
        for n in range(count - 1):
            cell = right1[pl.ds((n * tokens + k) * 8, 8), :]
            for t in range(rows):
                term = left1[pl.ds(k * 8 + shift + t, 1), :] * cell
                acc[n][t] = term if k == 0 else acc[n][t] + term
    tri = jnp.concatenate([acc[n][t] for n in range(count - 1) for t in range(rows)], 0)
    tnorm = tile_norm(tri).astype(jnp.bfloat16)
    out = own_state + gate_of(own_logit) * dot(tnorm, out_w[1])
    for n in range(count - 1):
        for t in range(rows):
            at = (n * rows + t) * 8
            updated[t, pl.ds(8 * n, 8), :] = out[at : at + 8]


def exchange(block, bits):
    ranks = lax.axis_size("row")
    hops = [(2 * i + c, 2 * (i ^ bits) + 1 - c) for i in range(ranks) for c in range(2)]
    return lax.ppermute(block, ("row", "col"), hops)


def call(body, inputs, outputs, scratch, name, flops, aliases={}, spaces=None):
    return pl.pallas_call(
        body,
        out_shape=outputs,
        in_specs=[pl.BlockSpec(memory_space=each) for each in spaces or [pltpu.VMEM] * len(inputs)],
        out_specs=[pl.BlockSpec(memory_space=pltpu.VMEM)] * len(outputs),
        scratch_shapes=scratch,
        compiler_params=pltpu.CompilerParams(vmem_limit_bytes=32 << 20),
        input_output_aliases=aliases,
        cost_estimate=pl.CostEstimate(flops=flops, bytes_accessed=1 << 21, transcendentals=0),
        name=name,
    )(*inputs)


def floats(*shapes):
    return [jax.ShapeDtypeStruct(shape, jnp.float32) for shape in shapes]


def like(*arrays):
    return [jax.ShapeDtypeStruct(array.shape, array.dtype) for array in arrays]


def whole_crop_plan(pair, token_mask, chains, chain_bias, proj_weight, gate_weight, out_weight):
    rows, cols, width = pair.shape
    ranks = lax.axis_size("row")
    tokens = token_mask.shape[0]
    hidden = proj_weight.shape[2] // 4
    bias = chain_bias[None, :]
    half = [(2, tokens * cols, width), (2, tokens * cols, width), (2, tokens, cols, hidden), (2, tokens * cols, hidden)]
    half = floats(*half)
    flops = 2 * tokens * cols * width * 5 * hidden
    top = ranks // 2
    masks, halves = [top], [1]
    for bits in range(1, top):
        masks += [bits, bits ^ top]
        halves += [1, 0]
    masks, halves = masks + [0], halves + [0]
    near = [bits for bits in range(1, top) if bits & (bits - 1) == 0]
    early = [masks.index(bits) for bits in [top] + near]
    far = exchange(pair, top)
    sent = {bits: exchange(pair, bits) for bits in near}
    loaded = (pair, bias, proj_weight, gate_weight, out_weight, chains[None, :], token_mask[None, :])
    joined = jax.ShapeDtypeStruct((2, width, 4 * hidden + width), proj_weight.dtype)
    own, bias, weights, out_weight, chains_t, mask_t, *partial = call(
        functools.partial(prep_kernel, masks, halves, early),
        [far, *sent.values()] + [pltpu.with_memory_space_constraint(each, pltpu.HBM) for each in loaded],
        like(pair, bias) + [joined] + like(out_weight) + floats((tokens, width), (tokens, width)) + half,
        [pltpu.VMEM((1, tokens), jnp.int32), pltpu.VMEM((1, tokens), jnp.int32), pltpu.SemaphoreType.DMA((7,))],
        "prep",
        flops // ranks,
        spaces=[pltpu.VMEM] * len(early) + [pltpu.HBM] * 7,
    )
    two = jnp.stack([pair, far])
    parts = [far[None]]
    for bits in range(1, top):
        if bits in sent:
            parts += [sent[bits][None], exchange(far, bits)[None]]
        else:
            parts.append(exchange(two, bits))
    mine = jnp.concatenate(parts + [own[None]], 0)
    other = lax.ppermute(mine, "col", [(0, 1), (1, 0)])
    edge_inputs = (chains_t, mask_t, bias, weights)
    partial = call(
        functools.partial(mine_kernel, masks, halves, early),
        (mine, *edge_inputs, *partial),
        half,
        [],
        "mine",
        flops,
        {n + 5: n for n in range(4)},
    )
    groups = cols // 8 + 1
    extra = [(groups * tokens * 8, hidden), (tokens * 8, hidden), ((groups - 1) * tokens * 8, hidden)]
    return call(
        functools.partial(crop_kernel, masks, halves),
        (other, *edge_inputs, out_weight, *partial),
        floats(pair.shape) + half,
        [pltpu.VMEM(each.shape, jnp.float32) for each in floats(*extra)],
        "crop",
        4 * flops,
        {n + 6: n + 1 for n in range(4)},
    )[0]


def shards(pair, token_mask, *rest):
    tokens = token_mask.shape[0]
    ranks = lax.axis_size("row")
    small = tokens * tokens * pair.shape[2] <= 1 << 18 and ranks & (ranks - 1) == 0 and pair.shape[1] % 8 == 0
    plan = whole_crop_plan if small and lax.axis_size("col") == 2 else sharded_plan
    return plan(pair, token_mask, *rest)


def solution(mesh):
    placed = (P(("group", "row"), "col", None), P("group"), P("group"), P(), P(), P(), P())
    return jax.shard_map(
        shards,
        mesh=mesh,
        in_specs=placed,
        out_specs=P(("group", "row"), "col", None),
        check_vma=False,
    )
```

```python
import functools
import jax
import jax.numpy as jnp
from jax import lax
from jax.experimental import pallas as pl
from jax.experimental.pallas import tpu as pltpu
from jax.sharding import PartitionSpec as P


def layer_norm(values):
    mean = jnp.mean(values, -1, keepdims=True)
    centred = values - mean
    var = jnp.mean(centred * centred, -1, keepdims=True)
    return centred * lax.rsqrt(var + 1e-05)


def flat_dot(values, weight):
    shape = values.shape
    result = jnp.dot(values.reshape(-1, shape[-1]), weight, preferred_element_type=jnp.float32)
    return result.reshape(shape[:-1] + (weight.shape[1],))


def project(state, pmask, p_weight):
    normed = layer_norm(state).astype(jnp.bfloat16)
    proj = flat_dot(normed, p_weight)
    hidden = p_weight.shape[1] // 4
    gate_a = proj[..., :hidden]
    value_a = proj[..., hidden : 2 * hidden]
    gate_b = proj[..., 2 * hidden : 3 * hidden]
    value_b = proj[..., 3 * hidden :]
    left = (jax.nn.sigmoid(gate_a) * value_a * pmask[..., None]).astype(jnp.bfloat16)
    right = (jax.nn.sigmoid(gate_b) * value_b * pmask[..., None]).astype(jnp.bfloat16)
    return (normed, left, right)


def finish(state, normed, tri, g_weight, o_weight):
    tnorm = layer_norm(tri).astype(jnp.bfloat16)
    gate = jax.nn.sigmoid(flat_dot(normed, g_weight))
    return state + gate * flat_dot(tnorm, o_weight)


def sharded_plan(pair, token_mask, chains, chain_bias, proj_weight, gate_weight, out_weight):
    rows, cols, width = pair.shape
    row_start = lax.axis_index("row") * rows
    col_start = lax.axis_index("col") * cols
    chain_rows = lax.dynamic_slice_in_dim(chains, row_start, rows)
    chain_cols = lax.dynamic_slice_in_dim(chains, col_start, cols)
    mask_rows = lax.dynamic_slice_in_dim(token_mask, row_start, rows).astype(jnp.float32)
    mask_cols = lax.dynamic_slice_in_dim(token_mask, col_start, cols).astype(jnp.float32)
    same = (chain_rows[:, None] == chain_cols[None, :]).astype(jnp.float32)
    state = pair + same[..., None] * chain_bias
    pmask = mask_rows[:, None] * mask_cols[None, :]
    normed, left, right = project(state, pmask, proj_weight[0])
    left_rows, right_rows = (
        lax.all_gather(left, "col", axis=1, tiled=True),
        lax.all_gather(right, "col", axis=1, tiled=True),
    )
    every = jnp.einsum(
        "ikh,jkh->ijh",
        left_rows,
        lax.all_gather(right_rows, "row", axis=0, tiled=True),
        preferred_element_type=jnp.float32,
    )
    tri = lax.dynamic_slice_in_dim(every, col_start, cols, 1)
    state = finish(state, normed, tri, gate_weight[0], out_weight[0])
    normed, left, right = project(state, pmask, proj_weight[1])
    left_rows = lax.all_gather(left, "col", axis=1, tiled=True)
    left_cols = lax.all_to_all(left_rows, "row", split_axis=1, concat_axis=0, tiled=True)
    tri = jnp.einsum(
        "kih,kjh->ijh",
        left_cols,
        lax.all_gather(right, "row", axis=0, tiled=True),
        preferred_element_type=jnp.float32,
    )
    return finish(state, normed, tri, gate_weight[1], out_weight[1])


def tile_norm(values):
    mean = jnp.mean(values, -1, keepdims=True)
    centred = values - mean
    var = jnp.mean(centred * centred, -1, keepdims=True)
    return centred * lax.rsqrt(var + 1e-05)


def gate_of(values):
    return 0.5 * jnp.tanh(0.5 * values) + 0.5


def dot(values, weight):
    return jnp.dot(values, weight, preferred_element_type=jnp.float32)


def rounded(values):
    return values.astype(jnp.bfloat16).astype(jnp.float32)


def table(row, out):
    tokens, width = out.shape
    at = lax.broadcasted_iota(jnp.int32, (tokens, tokens), 0)
    lane = lax.broadcasted_iota(jnp.int32, (tokens, tokens), 1)
    spread = jnp.where(at == lane, jnp.broadcast_to(row[...].astype(jnp.float32), (tokens, tokens)), 0.0)
    out[...] = jnp.broadcast_to(jnp.sum(spread, -1, keepdims=True), (tokens, width))


def edges(masks, items, chains, mask, bias, weights, start, gates, left, right):
    rows, cols, width = items[0][2].shape
    tokens = chains.shape[0]
    me = lax.axis_index("row")
    col = lax.axis_index("col")
    bias_v = bias[...]
    hidden = left.shape[-1]
    firsts = [pl.multiple_of(each * cols, cols) for each in (col, 1 - col)]
    chain_cols = [chains[pl.ds(first, cols), :] for first in firsts]
    mask_cols = [mask[pl.ds(first, cols), :] for first in firsts]
    states, pmasks = [], []
    for slot, half, block in items:
        for t in range(rows):
            token = (me ^ masks[slot]) * rows + t
            same = chain_cols[half] == chains[pl.ds(token, 1), :]
            states.append(block[t] + jnp.where(same, bias_v, 0.0))
            pmasks.append(mask_cols[half] * mask[pl.ds(token, 1), :])
    state = jnp.concatenate(states, 0)
    pmask = jnp.concatenate(pmasks, 0)
    proj = dot(tile_norm(state).astype(jnp.bfloat16), weights[0])
    lft = rounded(gate_of(proj[:, :hidden]) * proj[:, hidden : 2 * hidden] * pmask)
    rgt = rounded(gate_of(proj[:, 2 * hidden : 3 * hidden]) * proj[:, 3 * hidden : 4 * hidden] * pmask)
    size = rows * cols
    for n, (slot, half, _) in enumerate(items):
        span, part = pl.ds(slot * size, size), slice(n * size, (n + 1) * size)
        start[half, span, :] = state[part]
        gates[half, span, :] = proj[part, 4 * hidden :]
        for t in range(rows):
            token = (me ^ masks[slot]) * rows + t
            at = n * size + t * cols
            left[half, slot * rows + t] = lft[at : at + cols]
            right[half, pl.ds(token, cols, tokens), :] = rgt[at : at + cols]


def keep_kernel(source, target, sem):
    load = pltpu.make_async_copy(source, target, sem)
    load.start()
    load.wait()


def prep_kernel(masks, halves, early, *refs):
    blocks, refs = refs[: len(early)], refs[len(early) :]
    sources, rest = refs[:7], refs[7:]
    pair, bias, weights, out_w, chains, mask, start, gates, left, right, chains_v, mask_v, sems = rest
    split = sources[2].shape[-1]
    proj_w, gate_w = weights.at[:, :, pl.ds(0, split)], weights.at[:, :, pl.ds(split, weights.shape[-1] - split)]
    loads = []
    for n, (source, target) in enumerate(zip(sources, (pair, bias, proj_w, gate_w, out_w, chains_v, mask_v))):
        loads.append(pltpu.make_async_copy(source, target, sems.at[n]))
    for load in loads:
        load.start()
    for load in loads:
        load.wait()
    table(chains_v, chains)
    table(mask_v, mask)
    items = [(len(masks) - 1, halves[-1], pair[...])] + [(slot, halves[slot], block[...]) for slot, block in zip(early, blocks)]
    edges(masks, items, chains, mask, bias, weights, start, gates, left, right)


def mine_kernel(masks, halves, early, mine, chains, mask, bias, weights, s_in, g_in, l_in, r_in, *outs):
    items = [(slot, halves[slot], mine[slot]) for slot in range(len(masks) - 1) if slot not in early]
    edges(masks, items, chains, mask, bias, weights, *outs)


def crop_kernel(
    masks,
    halves,
    other,
    chains,
    mask,
    bias,
    weights,
    out_w,
    start_in,
    gates_in,
    left_in,
    right_in,
    updated,
    start,
    gates,
    left,
    right,
    tris,
    left1,
    right1,
):
    ranks, rows, cols, width = other.shape
    tokens = ranks * rows
    me = lax.axis_index("row")
    col = lax.axis_index("col")
    hidden = left.shape[-1]
    items = [(slot, 1 - halves[slot], other[slot]) for slot in range(ranks)]
    edges(masks, items, chains, mask, bias, weights, start, gates, left, right)

    low = me * rows // 8 * 8
    groups = [col * cols + 8 * n for n in range(cols // 8)] + [low]
    groups = [pl.multiple_of(g, 8) for g in groups]
    count = len(groups)
    block = 8

    def tri_block(step, carry):
        k0 = step * block
        acc = [[None] * count for _ in range(block)]
        for half in range(2):
            for l in range(cols):
                cells = [right[half, pl.ds(pl.multiple_of(l * tokens + g, 8), 8), :] for g in groups]
                for k in range(block):
                    row = left[half, k0 + k, pl.ds(l, 1), :]
                    for n in range(count):
                        term = row * cells[n]
                        acc[k][n] = term if half + l == 0 else acc[k][n] + term
        for n in range(count):
            for k in range(block):
                tris[pl.ds(pl.multiple_of((n * tokens + k0 + k) * 8, 8), 8), :] = acc[k][n]
        return carry

    lax.fori_loop(0, tokens // block, tri_block, 0)

    low_half = jnp.where(low // cols == col, 0, 1)
    low_off = lax.rem(low, cols)
    mask_left = mask[pl.ds(pl.multiple_of(low, 8), 8), :]
    mask_right = mask[pl.ds(pl.multiple_of(col * cols, cols), cols), :]

    def gather(values, n, k):
        if n < count - 1:
            return values[0, pl.ds(k * cols + 8 * n, 8), :]
        return values[low_half, pl.ds(pl.multiple_of(k * cols + low_off, 8), 8), :]

    row_masks = []
    for slot in range(ranks):
        for t in range(rows):
            row_masks.append(mask[pl.ds((me ^ masks[slot]) * rows + t, 1), :])

    cells = [(n, k) for n in range(count) for k in range(tokens)]
    tnorm = tile_norm(tris[...]).astype(jnp.bfloat16)
    gate = gate_of(jnp.concatenate([gather(gates, n, k) for n, k in cells], 0))
    state = jnp.concatenate([gather(start, n, k) for n, k in cells], 0)
    state = state + gate * dot(tnorm, out_w[0])
    normed = tile_norm(state).astype(jnp.bfloat16)
    edge_rows = (count - 1) * tokens * 8
    proj_r = dot(normed[:edge_rows], weights[1, :, 2 * hidden : 4 * hidden])
    proj_l = dot(normed[edge_rows:], weights[1, :, : 2 * hidden])
    ends = [(n + 1) * tokens * 8 for n in range(count - 1)]
    own = [slice(end - rows * 8, end) for end in ends]
    own_state = jnp.concatenate([state[part] for part in own], 0)
    own_logit = dot(jnp.concatenate([normed[part] for part in own], 0), weights[1, :, 4 * hidden :])
    pm = jnp.concatenate([mask_left * m for m in row_masks], 0)
    left1[...] = rounded(gate_of(proj_l[:, :hidden]) * proj_l[:, hidden:] * pm)
    pm = jnp.concatenate([mask_right[8 * n : 8 * n + 8] * m for n in range(count - 1) for m in row_masks], 0)
    right1[...] = rounded(gate_of(proj_r[:, :hidden]) * proj_r[:, hidden:] * pm)

    shift = lax.rem(me * rows, 8)
    acc = [[None] * rows for _ in range(count - 1)]
    for k in range(tokens):
        for n in range(count - 1):
            cell = right1[pl.ds((n * tokens + k) * 8, 8), :]
            for t in range(rows):
                term = left1[pl.ds(k * 8 + shift + t, 1), :] * cell
                acc[n][t] = term if k == 0 else acc[n][t] + term
    tri = jnp.concatenate([acc[n][t] for n in range(count - 1) for t in range(rows)], 0)
    tnorm = tile_norm(tri).astype(jnp.bfloat16)
    out = own_state + gate_of(own_logit) * dot(tnorm, out_w[1])
    for n in range(count - 1):
        for t in range(rows):
            at = (n * rows + t) * 8
            updated[t, pl.ds(8 * n, 8), :] = out[at : at + 8]


def exchange(block, bits):
    ranks = lax.axis_size("row")
    hops = [(2 * i + c, 2 * (i ^ bits) + 1 - c) for i in range(ranks) for c in range(2)]
    return lax.ppermute(block, ("row", "col"), hops)


def call(body, inputs, outputs, scratch, name, flops, aliases={}, spaces=None):
    return pl.pallas_call(
        body,
        out_shape=outputs,
        in_specs=[pl.BlockSpec(memory_space=each) for each in spaces or [pltpu.VMEM] * len(inputs)],
        out_specs=[pl.BlockSpec(memory_space=pltpu.VMEM)] * len(outputs),
        scratch_shapes=scratch,
        compiler_params=pltpu.CompilerParams(vmem_limit_bytes=32 << 20),
        input_output_aliases=aliases,
        cost_estimate=pl.CostEstimate(flops=flops, bytes_accessed=1 << 21, transcendentals=0),
        name=name,
    )(*inputs)


def floats(*shapes):
    return [jax.ShapeDtypeStruct(shape, jnp.float32) for shape in shapes]


def like(*arrays):
    return [jax.ShapeDtypeStruct(array.shape, array.dtype) for array in arrays]


def whole_crop_plan(pair, token_mask, chains, chain_bias, proj_weight, gate_weight, out_weight):
    rows, cols, width = pair.shape
    ranks = lax.axis_size("row")
    tokens = token_mask.shape[0]
    hidden = proj_weight.shape[2] // 4
    bias = chain_bias[None, :]
    half = [(2, tokens * cols, width), (2, tokens * cols, width), (2, tokens, cols, hidden), (2, tokens * cols, hidden)]
    half = floats(*half)
    flops = 2 * tokens * cols * width * 5 * hidden
    top = ranks // 2
    masks, halves = [top], [1]
    for bits in range(1, top):
        masks += [bits, bits ^ top]
        halves += [1, 0]
    masks, halves = masks + [0], halves + [0]
    near = [bits for bits in range(1, top) if bits & (bits - 1) == 0]
    early = [masks.index(bits) for bits in [top] + near]
    far = exchange(pair, top)
    sent = {bits: exchange(pair, bits) for bits in near}
    kept = call(
        keep_kernel,
        [pltpu.with_memory_space_constraint(pair, pltpu.HBM)],
        like(pair),
        [pltpu.SemaphoreType.DMA],
        "keep",
        flops // ranks,
        spaces=[pltpu.HBM],
    )[0]
    loaded = (pair, bias, proj_weight, gate_weight, out_weight, chains[None, :], token_mask[None, :])
    joined = jax.ShapeDtypeStruct((2, width, 4 * hidden + width), proj_weight.dtype)
    own, bias, weights, out_weight, chains_t, mask_t, *partial = call(
        functools.partial(prep_kernel, masks, halves, early),
        [far, *sent.values()] + [pltpu.with_memory_space_constraint(each, pltpu.HBM) for each in loaded],
        like(pair, bias) + [joined] + like(out_weight) + floats((tokens, width), (tokens, width)) + half,
        [pltpu.VMEM((1, tokens), jnp.int32), pltpu.VMEM((1, tokens), jnp.int32), pltpu.SemaphoreType.DMA((7,))],
        "prep",
        flops // ranks,
        spaces=[pltpu.VMEM] * len(early) + [pltpu.HBM] * 7,
    )
    two = jnp.stack([kept, far])
    parts = [far[None]]
    for bits in range(1, top):
        if bits in sent:
            parts += [sent[bits][None], exchange(far, bits)[None]]
        else:
            parts.append(exchange(two, bits))
    mine = jnp.concatenate(parts + [own[None]], 0)
    other = lax.ppermute(mine, "col", [(0, 1), (1, 0)])
    edge_inputs = (chains_t, mask_t, bias, weights)
    partial = call(
        functools.partial(mine_kernel, masks, halves, early),
        (mine, *edge_inputs, *partial),
        half,
        [],
        "mine",
        flops,
        {n + 5: n for n in range(4)},
    )
    groups = cols // 8 + 1
    extra = [(groups * tokens * 8, hidden), (tokens * 8, hidden), ((groups - 1) * tokens * 8, hidden)]
    return call(
        functools.partial(crop_kernel, masks, halves),
        (other, *edge_inputs, out_weight, *partial),
        floats(pair.shape) + half,
        [pltpu.VMEM(each.shape, jnp.float32) for each in floats(*extra)],
        "crop",
        4 * flops,
        {n + 6: n + 1 for n in range(4)},
    )[0]


def shards(pair, token_mask, *rest):
    tokens = token_mask.shape[0]
    ranks = lax.axis_size("row")
    small = tokens * tokens * pair.shape[2] <= 1 << 18 and ranks & (ranks - 1) == 0 and pair.shape[1] % 8 == 0
    plan = whole_crop_plan if small and lax.axis_size("col") == 2 else sharded_plan
    return plan(pair, token_mask, *rest)


def solution(mesh):
    placed = (P(("group", "row"), "col", None), P("group"), P("group"), P(), P(), P(), P())
    return jax.shard_map(
        shards,
        mesh=mesh,
        in_specs=placed,
        out_specs=P(("group", "row"), "col", None),
        check_vma=False,
    )
```

```python
import functools
import jax
import jax.numpy as jnp
from jax import lax
from jax.experimental import pallas as pl
from jax.experimental.pallas import tpu as pltpu
from jax.sharding import PartitionSpec as P


def layer_norm(values):
    mean = jnp.mean(values, -1, keepdims=True)
    centred = values - mean
    var = jnp.mean(centred * centred, -1, keepdims=True)
    return centred * lax.rsqrt(var + 1e-05)


def flat_dot(values, weight):
    shape = values.shape
    result = jnp.dot(values.reshape(-1, shape[-1]), weight, preferred_element_type=jnp.float32)
    return result.reshape(shape[:-1] + (weight.shape[1],))


def project(state, pmask, p_weight):
    normed = layer_norm(state).astype(jnp.bfloat16)
    proj = flat_dot(normed, p_weight)
    hidden = p_weight.shape[1] // 4
    gate_a = proj[..., :hidden]
    value_a = proj[..., hidden : 2 * hidden]
    gate_b = proj[..., 2 * hidden : 3 * hidden]
    value_b = proj[..., 3 * hidden :]
    left = (jax.nn.sigmoid(gate_a) * value_a * pmask[..., None]).astype(jnp.bfloat16)
    right = (jax.nn.sigmoid(gate_b) * value_b * pmask[..., None]).astype(jnp.bfloat16)
    return (normed, left, right)


def finish(state, normed, tri, g_weight, o_weight):
    tnorm = layer_norm(tri).astype(jnp.bfloat16)
    gate = jax.nn.sigmoid(flat_dot(normed, g_weight))
    return state + gate * flat_dot(tnorm, o_weight)


def sharded_plan(pair, token_mask, chains, chain_bias, proj_weight, gate_weight, out_weight):
    rows, cols, width = pair.shape
    row_start = lax.axis_index("row") * rows
    col_start = lax.axis_index("col") * cols
    chain_rows = lax.dynamic_slice_in_dim(chains, row_start, rows)
    chain_cols = lax.dynamic_slice_in_dim(chains, col_start, cols)
    mask_rows = lax.dynamic_slice_in_dim(token_mask, row_start, rows).astype(jnp.float32)
    mask_cols = lax.dynamic_slice_in_dim(token_mask, col_start, cols).astype(jnp.float32)
    same = (chain_rows[:, None] == chain_cols[None, :]).astype(jnp.float32)
    state = pair + same[..., None] * chain_bias
    pmask = mask_rows[:, None] * mask_cols[None, :]
    normed, left, right = project(state, pmask, proj_weight[0])
    left_rows, right_rows = (
        lax.all_gather(left, "col", axis=1, tiled=True),
        lax.all_gather(right, "col", axis=1, tiled=True),
    )
    every = jnp.einsum(
        "ikh,jkh->ijh",
        left_rows,
        lax.all_gather(right_rows, "row", axis=0, tiled=True),
        preferred_element_type=jnp.float32,
    )
    tri = lax.dynamic_slice_in_dim(every, col_start, cols, 1)
    state = finish(state, normed, tri, gate_weight[0], out_weight[0])
    normed, left, right = project(state, pmask, proj_weight[1])
    left_rows = lax.all_gather(left, "col", axis=1, tiled=True)
    left_cols = lax.all_to_all(left_rows, "row", split_axis=1, concat_axis=0, tiled=True)
    tri = jnp.einsum(
        "kih,kjh->ijh",
        left_cols,
        lax.all_gather(right, "row", axis=0, tiled=True),
        preferred_element_type=jnp.float32,
    )
    return finish(state, normed, tri, gate_weight[1], out_weight[1])


def tile_norm(values):
    mean = jnp.mean(values, -1, keepdims=True)
    centred = values - mean
    var = jnp.mean(centred * centred, -1, keepdims=True)
    return centred * lax.rsqrt(var + 1e-05)


def gate_of(values):
    return 0.5 * jnp.tanh(0.5 * values) + 0.5


def dot(values, weight):
    return jnp.dot(values, weight, preferred_element_type=jnp.float32)


def rounded(values):
    return values.astype(jnp.bfloat16).astype(jnp.float32)


def table(row, out):
    tokens, width = out.shape
    at = lax.broadcasted_iota(jnp.int32, (tokens, tokens), 0)
    lane = lax.broadcasted_iota(jnp.int32, (tokens, tokens), 1)
    spread = jnp.where(at == lane, jnp.broadcast_to(row[...].astype(jnp.float32), (tokens, tokens)), 0.0)
    out[...] = jnp.broadcast_to(jnp.sum(spread, -1, keepdims=True), (tokens, width))


def edges(masks, items, chains, mask, bias, weights, start, gates, left, right):
    rows, cols, width = items[0][2].shape
    tokens = chains.shape[0]
    me = lax.axis_index("row")
    col = lax.axis_index("col")
    bias_v = bias[...]
    hidden = left.shape[-1]
    firsts = [pl.multiple_of(each * cols, cols) for each in (col, 1 - col)]
    chain_cols = [chains[pl.ds(first, cols), :] for first in firsts]
    mask_cols = [mask[pl.ds(first, cols), :] for first in firsts]
    states, pmasks = [], []
    for slot, half, block in items:
        for t in range(rows):
            token = (me ^ masks[slot]) * rows + t
            same = chain_cols[half] == chains[pl.ds(token, 1), :]
            states.append(block[t] + jnp.where(same, bias_v, 0.0))
            pmasks.append(mask_cols[half] * mask[pl.ds(token, 1), :])
    state = jnp.concatenate(states, 0)
    pmask = jnp.concatenate(pmasks, 0)
    proj = dot(tile_norm(state).astype(jnp.bfloat16), weights[0])
    lft = rounded(gate_of(proj[:, :hidden]) * proj[:, hidden : 2 * hidden] * pmask)
    rgt = rounded(gate_of(proj[:, 2 * hidden : 3 * hidden]) * proj[:, 3 * hidden : 4 * hidden] * pmask)
    size = rows * cols
    for n, (slot, half, _) in enumerate(items):
        span, part = pl.ds(slot * size, size), slice(n * size, (n + 1) * size)
        start[half, span, :] = state[part]
        gates[half, span, :] = proj[part, 4 * hidden :]
        for t in range(rows):
            token = (me ^ masks[slot]) * rows + t
            at = n * size + t * cols
            left[half, slot * rows + t] = lft[at : at + cols]
            right[half, pl.ds(token, cols, tokens), :] = rgt[at : at + cols]


def keep_kernel(source, target, sem):
    load = pltpu.make_async_copy(source, target, sem)
    load.start()
    load.wait()


def prep_kernel(masks, halves, early, *refs):
    blocks, refs = refs[: len(early)], refs[len(early) :]
    sources, rest = refs[:7], refs[7:]
    pair, bias, weights, out_w, chains, mask, start, gates, left, right, chains_v, mask_v, sems = rest
    split = sources[2].shape[-1]
    proj_w, gate_w = weights.at[:, :, pl.ds(0, split)], weights.at[:, :, pl.ds(split, weights.shape[-1] - split)]
    loads = []
    for n, (source, target) in enumerate(zip(sources, (pair, bias, proj_w, gate_w, out_w, chains_v, mask_v))):
        loads.append(pltpu.make_async_copy(source, target, sems.at[n]))
    for load in loads:
        load.start()
    for load in loads:
        load.wait()
    table(chains_v, chains)
    table(mask_v, mask)
    items = [(len(masks) - 1, halves[-1], pair[...])] + [(slot, halves[slot], block[...]) for slot, block in zip(early, blocks)]
    edges(masks, items, chains, mask, bias, weights, start, gates, left, right)


def mine_kernel(masks, halves, early, mine, chains, mask, bias, weights, s_in, g_in, l_in, r_in, *outs):
    items = [(slot, halves[slot], mine[slot]) for slot in range(len(masks) - 1) if slot not in early]
    edges(masks, items, chains, mask, bias, weights, *outs)


def crop_kernel(
    masks,
    halves,
    other,
    chains,
    mask,
    bias,
    weights,
    out_w,
    start_in,
    gates_in,
    left_in,
    right_in,
    updated,
    start,
    gates,
    left,
    right,
    tris,
    left1,
    right1,
):
    ranks, rows, cols, width = other.shape
    tokens = ranks * rows
    me = lax.axis_index("row")
    col = lax.axis_index("col")
    hidden = left.shape[-1]
    items = [(slot, 1 - halves[slot], other[slot]) for slot in range(ranks)]
    edges(masks, items, chains, mask, bias, weights, start, gates, left, right)

    low = me * rows // 8 * 8
    groups = [col * cols + 8 * n for n in range(cols // 8)] + [low]
    groups = [pl.multiple_of(g, 8) for g in groups]
    count = len(groups)
    block = 8

    def tri_block(step, carry):
        k0 = step * block
        acc = [[None] * count for _ in range(block)]
        for half in range(2):
            for l in range(cols):
                cells = [right[half, pl.ds(pl.multiple_of(l * tokens + g, 8), 8), :] for g in groups]
                for k in range(block):
                    row = left[half, k0 + k, pl.ds(l, 1), :]
                    for n in range(count):
                        term = row * cells[n]
                        acc[k][n] = term if half + l == 0 else acc[k][n] + term
        for n in range(count):
            for k in range(block):
                tris[pl.ds(pl.multiple_of((n * tokens + k0 + k) * 8, 8), 8), :] = acc[k][n]
        return carry

    lax.fori_loop(0, tokens // block, tri_block, 0)

    low_half = jnp.where(low // cols == col, 0, 1)
    low_off = lax.rem(low, cols)
    mask_left = mask[pl.ds(pl.multiple_of(low, 8), 8), :]
    mask_right = mask[pl.ds(pl.multiple_of(col * cols, cols), cols), :]

    def gather(values, n, k):
        if n < count - 1:
            return values[0, pl.ds(k * cols + 8 * n, 8), :]
        return values[low_half, pl.ds(pl.multiple_of(k * cols + low_off, 8), 8), :]

    row_masks = []
    for slot in range(ranks):
        for t in range(rows):
            row_masks.append(mask[pl.ds((me ^ masks[slot]) * rows + t, 1), :])

    cells = [(n, k) for n in range(count) for k in range(tokens)]
    tnorm = tile_norm(tris[...]).astype(jnp.bfloat16)
    gate = gate_of(jnp.concatenate([gather(gates, n, k) for n, k in cells], 0))
    state = jnp.concatenate([gather(start, n, k) for n, k in cells], 0)
    state = state + gate * dot(tnorm, out_w[0])
    normed = tile_norm(state).astype(jnp.bfloat16)
    edge_rows = (count - 1) * tokens * 8
    proj_r = dot(normed[:edge_rows], weights[1, :, 2 * hidden : 4 * hidden])
    proj_l = dot(normed[edge_rows:], weights[1, :, : 2 * hidden])
    ends = [(n + 1) * tokens * 8 for n in range(count - 1)]
    own = [slice(end - rows * 8, end) for end in ends]
    own_state = jnp.concatenate([state[part] for part in own], 0)
    own_logit = dot(jnp.concatenate([normed[part] for part in own], 0), weights[1, :, 4 * hidden :])
    pm = jnp.concatenate([mask_left * m for m in row_masks], 0)
    left1[...] = rounded(gate_of(proj_l[:, :hidden]) * proj_l[:, hidden:] * pm)
    pm = jnp.concatenate([mask_right[8 * n : 8 * n + 8] * m for n in range(count - 1) for m in row_masks], 0)
    right1[...] = rounded(gate_of(proj_r[:, :hidden]) * proj_r[:, hidden:] * pm)

    shift = lax.rem(me * rows, 8)
    acc = [[None] * rows for _ in range(count - 1)]
    for k in range(tokens):
        for n in range(count - 1):
            cell = right1[pl.ds((n * tokens + k) * 8, 8), :]
            for t in range(rows):
                term = left1[pl.ds(k * 8 + shift + t, 1), :] * cell
                acc[n][t] = term if k == 0 else acc[n][t] + term
    tri = jnp.concatenate([acc[n][t] for n in range(count - 1) for t in range(rows)], 0)
    tnorm = tile_norm(tri).astype(jnp.bfloat16)
    out = own_state + gate_of(own_logit) * dot(tnorm, out_w[1])
    for n in range(count - 1):
        for t in range(rows):
            at = (n * rows + t) * 8
            updated[t, pl.ds(8 * n, 8), :] = out[at : at + 8]


def exchange(block, bits):
    ranks = lax.axis_size("row")
    hops = [(2 * i + c, 2 * (i ^ bits) + 1 - c) for i in range(ranks) for c in range(2)]
    return lax.ppermute(block, ("row", "col"), hops)


def call(body, inputs, outputs, scratch, name, flops, aliases={}, spaces=None):
    return pl.pallas_call(
        body,
        out_shape=outputs,
        in_specs=[pl.BlockSpec(memory_space=each) for each in spaces or [pltpu.VMEM] * len(inputs)],
        out_specs=[pl.BlockSpec(memory_space=pltpu.VMEM)] * len(outputs),
        scratch_shapes=scratch,
        compiler_params=pltpu.CompilerParams(vmem_limit_bytes=32 << 20),
        input_output_aliases=aliases,
        cost_estimate=pl.CostEstimate(flops=flops, bytes_accessed=1 << 21, transcendentals=0),
        name=name,
    )(*inputs)


def floats(*shapes):
    return [jax.ShapeDtypeStruct(shape, jnp.float32) for shape in shapes]


def like(*arrays):
    return [jax.ShapeDtypeStruct(array.shape, array.dtype) for array in arrays]


def whole_crop_plan(pair, token_mask, chains, chain_bias, proj_weight, gate_weight, out_weight):
    rows, cols, width = pair.shape
    ranks = lax.axis_size("row")
    tokens = token_mask.shape[0]
    hidden = proj_weight.shape[2] // 4
    bias = chain_bias[None, :]
    half = [(2, tokens * cols, width), (2, tokens * cols, width), (2, tokens, cols, hidden), (2, tokens * cols, hidden)]
    half = floats(*half)
    flops = 2 * tokens * cols * width * 5 * hidden
    top = ranks // 2
    masks, halves = [top], [1]
    for bits in range(1, top):
        masks += [bits, bits ^ top]
        halves += [1, 0]
    masks, halves = masks + [0], halves + [0]
    near = [bits for bits in range(1, top) if bits & (bits - 1) == 0]
    early = [masks.index(bits) for bits in [top] + near]
    far = exchange(pair, top)
    sent = {bits: exchange(pair, bits) for bits in near}
    kept = call(
        keep_kernel,
        [pltpu.with_memory_space_constraint(pair, pltpu.HBM)],
        like(pair),
        [pltpu.SemaphoreType.DMA],
        "keep",
        10 * flops,
        spaces=[pltpu.HBM],
    )[0]
    loaded = (pair, bias, proj_weight, gate_weight, out_weight, chains[None, :], token_mask[None, :])
    joined = jax.ShapeDtypeStruct((2, width, 4 * hidden + width), proj_weight.dtype)
    own, bias, weights, out_weight, chains_t, mask_t, *partial = call(
        functools.partial(prep_kernel, masks, halves, early),
        [far, *sent.values()] + [pltpu.with_memory_space_constraint(each, pltpu.HBM) for each in loaded],
        like(pair, bias) + [joined] + like(out_weight) + floats((tokens, width), (tokens, width)) + half,
        [pltpu.VMEM((1, tokens), jnp.int32), pltpu.VMEM((1, tokens), jnp.int32), pltpu.SemaphoreType.DMA((7,))],
        "prep",
        flops // ranks,
        spaces=[pltpu.VMEM] * len(early) + [pltpu.HBM] * 7,
    )
    two = jnp.stack([kept, far])
    parts = [far[None]]
    for bits in range(1, top):
        if bits in sent:
            parts += [sent[bits][None], exchange(far, bits)[None]]
        else:
            parts.append(exchange(two, bits))
    mine = jnp.concatenate(parts + [own[None]], 0)
    other = lax.ppermute(mine, "col", [(0, 1), (1, 0)])
    edge_inputs = (chains_t, mask_t, bias, weights)
    partial = call(
        functools.partial(mine_kernel, masks, halves, early),
        (mine, *edge_inputs, *partial),
        half,
        [],
        "mine",
        flops,
        {n + 5: n for n in range(4)},
    )
    groups = cols // 8 + 1
    extra = [(groups * tokens * 8, hidden), (tokens * 8, hidden), ((groups - 1) * tokens * 8, hidden)]
    return call(
        functools.partial(crop_kernel, masks, halves),
        (other, *edge_inputs, out_weight, *partial),
        floats(pair.shape) + half,
        [pltpu.VMEM(each.shape, jnp.float32) for each in floats(*extra)],
        "crop",
        4 * flops,
        {n + 6: n + 1 for n in range(4)},
    )[0]


def shards(pair, token_mask, *rest):
    tokens = token_mask.shape[0]
    ranks = lax.axis_size("row")
    small = tokens * tokens * pair.shape[2] <= 1 << 18 and ranks & (ranks - 1) == 0 and pair.shape[1] % 8 == 0
    plan = whole_crop_plan if small and lax.axis_size("col") == 2 else sharded_plan
    return plan(pair, token_mask, *rest)


def solution(mesh):
    placed = (P(("group", "row"), "col", None), P("group"), P("group"), P(), P(), P(), P())
    return jax.shard_map(
        shards,
        mesh=mesh,
        in_specs=placed,
        out_specs=P(("group", "row"), "col", None),
        check_vma=False,
    )
```

```python
import functools
import jax
import jax.numpy as jnp
from jax import lax
from jax.experimental import pallas as pl
from jax.experimental.pallas import tpu as pltpu
from jax.sharding import PartitionSpec as P


def layer_norm(values):
    mean = jnp.mean(values, -1, keepdims=True)
    centred = values - mean
    var = jnp.mean(centred * centred, -1, keepdims=True)
    return centred * lax.rsqrt(var + 1e-05)


def flat_dot(values, weight):
    shape = values.shape
    result = jnp.dot(values.reshape(-1, shape[-1]), weight, preferred_element_type=jnp.float32)
    return result.reshape(shape[:-1] + (weight.shape[1],))


def project(state, pmask, p_weight):
    normed = layer_norm(state).astype(jnp.bfloat16)
    proj = flat_dot(normed, p_weight)
    hidden = p_weight.shape[1] // 4
    gate_a = proj[..., :hidden]
    value_a = proj[..., hidden : 2 * hidden]
    gate_b = proj[..., 2 * hidden : 3 * hidden]
    value_b = proj[..., 3 * hidden :]
    left = (jax.nn.sigmoid(gate_a) * value_a * pmask[..., None]).astype(jnp.bfloat16)
    right = (jax.nn.sigmoid(gate_b) * value_b * pmask[..., None]).astype(jnp.bfloat16)
    return (normed, left, right)


def finish(state, normed, tri, g_weight, o_weight):
    tnorm = layer_norm(tri).astype(jnp.bfloat16)
    gate = jax.nn.sigmoid(flat_dot(normed, g_weight))
    return state + gate * flat_dot(tnorm, o_weight)


def sharded_plan(pair, token_mask, chains, chain_bias, proj_weight, gate_weight, out_weight):
    rows, cols, width = pair.shape
    row_start = lax.axis_index("row") * rows
    col_start = lax.axis_index("col") * cols
    chain_rows = lax.dynamic_slice_in_dim(chains, row_start, rows)
    chain_cols = lax.dynamic_slice_in_dim(chains, col_start, cols)
    mask_rows = lax.dynamic_slice_in_dim(token_mask, row_start, rows).astype(jnp.float32)
    mask_cols = lax.dynamic_slice_in_dim(token_mask, col_start, cols).astype(jnp.float32)
    same = (chain_rows[:, None] == chain_cols[None, :]).astype(jnp.float32)
    state = pair + same[..., None] * chain_bias
    pmask = mask_rows[:, None] * mask_cols[None, :]
    normed, left, right = project(state, pmask, proj_weight[0])
    left_rows, right_rows = (
        lax.all_gather(left, "col", axis=1, tiled=True),
        lax.all_gather(right, "col", axis=1, tiled=True),
    )
    every = jnp.einsum(
        "ikh,jkh->ijh",
        left_rows,
        lax.all_gather(right_rows, "row", axis=0, tiled=True),
        preferred_element_type=jnp.float32,
    )
    tri = lax.dynamic_slice_in_dim(every, col_start, cols, 1)
    state = finish(state, normed, tri, gate_weight[0], out_weight[0])
    normed, left, right = project(state, pmask, proj_weight[1])
    left_rows = lax.all_gather(left, "col", axis=1, tiled=True)
    left_cols = lax.all_to_all(left_rows, "row", split_axis=1, concat_axis=0, tiled=True)
    tri = jnp.einsum(
        "kih,kjh->ijh",
        left_cols,
        lax.all_gather(right, "row", axis=0, tiled=True),
        preferred_element_type=jnp.float32,
    )
    return finish(state, normed, tri, gate_weight[1], out_weight[1])


def tile_norm(values):
    mean = jnp.mean(values, -1, keepdims=True)
    centred = values - mean
    var = jnp.mean(centred * centred, -1, keepdims=True)
    return centred * lax.rsqrt(var + 1e-05)


def gate_of(values):
    return 0.5 * jnp.tanh(0.5 * values) + 0.5


def dot(values, weight):
    return jnp.dot(values, weight, preferred_element_type=jnp.float32)


def rounded(values):
    return values.astype(jnp.bfloat16).astype(jnp.float32)


def table(row, out):
    tokens, width = out.shape
    at = lax.broadcasted_iota(jnp.int32, (tokens, tokens), 0)
    lane = lax.broadcasted_iota(jnp.int32, (tokens, tokens), 1)
    spread = jnp.where(at == lane, jnp.broadcast_to(row[...].astype(jnp.float32), (tokens, tokens)), 0.0)
    out[...] = jnp.broadcast_to(jnp.sum(spread, -1, keepdims=True), (tokens, width))


def edges(masks, items, chains, mask, bias, weights, start, gates, left, right):
    rows, cols, width = items[0][2].shape
    tokens = chains.shape[0]
    me = lax.axis_index("row")
    col = lax.axis_index("col")
    bias_v = bias[...]
    hidden = left.shape[-1]
    firsts = [pl.multiple_of(each * cols, cols) for each in (col, 1 - col)]
    chain_cols = [chains[pl.ds(first, cols), :] for first in firsts]
    mask_cols = [mask[pl.ds(first, cols), :] for first in firsts]
    states, pmasks = [], []
    for slot, half, block in items:
        for t in range(rows):
            token = (me ^ masks[slot]) * rows + t
            same = chain_cols[half] == chains[pl.ds(token, 1), :]
            states.append(block[t] + jnp.where(same, bias_v, 0.0))
            pmasks.append(mask_cols[half] * mask[pl.ds(token, 1), :])
    state = jnp.concatenate(states, 0)
    pmask = jnp.concatenate(pmasks, 0)
    proj = dot(tile_norm(state).astype(jnp.bfloat16), weights[0])
    lft = rounded(gate_of(proj[:, :hidden]) * proj[:, hidden : 2 * hidden] * pmask)
    rgt = rounded(gate_of(proj[:, 2 * hidden : 3 * hidden]) * proj[:, 3 * hidden : 4 * hidden] * pmask)
    size = rows * cols
    for n, (slot, half, _) in enumerate(items):
        span, part = pl.ds(slot * size, size), slice(n * size, (n + 1) * size)
        start[half, span, :] = state[part]
        gates[half, span, :] = proj[part, 4 * hidden :]
        for t in range(rows):
            token = (me ^ masks[slot]) * rows + t
            at = n * size + t * cols
            left[half, slot * rows + t] = lft[at : at + cols]
            right[half, pl.ds(token, cols, tokens), :] = rgt[at : at + cols]


def keep_kernel(source, target, sem):
    load = pltpu.make_async_copy(source, target, sem)
    load.start()
    load.wait()


def prep_kernel(masks, halves, early, *refs):
    blocks, refs = refs[: len(early)], refs[len(early) :]
    sources, rest = refs[:7], refs[7:]
    pair, bias, weights, out_w, chains, mask, start, gates, left, right, chains_v, mask_v, sems = rest
    split = sources[2].shape[-1]
    proj_w, gate_w = weights.at[:, :, pl.ds(0, split)], weights.at[:, :, pl.ds(split, weights.shape[-1] - split)]
    loads = []
    for n, (source, target) in enumerate(zip(sources, (pair, bias, proj_w, gate_w, out_w, chains_v, mask_v))):
        loads.append(pltpu.make_async_copy(source, target, sems.at[n]))
    for load in loads:
        load.start()
    for load in loads:
        load.wait()
    table(chains_v, chains)
    table(mask_v, mask)
    items = [(len(masks) - 1, halves[-1], pair[...])] + [(slot, halves[slot], block[...]) for slot, block in zip(early, blocks)]
    edges(masks, items, chains, mask, bias, weights, start, gates, left, right)


def mine_kernel(masks, halves, early, mine, chains, mask, bias, weights, s_in, g_in, l_in, r_in, *outs):
    items = [(slot, halves[slot], mine[slot]) for slot in range(len(masks) - 1) if slot not in early]
    edges(masks, items, chains, mask, bias, weights, *outs)


def crop_kernel(
    masks,
    halves,
    other,
    chains,
    mask,
    bias,
    weights,
    out_w,
    start_in,
    gates_in,
    left_in,
    right_in,
    updated,
    start,
    gates,
    left,
    right,
    tris,
    left1,
    right1,
):
    ranks, rows, cols, width = other.shape
    tokens = ranks * rows
    me = lax.axis_index("row")
    col = lax.axis_index("col")
    hidden = left.shape[-1]
    items = [(slot, 1 - halves[slot], other[slot]) for slot in range(ranks)]
    edges(masks, items, chains, mask, bias, weights, start, gates, left, right)

    low = me * rows // 8 * 8
    groups = [col * cols + 8 * n for n in range(cols // 8)] + [low]
    groups = [pl.multiple_of(g, 8) for g in groups]
    count = len(groups)
    block = 8

    def tri_block(step, carry):
        k0 = step * block
        acc = [[None] * count for _ in range(block)]
        for half in range(2):
            for l in range(cols):
                cells = [right[half, pl.ds(pl.multiple_of(l * tokens + g, 8), 8), :] for g in groups]
                for k in range(block):
                    row = left[half, k0 + k, pl.ds(l, 1), :]
                    for n in range(count):
                        term = row * cells[n]
                        acc[k][n] = term if half + l == 0 else acc[k][n] + term
        for n in range(count):
            for k in range(block):
                tris[pl.ds(pl.multiple_of((n * tokens + k0 + k) * 8, 8), 8), :] = acc[k][n]
        return carry

    lax.fori_loop(0, tokens // block, tri_block, 0)

    low_half = jnp.where(low // cols == col, 0, 1)
    low_off = lax.rem(low, cols)
    mask_left = mask[pl.ds(pl.multiple_of(low, 8), 8), :]
    mask_right = mask[pl.ds(pl.multiple_of(col * cols, cols), cols), :]

    def gather(values, n, k):
        if n < count - 1:
            return values[0, pl.ds(k * cols + 8 * n, 8), :]
        return values[low_half, pl.ds(pl.multiple_of(k * cols + low_off, 8), 8), :]

    row_masks = []
    for slot in range(ranks):
        for t in range(rows):
            row_masks.append(mask[pl.ds((me ^ masks[slot]) * rows + t, 1), :])

    cells = [(n, k) for n in range(count) for k in range(tokens)]
    tnorm = tile_norm(tris[...]).astype(jnp.bfloat16)
    gate = gate_of(jnp.concatenate([gather(gates, n, k) for n, k in cells], 0))
    state = jnp.concatenate([gather(start, n, k) for n, k in cells], 0)
    state = state + gate * dot(tnorm, out_w[0])
    normed = tile_norm(state).astype(jnp.bfloat16)
    edge_rows = (count - 1) * tokens * 8
    proj_r = dot(normed[:edge_rows], weights[1, :, 2 * hidden : 4 * hidden])
    proj_l = dot(normed[edge_rows:], weights[1, :, : 2 * hidden])
    ends = [(n + 1) * tokens * 8 for n in range(count - 1)]
    own = [slice(end - rows * 8, end) for end in ends]
    own_state = jnp.concatenate([state[part] for part in own], 0)
    own_logit = dot(jnp.concatenate([normed[part] for part in own], 0), weights[1, :, 4 * hidden :])
    pm = jnp.concatenate([mask_left * m for m in row_masks], 0)
    left1[...] = rounded(gate_of(proj_l[:, :hidden]) * proj_l[:, hidden:] * pm)
    pm = jnp.concatenate([mask_right[8 * n : 8 * n + 8] * m for n in range(count - 1) for m in row_masks], 0)
    right1[...] = rounded(gate_of(proj_r[:, :hidden]) * proj_r[:, hidden:] * pm)

    shift = lax.rem(me * rows, 8)
    acc = [[None] * rows for _ in range(count - 1)]
    for k in range(tokens):
        for n in range(count - 1):
            cell = right1[pl.ds((n * tokens + k) * 8, 8), :]
            for t in range(rows):
                term = left1[pl.ds(k * 8 + shift + t, 1), :] * cell
                acc[n][t] = term if k == 0 else acc[n][t] + term
    tri = jnp.concatenate([acc[n][t] for n in range(count - 1) for t in range(rows)], 0)
    tnorm = tile_norm(tri).astype(jnp.bfloat16)
    out = own_state + gate_of(own_logit) * dot(tnorm, out_w[1])
    for n in range(count - 1):
        for t in range(rows):
            at = (n * rows + t) * 8
            updated[t, pl.ds(8 * n, 8), :] = out[at : at + 8]


def exchange(block, bits):
    ranks = lax.axis_size("row")
    hops = [(2 * i + c, 2 * (i ^ bits) + 1 - c) for i in range(ranks) for c in range(2)]
    return lax.ppermute(block, ("row", "col"), hops)


def call(body, inputs, outputs, scratch, name, flops, aliases={}, spaces=None):
    return pl.pallas_call(
        body,
        out_shape=outputs,
        in_specs=[pl.BlockSpec(memory_space=each) for each in spaces or [pltpu.VMEM] * len(inputs)],
        out_specs=[pl.BlockSpec(memory_space=pltpu.VMEM)] * len(outputs),
        scratch_shapes=scratch,
        compiler_params=pltpu.CompilerParams(vmem_limit_bytes=32 << 20),
        input_output_aliases=aliases,
        cost_estimate=pl.CostEstimate(flops=flops, bytes_accessed=1 << 21, transcendentals=0),
        name=name,
    )(*inputs)


def floats(*shapes):
    return [jax.ShapeDtypeStruct(shape, jnp.float32) for shape in shapes]


def like(*arrays):
    return [jax.ShapeDtypeStruct(array.shape, array.dtype) for array in arrays]


def whole_crop_plan(pair, token_mask, chains, chain_bias, proj_weight, gate_weight, out_weight):
    rows, cols, width = pair.shape
    ranks = lax.axis_size("row")
    tokens = token_mask.shape[0]
    hidden = proj_weight.shape[2] // 4
    bias = chain_bias[None, :]
    half = [(2, tokens * cols, width), (2, tokens * cols, width), (2, tokens, cols, hidden), (2, tokens * cols, hidden)]
    half = floats(*half)
    flops = 2 * tokens * cols * width * 5 * hidden
    top = ranks // 2
    masks, halves = [top], [1]
    for bits in range(1, top):
        masks += [bits, bits ^ top]
        halves += [1, 0]
    masks, halves = masks + [0], halves + [0]
    near = [top - 1]
    early = [masks.index(bits) for bits in [top] + near]
    far = exchange(pair, top)
    sent = {bits: exchange(pair, bits) for bits in near}
    kept = call(
        keep_kernel,
        [pltpu.with_memory_space_constraint(pair, pltpu.HBM)],
        like(pair),
        [pltpu.SemaphoreType.DMA],
        "keep",
        flops // ranks,
        spaces=[pltpu.HBM],
    )[0]
    loaded = (pair, bias, proj_weight, gate_weight, out_weight, chains[None, :], token_mask[None, :])
    joined = jax.ShapeDtypeStruct((2, width, 4 * hidden + width), proj_weight.dtype)
    own, bias, weights, out_weight, chains_t, mask_t, *partial = call(
        functools.partial(prep_kernel, masks, halves, early),
        [far, *sent.values()] + [pltpu.with_memory_space_constraint(each, pltpu.HBM) for each in loaded],
        like(pair, bias) + [joined] + like(out_weight) + floats((tokens, width), (tokens, width)) + half,
        [pltpu.VMEM((1, tokens), jnp.int32), pltpu.VMEM((1, tokens), jnp.int32), pltpu.SemaphoreType.DMA((7,))],
        "prep",
        flops // ranks,
        spaces=[pltpu.VMEM] * len(early) + [pltpu.HBM] * 7,
    )
    two = jnp.stack([kept, far])
    parts = [far[None]]
    for bits in range(1, top):
        if bits in sent:
            parts += [sent[bits][None], exchange(far, bits)[None]]
        else:
            parts.append(exchange(two, bits))
    mine = jnp.concatenate(parts + [own[None]], 0)
    other = lax.ppermute(mine, "col", [(0, 1), (1, 0)])
    edge_inputs = (chains_t, mask_t, bias, weights)
    partial = call(
        functools.partial(mine_kernel, masks, halves, early),
        (mine, *edge_inputs, *partial),
        half,
        [],
        "mine",
        flops,
        {n + 5: n for n in range(4)},
    )
    groups = cols // 8 + 1
    extra = [(groups * tokens * 8, hidden), (tokens * 8, hidden), ((groups - 1) * tokens * 8, hidden)]
    return call(
        functools.partial(crop_kernel, masks, halves),
        (other, *edge_inputs, out_weight, *partial),
        floats(pair.shape) + half,
        [pltpu.VMEM(each.shape, jnp.float32) for each in floats(*extra)],
        "crop",
        4 * flops,
        {n + 6: n + 1 for n in range(4)},
    )[0]


def shards(pair, token_mask, *rest):
    tokens = token_mask.shape[0]
    ranks = lax.axis_size("row")
    small = tokens * tokens * pair.shape[2] <= 1 << 18 and ranks & (ranks - 1) == 0 and pair.shape[1] % 8 == 0
    plan = whole_crop_plan if small and lax.axis_size("col") == 2 else sharded_plan
    return plan(pair, token_mask, *rest)


def solution(mesh):
    placed = (P(("group", "row"), "col", None), P("group"), P("group"), P(), P(), P(), P())
    return jax.shard_map(
        shards,
        mesh=mesh,
        in_specs=placed,
        out_specs=P(("group", "row"), "col", None),
        check_vma=False,
    )
```

```python
import functools
import jax
import jax.numpy as jnp
from jax import lax
from jax.experimental import pallas as pl
from jax.experimental.pallas import tpu as pltpu
from jax.sharding import PartitionSpec as P


def layer_norm(values):
    mean = jnp.mean(values, -1, keepdims=True)
    centred = values - mean
    var = jnp.mean(centred * centred, -1, keepdims=True)
    return centred * lax.rsqrt(var + 1e-05)


def flat_dot(values, weight):
    shape = values.shape
    result = jnp.dot(values.reshape(-1, shape[-1]), weight, preferred_element_type=jnp.float32)
    return result.reshape(shape[:-1] + (weight.shape[1],))


def project(state, pmask, p_weight):
    normed = layer_norm(state).astype(jnp.bfloat16)
    proj = flat_dot(normed, p_weight)
    hidden = p_weight.shape[1] // 4
    gate_a = proj[..., :hidden]
    value_a = proj[..., hidden : 2 * hidden]
    gate_b = proj[..., 2 * hidden : 3 * hidden]
    value_b = proj[..., 3 * hidden :]
    left = (jax.nn.sigmoid(gate_a) * value_a * pmask[..., None]).astype(jnp.bfloat16)
    right = (jax.nn.sigmoid(gate_b) * value_b * pmask[..., None]).astype(jnp.bfloat16)
    return (normed, left, right)


def finish(state, normed, tri, g_weight, o_weight):
    tnorm = layer_norm(tri).astype(jnp.bfloat16)
    gate = jax.nn.sigmoid(flat_dot(normed, g_weight))
    return state + gate * flat_dot(tnorm, o_weight)


def sharded_plan(pair, token_mask, chains, chain_bias, proj_weight, gate_weight, out_weight):
    rows, cols, width = pair.shape
    row_start = lax.axis_index("row") * rows
    col_start = lax.axis_index("col") * cols
    chain_rows = lax.dynamic_slice_in_dim(chains, row_start, rows)
    chain_cols = lax.dynamic_slice_in_dim(chains, col_start, cols)
    mask_rows = lax.dynamic_slice_in_dim(token_mask, row_start, rows).astype(jnp.float32)
    mask_cols = lax.dynamic_slice_in_dim(token_mask, col_start, cols).astype(jnp.float32)
    same = (chain_rows[:, None] == chain_cols[None, :]).astype(jnp.float32)
    state = pair + same[..., None] * chain_bias
    pmask = mask_rows[:, None] * mask_cols[None, :]
    normed, left, right = project(state, pmask, proj_weight[0])
    left_rows, right_rows = (
        lax.all_gather(left, "col", axis=1, tiled=True),
        lax.all_gather(right, "col", axis=1, tiled=True),
    )
    every = jnp.einsum(
        "ikh,jkh->ijh",
        left_rows,
        lax.all_gather(right_rows, "row", axis=0, tiled=True),
        preferred_element_type=jnp.float32,
    )
    tri = lax.dynamic_slice_in_dim(every, col_start, cols, 1)
    state = finish(state, normed, tri, gate_weight[0], out_weight[0])
    normed, left, right = project(state, pmask, proj_weight[1])
    left_rows = lax.all_gather(left, "col", axis=1, tiled=True)
    left_cols = lax.all_to_all(left_rows, "row", split_axis=1, concat_axis=0, tiled=True)
    tri = jnp.einsum(
        "kih,kjh->ijh",
        left_cols,
        lax.all_gather(right, "row", axis=0, tiled=True),
        preferred_element_type=jnp.float32,
    )
    return finish(state, normed, tri, gate_weight[1], out_weight[1])


def tile_norm(values):
    mean = jnp.mean(values, -1, keepdims=True)
    centred = values - mean
    var = jnp.mean(centred * centred, -1, keepdims=True)
    return centred * lax.rsqrt(var + 1e-05)


def gate_of(values):
    return 0.5 * jnp.tanh(0.5 * values) + 0.5


def dot(values, weight):
    return jnp.dot(values, weight, preferred_element_type=jnp.float32)


def rounded(values):
    return values.astype(jnp.bfloat16).astype(jnp.float32)


def table(row, out):
    tokens, width = out.shape
    at = lax.broadcasted_iota(jnp.int32, (tokens, tokens), 0)
    lane = lax.broadcasted_iota(jnp.int32, (tokens, tokens), 1)
    spread = jnp.where(at == lane, jnp.broadcast_to(row[...].astype(jnp.float32), (tokens, tokens)), 0.0)
    out[...] = jnp.broadcast_to(jnp.sum(spread, -1, keepdims=True), (tokens, width))


def edges(masks, items, chains, mask, bias, weights, start, gates, left, right):
    rows, cols, width = items[0][2].shape
    tokens = chains.shape[0]
    me = lax.axis_index("row")
    col = lax.axis_index("col")
    bias_v = bias[...]
    hidden = left.shape[-1]
    firsts = [pl.multiple_of(each * cols, cols) for each in (col, 1 - col)]
    chain_cols = [chains[pl.ds(first, cols), :] for first in firsts]
    mask_cols = [mask[pl.ds(first, cols), :] for first in firsts]
    states, pmasks = [], []
    for slot, half, block in items:
        for t in range(rows):
            token = (me ^ masks[slot]) * rows + t
            same = chain_cols[half] == chains[pl.ds(token, 1), :]
            states.append(block[t] + jnp.where(same, bias_v, 0.0))
            pmasks.append(mask_cols[half] * mask[pl.ds(token, 1), :])
    state = jnp.concatenate(states, 0)
    pmask = jnp.concatenate(pmasks, 0)
    proj = dot(tile_norm(state).astype(jnp.bfloat16), weights[0])
    lft = rounded(gate_of(proj[:, :hidden]) * proj[:, hidden : 2 * hidden] * pmask)
    rgt = rounded(gate_of(proj[:, 2 * hidden : 3 * hidden]) * proj[:, 3 * hidden : 4 * hidden] * pmask)
    size = rows * cols
    for n, (slot, half, _) in enumerate(items):
        span, part = pl.ds(slot * size, size), slice(n * size, (n + 1) * size)
        start[half, span, :] = state[part]
        gates[half, span, :] = proj[part, 4 * hidden :]
        for t in range(rows):
            token = (me ^ masks[slot]) * rows + t
            at = n * size + t * cols
            left[half, slot * rows + t] = lft[at : at + cols]
            right[half, pl.ds(token, cols, tokens), :] = rgt[at : at + cols]


def own_kernel(masks, *refs):
    sources, rest = refs[:7], refs[7:]
    pair, bias, weights, out_w, chains, mask, start, gates, left, right, chains_v, mask_v, sems = rest
    split = sources[2].shape[-1]
    proj_w, gate_w = weights.at[:, :, pl.ds(0, split)], weights.at[:, :, pl.ds(split, weights.shape[-1] - split)]
    loads = []
    for n, (source, target) in enumerate(zip(sources, (pair, bias, proj_w, gate_w, out_w, chains_v, mask_v))):
        loads.append(pltpu.make_async_copy(source, target, sems.at[n]))
    for load in loads:
        load.start()
    for load in loads:
        load.wait()
    table(chains_v, chains)
    table(mask_v, mask)
    edges(masks, [(0, 0, pair[...])], chains, mask, bias, weights, start, gates, left, right)


def mine_kernel(masks, halves, mine, chains, mask, bias, weights, s_in, g_in, l_in, r_in, *outs):
    items = [(slot, halves[slot], mine[slot]) for slot in range(1, len(masks))]
    edges(masks, items, chains, mask, bias, weights, *outs)


def crop_kernel(
    masks,
    halves,
    other,
    chains,
    mask,
    bias,
    weights,
    out_w,
    start_in,
    gates_in,
    left_in,
    right_in,
    updated,
    start,
    gates,
    left,
    right,
    tris,
    left1,
    right1,
):
    ranks, rows, cols, width = other.shape
    tokens = ranks * rows
    me = lax.axis_index("row")
    col = lax.axis_index("col")
    hidden = left.shape[-1]
    items = [(slot, 1 - halves[slot], other[slot]) for slot in range(ranks)]
    edges(masks, items, chains, mask, bias, weights, start, gates, left, right)

    low = me * rows // 8 * 8
    groups = [col * cols + 8 * n for n in range(cols // 8)] + [low]
    groups = [pl.multiple_of(g, 8) for g in groups]
    count = len(groups)
    block = 8

    real = jnp.sum(mask[...][:, :1]).astype(jnp.int32)
    lower = jnp.where(col == 0, 0, 1)

    def add_terms(acc, half, l, slots):
        cells = [right[half, pl.ds(pl.multiple_of(l * tokens + g, 8), 8), :] for g in groups]
        sums = []
        for k in range(block):
            row = left[half, slots[k // rows] * rows + k % rows, pl.ds(l, 1), :]
            for n in range(count):
                term = row * cells[n]
                sums.append(term if acc is None else acc[k * count + n] + term)
        return tuple(sums)

    def slots_of(step):
        ids = [(step * (block // rows) + n) ^ me for n in range(block // rows)]
        return [2 * lax.rem(each, ranks // 2) + each // (ranks // 2) for each in ids]

    def store(slots, values):
        for k in range(block):
            at = slots[k // rows] * rows + k % rows
            for n in range(count):
                tris[pl.ds(pl.multiple_of((n * tokens + at) * 8, 8), 8), :] = values[k * count + n]

    def tri_block(step, carry):
        slots = slots_of(step)
        acc = None
        for l in range(cols):
            acc = add_terms(acc, lower, l, slots)

        def upper(chunk, acc):
            for n in range(4):
                acc = add_terms(acc, 1 - lower, chunk * 4 + n, slots)
            return acc

        store(slots, lax.fori_loop(0, (real - cols + 3) // 4, upper, acc))
        return carry

    def zero_block(step, carry):
        store(slots_of(step), [jnp.zeros((8, hidden), jnp.float32)] * (block * count))
        return carry

    filled = (real + block - 1) // block
    lax.fori_loop(0, filled, tri_block, 0)
    lax.fori_loop(filled, tokens // block, zero_block, 0)

    low_half = jnp.where(low // cols == col, 0, 1)
    low_off = lax.rem(low, cols)
    mask_left = mask[pl.ds(pl.multiple_of(low, 8), 8), :]
    mask_right = mask[pl.ds(pl.multiple_of(col * cols, cols), cols), :]

    def gather(values, n, k):
        if n < count - 1:
            return values[0, pl.ds(k * cols + 8 * n, 8), :]
        return values[low_half, pl.ds(pl.multiple_of(k * cols + low_off, 8), 8), :]

    row_masks = []
    for slot in range(ranks):
        for t in range(rows):
            row_masks.append(mask[pl.ds((me ^ masks[slot]) * rows + t, 1), :])

    cells = [(n, k) for n in range(count) for k in range(tokens)]
    tnorm = tile_norm(tris[...]).astype(jnp.bfloat16)
    gate = gate_of(jnp.concatenate([gather(gates, n, k) for n, k in cells], 0))
    state = jnp.concatenate([gather(start, n, k) for n, k in cells], 0)
    state = state + gate * dot(tnorm, out_w[0])
    normed = tile_norm(state).astype(jnp.bfloat16)
    edge_rows = (count - 1) * tokens * 8
    proj_r = dot(normed[:edge_rows], weights[1, :, 2 * hidden : 4 * hidden])
    proj_l = dot(normed[edge_rows:], weights[1, :, : 2 * hidden])
    own = [slice(n * tokens * 8, n * tokens * 8 + rows * 8) for n in range(count - 1)]
    own_state = jnp.concatenate([state[part] for part in own], 0)
    own_logit = dot(jnp.concatenate([normed[part] for part in own], 0), weights[1, :, 4 * hidden :])
    pm = jnp.concatenate([mask_left * m for m in row_masks], 0)
    left1[...] = rounded(gate_of(proj_l[:, :hidden]) * proj_l[:, hidden:] * pm)
    pm = jnp.concatenate([mask_right[8 * n : 8 * n + 8] * m for n in range(count - 1) for m in row_masks], 0)
    right1[...] = rounded(gate_of(proj_r[:, :hidden]) * proj_r[:, hidden:] * pm)

    shift = lax.rem(me * rows, 8)
    acc = [[None] * rows for _ in range(count - 1)]
    for k in range(tokens):
        for n in range(count - 1):
            cell = right1[pl.ds((n * tokens + k) * 8, 8), :]
            for t in range(rows):
                term = left1[pl.ds(k * 8 + shift + t, 1), :] * cell
                acc[n][t] = term if k == 0 else acc[n][t] + term
    tri = jnp.concatenate([acc[n][t] for n in range(count - 1) for t in range(rows)], 0)
    tnorm = tile_norm(tri).astype(jnp.bfloat16)
    out = own_state + gate_of(own_logit) * dot(tnorm, out_w[1])
    for n in range(count - 1):
        for t in range(rows):
            at = (n * rows + t) * 8
            updated[t, pl.ds(8 * n, 8), :] = out[at : at + 8]


def exchange(block, bits):
    ranks = lax.axis_size("row")
    hops = [(2 * i + c, 2 * (i ^ bits) + 1 - c) for i in range(ranks) for c in range(2)]
    return lax.ppermute(block, ("row", "col"), hops)


def call(body, inputs, outputs, scratch, name, flops, aliases={}, space=pltpu.VMEM):
    return pl.pallas_call(
        body,
        out_shape=outputs,
        in_specs=[pl.BlockSpec(memory_space=space)] * len(inputs),
        out_specs=[pl.BlockSpec(memory_space=pltpu.VMEM)] * len(outputs),
        scratch_shapes=scratch,
        compiler_params=pltpu.CompilerParams(vmem_limit_bytes=32 << 20),
        input_output_aliases=aliases,
        cost_estimate=pl.CostEstimate(flops=flops, bytes_accessed=1 << 21, transcendentals=0),
        name=name,
    )(*inputs)


def floats(*shapes):
    return [jax.ShapeDtypeStruct(shape, jnp.float32) for shape in shapes]


def like(*arrays):
    return [jax.ShapeDtypeStruct(array.shape, array.dtype) for array in arrays]


def whole_crop_plan(pair, token_mask, chains, chain_bias, proj_weight, gate_weight, out_weight):
    rows, cols, width = pair.shape
    ranks = lax.axis_size("row")
    tokens = token_mask.shape[0]
    hidden = proj_weight.shape[2] // 4
    bias = chain_bias[None, :]
    half = [(2, tokens * cols, width), (2, tokens * cols, width), (2, tokens, cols, hidden), (2, tokens * cols, hidden)]
    half = floats(*half)
    flops = 2 * tokens * cols * width * 5 * hidden
    top = ranks // 2
    masks, halves = [0, top], [0, 1]
    for bits in range(1, top):
        masks += [bits, bits ^ top]
        halves += [1, 0]
    far = exchange(pair, top)
    loaded = (pair, bias, proj_weight, gate_weight, out_weight, chains[None, :], token_mask[None, :])
    joined = jax.ShapeDtypeStruct((2, width, 4 * hidden + width), proj_weight.dtype)
    own, bias, weights, out_weight, chains_t, mask_t, *partial = call(
        functools.partial(own_kernel, masks),
        [pltpu.with_memory_space_constraint(each, pltpu.HBM) for each in loaded],
        like(pair, bias) + [joined] + like(out_weight) + floats((tokens, width), (tokens, width)) + half,
        [pltpu.VMEM((1, tokens), jnp.int32), pltpu.VMEM((1, tokens), jnp.int32), pltpu.SemaphoreType.DMA((7,))],
        "own",
        flops // ranks,
        space=pltpu.HBM,
    )
    two = jnp.stack([own, far])
    mine = jnp.concatenate([two] + [exchange(two, bits) for bits in range(1, top)], 0)
    other = lax.ppermute(mine, "col", [(0, 1), (1, 0)])
    edge_inputs = (chains_t, mask_t, bias, weights)
    partial = call(
        functools.partial(mine_kernel, masks, halves),
        (mine, *edge_inputs, *partial),
        half,
        [],
        "mine",
        flops,
        {n + 5: n for n in range(4)},
    )
    groups = cols // 8 + 1
    extra = [(groups * tokens * 8, hidden), (tokens * 8, hidden), ((groups - 1) * tokens * 8, hidden)]
    return call(
        functools.partial(crop_kernel, masks, halves),
        (other, *edge_inputs, out_weight, *partial),
        floats(pair.shape) + half,
        [pltpu.VMEM(each.shape, jnp.float32) for each in floats(*extra)],
        "crop",
        4 * flops,
        {n + 6: n + 1 for n in range(4)},
    )[0]


def shards(pair, token_mask, *rest):
    tokens = token_mask.shape[0]
    ranks = lax.axis_size("row")
    small = tokens * tokens * pair.shape[2] <= 1 << 18 and ranks & (ranks - 1) == 0 and pair.shape[1] % 8 == 0
    plan = whole_crop_plan if small and lax.axis_size("col") == 2 else sharded_plan
    return plan(pair, token_mask, *rest)


def solution(mesh):
    placed = (P(("group", "row"), "col", None), P("group"), P("group"), P(), P(), P(), P())
    return jax.shard_map(
        shards,
        mesh=mesh,
        in_specs=placed,
        out_specs=P(("group", "row"), "col", None),
        check_vma=False,
    )
```

```python
import functools
import jax
import jax.numpy as jnp
from jax import lax
from jax.experimental import pallas as pl
from jax.experimental.pallas import tpu as pltpu
from jax.sharding import PartitionSpec as P


def layer_norm(values):
    mean = jnp.mean(values, -1, keepdims=True)
    centred = values - mean
    var = jnp.mean(centred * centred, -1, keepdims=True)
    return centred * lax.rsqrt(var + 1e-05)


def flat_dot(values, weight):
    shape = values.shape
    result = jnp.dot(values.reshape(-1, shape[-1]), weight, preferred_element_type=jnp.float32)
    return result.reshape(shape[:-1] + (weight.shape[1],))


def project(state, pmask, p_weight):
    normed = layer_norm(state).astype(jnp.bfloat16)
    proj = flat_dot(normed, p_weight)
    hidden = p_weight.shape[1] // 4
    gate_a = proj[..., :hidden]
    value_a = proj[..., hidden : 2 * hidden]
    gate_b = proj[..., 2 * hidden : 3 * hidden]
    value_b = proj[..., 3 * hidden :]
    left = (jax.nn.sigmoid(gate_a) * value_a * pmask[..., None]).astype(jnp.bfloat16)
    right = (jax.nn.sigmoid(gate_b) * value_b * pmask[..., None]).astype(jnp.bfloat16)
    return (normed, left, right)


def finish(state, normed, tri, g_weight, o_weight):
    tnorm = layer_norm(tri).astype(jnp.bfloat16)
    gate = jax.nn.sigmoid(flat_dot(normed, g_weight))
    return state + gate * flat_dot(tnorm, o_weight)


def sharded_plan(pair, token_mask, chains, chain_bias, proj_weight, gate_weight, out_weight):
    rows, cols, width = pair.shape
    row_start = lax.axis_index("row") * rows
    col_start = lax.axis_index("col") * cols
    chain_rows = lax.dynamic_slice_in_dim(chains, row_start, rows)
    chain_cols = lax.dynamic_slice_in_dim(chains, col_start, cols)
    mask_rows = lax.dynamic_slice_in_dim(token_mask, row_start, rows).astype(jnp.float32)
    mask_cols = lax.dynamic_slice_in_dim(token_mask, col_start, cols).astype(jnp.float32)
    same = (chain_rows[:, None] == chain_cols[None, :]).astype(jnp.float32)
    state = pair + same[..., None] * chain_bias
    pmask = mask_rows[:, None] * mask_cols[None, :]
    normed, left, right = project(state, pmask, proj_weight[0])
    left_rows, right_rows = (
        lax.all_gather(left, "col", axis=1, tiled=True),
        lax.all_gather(right, "col", axis=1, tiled=True),
    )
    every = jnp.einsum(
        "ikh,jkh->ijh",
        left_rows,
        lax.all_gather(right_rows, "row", axis=0, tiled=True),
        preferred_element_type=jnp.float32,
    )
    tri = lax.dynamic_slice_in_dim(every, col_start, cols, 1)
    state = finish(state, normed, tri, gate_weight[0], out_weight[0])
    normed, left, right = project(state, pmask, proj_weight[1])
    left_rows = lax.all_gather(left, "col", axis=1, tiled=True)
    left_cols = lax.all_to_all(left_rows, "row", split_axis=1, concat_axis=0, tiled=True)
    tri = jnp.einsum(
        "kih,kjh->ijh",
        left_cols,
        lax.all_gather(right, "row", axis=0, tiled=True),
        preferred_element_type=jnp.float32,
    )
    return finish(state, normed, tri, gate_weight[1], out_weight[1])


def tile_norm(values):
    mean = jnp.mean(values, -1, keepdims=True)
    centred = values - mean
    var = jnp.mean(centred * centred, -1, keepdims=True)
    return centred * lax.rsqrt(var + 1e-05)


def gate_of(values):
    return 0.5 * jnp.tanh(0.5 * values) + 0.5


def dot(values, weight):
    return jnp.dot(values, weight, preferred_element_type=jnp.float32)


def rounded(values):
    return values.astype(jnp.bfloat16).astype(jnp.float32)


def table(row, out):
    tokens, width = out.shape
    at = lax.broadcasted_iota(jnp.int32, (tokens, tokens), 0)
    lane = lax.broadcasted_iota(jnp.int32, (tokens, tokens), 1)
    spread = jnp.where(at == lane, jnp.broadcast_to(row[...].astype(jnp.float32), (tokens, tokens)), 0.0)
    out[...] = jnp.broadcast_to(jnp.sum(spread, -1, keepdims=True), (tokens, width))


def edges(masks, items, chains, mask, bias, weights, start, gates, left, right):
    rows, cols, width = items[0][2].shape
    tokens = chains.shape[0]
    me = lax.axis_index("row")
    col = lax.axis_index("col")
    bias_v = bias[...]
    hidden = left.shape[-1]
    firsts = [pl.multiple_of(each * cols, cols) for each in (col, 1 - col)]
    chain_cols = [chains[pl.ds(first, cols), :] for first in firsts]
    mask_cols = [mask[pl.ds(first, cols), :] for first in firsts]
    states, pmasks = [], []
    for slot, half, block in items:
        for t in range(rows):
            token = (me ^ masks[slot]) * rows + t
            same = chain_cols[half] == chains[pl.ds(token, 1), :]
            states.append(block[t] + jnp.where(same, bias_v, 0.0))
            pmasks.append(mask_cols[half] * mask[pl.ds(token, 1), :])
    state = jnp.concatenate(states, 0)
    pmask = jnp.concatenate(pmasks, 0)
    proj = dot(tile_norm(state).astype(jnp.bfloat16), weights[0])
    lft = rounded(gate_of(proj[:, :hidden]) * proj[:, hidden : 2 * hidden] * pmask)
    rgt = rounded(gate_of(proj[:, 2 * hidden : 3 * hidden]) * proj[:, 3 * hidden : 4 * hidden] * pmask)
    size = rows * cols
    for n, (slot, half, _) in enumerate(items):
        span, part = pl.ds(slot * size, size), slice(n * size, (n + 1) * size)
        start[half, span, :] = state[part]
        gates[half, span, :] = proj[part, 4 * hidden :]
        for t in range(rows):
            token = (me ^ masks[slot]) * rows + t
            at = n * size + t * cols
            left[half, slot * rows + t] = lft[at : at + cols]
            right[half, pl.ds(token, cols, tokens), :] = rgt[at : at + cols]


def keep_kernel(source, target, sem):
    load = pltpu.make_async_copy(source, target, sem)
    load.start()
    load.wait()


def prep_kernel(masks, halves, early, *refs):
    blocks, refs = refs[: len(early)], refs[len(early) :]
    sources, rest = refs[:7], refs[7:]
    pair, bias, weights, out_w, chains, mask, start, gates, left, right, chains_v, mask_v, sems = rest
    split = sources[2].shape[-1]
    proj_w, gate_w = weights.at[:, :, pl.ds(0, split)], weights.at[:, :, pl.ds(split, weights.shape[-1] - split)]
    loads = []
    for n, (source, target) in enumerate(zip(sources, (pair, bias, proj_w, gate_w, out_w, chains_v, mask_v))):
        loads.append(pltpu.make_async_copy(source, target, sems.at[n]))
    for load in loads:
        load.start()
    for load in loads:
        load.wait()
    table(chains_v, chains)
    table(mask_v, mask)
    items = [(len(masks) - 1, halves[-1], pair[...])] + [(slot, halves[slot], block[...]) for slot, block in zip(early, blocks)]
    edges(masks, items, chains, mask, bias, weights, start, gates, left, right)


def mine_kernel(masks, halves, early, mine, chains, mask, bias, weights, s_in, g_in, l_in, r_in, *outs):
    items = [(slot, halves[slot], mine[slot]) for slot in range(len(masks) - 1) if slot not in early]
    edges(masks, items, chains, mask, bias, weights, *outs)


def crop_kernel(
    masks,
    halves,
    other,
    chains,
    mask,
    bias,
    weights,
    out_w,
    start_in,
    gates_in,
    left_in,
    right_in,
    updated,
    start,
    gates,
    left,
    right,
    tris,
    left1,
    right1,
):
    ranks, rows, cols, width = other.shape
    tokens = ranks * rows
    me = lax.axis_index("row")
    col = lax.axis_index("col")
    hidden = left.shape[-1]
    items = [(slot, 1 - halves[slot], other[slot]) for slot in range(ranks)]
    edges(masks, items, chains, mask, bias, weights, start, gates, left, right)

    low = me * rows // 8 * 8
    groups = [col * cols + 8 * n for n in range(cols // 8)] + [low]
    groups = [pl.multiple_of(g, 8) for g in groups]
    count = len(groups)
    block = 8

    real = jnp.sum(mask[...][:, :1]).astype(jnp.int32)
    lower = jnp.where(col == 0, 0, 1)

    def add_terms(acc, half, l, slots):
        cells = [right[half, pl.ds(pl.multiple_of(l * tokens + g, 8), 8), :] for g in groups]
        sums = []
        for k in range(block):
            row = left[half, slots[k // rows] * rows + k % rows, pl.ds(l, 1), :]
            for n in range(count):
                term = row * cells[n]
                sums.append(term if acc is None else acc[k * count + n] + term)
        return tuple(sums)

    def slots_of(step):
        ids = [(step * (block // rows) + n) ^ me for n in range(block // rows)]
        places = [2 * lax.rem(each, ranks // 2) + each // (ranks // 2) for each in ids]
        return [lax.rem(place + ranks - 1, ranks) for place in places]

    def store(slots, values):
        for k in range(block):
            at = slots[k // rows] * rows + k % rows
            for n in range(count):
                tris[pl.ds(pl.multiple_of((n * tokens + at) * 8, 8), 8), :] = values[k * count + n]

    def tri_block(step, carry):
        slots = slots_of(step)
        acc = None
        for l in range(cols):
            acc = add_terms(acc, lower, l, slots)

        def upper(chunk, acc):
            for n in range(4):
                acc = add_terms(acc, 1 - lower, chunk * 4 + n, slots)
            return acc

        store(slots, lax.fori_loop(0, (real - cols + 3) // 4, upper, acc))
        return carry

    def zero_block(step, carry):
        store(slots_of(step), [jnp.zeros((8, hidden), jnp.float32)] * (block * count))
        return carry

    filled = (real + block - 1) // block
    lax.fori_loop(0, filled, tri_block, 0)
    lax.fori_loop(filled, tokens // block, zero_block, 0)

    low_half = jnp.where(low // cols == col, 0, 1)
    low_off = lax.rem(low, cols)
    mask_left = mask[pl.ds(pl.multiple_of(low, 8), 8), :]
    mask_right = mask[pl.ds(pl.multiple_of(col * cols, cols), cols), :]

    def gather(values, n, k):
        if n < count - 1:
            return values[0, pl.ds(k * cols + 8 * n, 8), :]
        return values[low_half, pl.ds(pl.multiple_of(k * cols + low_off, 8), 8), :]

    row_masks = []
    for slot in range(ranks):
        for t in range(rows):
            row_masks.append(mask[pl.ds((me ^ masks[slot]) * rows + t, 1), :])

    cells = [(n, k) for n in range(count) for k in range(tokens)]
    tnorm = tile_norm(tris[...]).astype(jnp.bfloat16)
    gate = gate_of(jnp.concatenate([gather(gates, n, k) for n, k in cells], 0))
    state = jnp.concatenate([gather(start, n, k) for n, k in cells], 0)
    state = state + gate * dot(tnorm, out_w[0])
    normed = tile_norm(state).astype(jnp.bfloat16)
    edge_rows = (count - 1) * tokens * 8
    proj_r = dot(normed[:edge_rows], weights[1, :, 2 * hidden : 4 * hidden])
    proj_l = dot(normed[edge_rows:], weights[1, :, : 2 * hidden])
    ends = [(n + 1) * tokens * 8 for n in range(count - 1)]
    own = [slice(end - rows * 8, end) for end in ends]
    own_state = jnp.concatenate([state[part] for part in own], 0)
    own_logit = dot(jnp.concatenate([normed[part] for part in own], 0), weights[1, :, 4 * hidden :])
    pm = jnp.concatenate([mask_left * m for m in row_masks], 0)
    left1[...] = rounded(gate_of(proj_l[:, :hidden]) * proj_l[:, hidden:] * pm)
    pm = jnp.concatenate([mask_right[8 * n : 8 * n + 8] * m for n in range(count - 1) for m in row_masks], 0)
    right1[...] = rounded(gate_of(proj_r[:, :hidden]) * proj_r[:, hidden:] * pm)

    shift = lax.rem(me * rows, 8)
    acc = [[None] * rows for _ in range(count - 1)]
    for k in range(tokens):
        for n in range(count - 1):
            cell = right1[pl.ds((n * tokens + k) * 8, 8), :]
            for t in range(rows):
                term = left1[pl.ds(k * 8 + shift + t, 1), :] * cell
                acc[n][t] = term if k == 0 else acc[n][t] + term
    tri = jnp.concatenate([acc[n][t] for n in range(count - 1) for t in range(rows)], 0)
    tnorm = tile_norm(tri).astype(jnp.bfloat16)
    out = own_state + gate_of(own_logit) * dot(tnorm, out_w[1])
    for n in range(count - 1):
        for t in range(rows):
            at = (n * rows + t) * 8
            updated[t, pl.ds(8 * n, 8), :] = out[at : at + 8]


def exchange(block, bits):
    ranks = lax.axis_size("row")
    hops = [(2 * i + c, 2 * (i ^ bits) + 1 - c) for i in range(ranks) for c in range(2)]
    return lax.ppermute(block, ("row", "col"), hops)


def call(body, inputs, outputs, scratch, name, flops, aliases={}, spaces=None):
    return pl.pallas_call(
        body,
        out_shape=outputs,
        in_specs=[pl.BlockSpec(memory_space=each) for each in spaces or [pltpu.VMEM] * len(inputs)],
        out_specs=[pl.BlockSpec(memory_space=pltpu.VMEM)] * len(outputs),
        scratch_shapes=scratch,
        compiler_params=pltpu.CompilerParams(vmem_limit_bytes=32 << 20),
        input_output_aliases=aliases,
        cost_estimate=pl.CostEstimate(flops=flops, bytes_accessed=1 << 21, transcendentals=0),
        name=name,
    )(*inputs)


def floats(*shapes):
    return [jax.ShapeDtypeStruct(shape, jnp.float32) for shape in shapes]


def like(*arrays):
    return [jax.ShapeDtypeStruct(array.shape, array.dtype) for array in arrays]


def whole_crop_plan(pair, token_mask, chains, chain_bias, proj_weight, gate_weight, out_weight):
    rows, cols, width = pair.shape
    ranks = lax.axis_size("row")
    tokens = token_mask.shape[0]
    hidden = proj_weight.shape[2] // 4
    bias = chain_bias[None, :]
    half = [(2, tokens * cols, width), (2, tokens * cols, width), (2, tokens, cols, hidden), (2, tokens * cols, hidden)]
    half = floats(*half)
    flops = 2 * tokens * cols * width * 5 * hidden
    top = ranks // 2
    masks, halves = [top], [1]
    for bits in range(1, top):
        masks += [bits, bits ^ top]
        halves += [1, 0]
    masks, halves = masks + [0], halves + [0]
    near = [1]
    early = [masks.index(bits) for bits in [top] + near]
    far = exchange(pair, top)
    sent = {bits: exchange(pair, bits) for bits in near}
    kept = call(
        keep_kernel,
        [pltpu.with_memory_space_constraint(pair, pltpu.HBM)],
        like(pair),
        [pltpu.SemaphoreType.DMA],
        "keep",
        flops // ranks,
        spaces=[pltpu.HBM],
    )[0]
    loaded = (pair, bias, proj_weight, gate_weight, out_weight, chains[None, :], token_mask[None, :])
    joined = jax.ShapeDtypeStruct((2, width, 4 * hidden + width), proj_weight.dtype)
    own, bias, weights, out_weight, chains_t, mask_t, *partial = call(
        functools.partial(prep_kernel, masks, halves, early),
        [far, *sent.values()] + [pltpu.with_memory_space_constraint(each, pltpu.HBM) for each in loaded],
        like(pair, bias) + [joined] + like(out_weight) + floats((tokens, width), (tokens, width)) + half,
        [pltpu.VMEM((1, tokens), jnp.int32), pltpu.VMEM((1, tokens), jnp.int32), pltpu.SemaphoreType.DMA((7,))],
        "prep",
        flops // ranks,
        spaces=[pltpu.VMEM] * len(early) + [pltpu.HBM] * 7,
    )
    two = jnp.stack([kept, far])
    parts = [far[None]]
    for bits in range(1, top):
        if bits in sent:
            parts += [sent[bits][None], exchange(far, bits)[None]]
        else:
            parts.append(exchange(two, bits))
    mine = jnp.concatenate(parts + [own[None]], 0)
    other = lax.ppermute(mine, "col", [(0, 1), (1, 0)])
    edge_inputs = (chains_t, mask_t, bias, weights)
    partial = call(
        functools.partial(mine_kernel, masks, halves, early),
        (mine, *edge_inputs, *partial),
        half,
        [],
        "mine",
        flops,
        {n + 5: n for n in range(4)},
    )
    groups = cols // 8 + 1
    extra = [(groups * tokens * 8, hidden), (tokens * 8, hidden), ((groups - 1) * tokens * 8, hidden)]
    return call(
        functools.partial(crop_kernel, masks, halves),
        (other, *edge_inputs, out_weight, *partial),
        floats(pair.shape) + half,
        [pltpu.VMEM(each.shape, jnp.float32) for each in floats(*extra)],
        "crop",
        4 * flops,
        {n + 6: n + 1 for n in range(4)},
    )[0]


def shards(pair, token_mask, *rest):
    tokens = token_mask.shape[0]
    ranks = lax.axis_size("row")
    small = tokens * tokens * pair.shape[2] <= 1 << 18 and ranks & (ranks - 1) == 0 and pair.shape[1] % 8 == 0
    plan = whole_crop_plan if small and lax.axis_size("col") == 2 else sharded_plan
    return plan(pair, token_mask, *rest)


def solution(mesh):
    placed = (P(("group", "row"), "col", None), P("group"), P("group"), P(), P(), P(), P())
    return jax.shard_map(
        shards,
        mesh=mesh,
        in_specs=placed,
        out_specs=P(("group", "row"), "col", None),
        check_vma=False,
    )
```

```python
import functools
import jax
import jax.numpy as jnp
from jax import lax
from jax.experimental import pallas as pl
from jax.experimental.pallas import tpu as pltpu
from jax.sharding import PartitionSpec as P


def layer_norm(values):
    mean = jnp.mean(values, -1, keepdims=True)
    centred = values - mean
    var = jnp.mean(centred * centred, -1, keepdims=True)
    return centred * lax.rsqrt(var + 1e-05)


def flat_dot(values, weight):
    shape = values.shape
    result = jnp.dot(values.reshape(-1, shape[-1]), weight, preferred_element_type=jnp.float32)
    return result.reshape(shape[:-1] + (weight.shape[1],))


def project(state, pmask, p_weight):
    normed = layer_norm(state).astype(jnp.bfloat16)
    proj = flat_dot(normed, p_weight)
    hidden = p_weight.shape[1] // 4
    gate_a = proj[..., :hidden]
    value_a = proj[..., hidden : 2 * hidden]
    gate_b = proj[..., 2 * hidden : 3 * hidden]
    value_b = proj[..., 3 * hidden :]
    left = (jax.nn.sigmoid(gate_a) * value_a * pmask[..., None]).astype(jnp.bfloat16)
    right = (jax.nn.sigmoid(gate_b) * value_b * pmask[..., None]).astype(jnp.bfloat16)
    return (normed, left, right)


def finish(state, normed, tri, g_weight, o_weight):
    tnorm = layer_norm(tri).astype(jnp.bfloat16)
    gate = jax.nn.sigmoid(flat_dot(normed, g_weight))
    return state + gate * flat_dot(tnorm, o_weight)


def sharded_plan(pair, token_mask, chains, chain_bias, proj_weight, gate_weight, out_weight):
    rows, cols, width = pair.shape
    row_start = lax.axis_index("row") * rows
    col_start = lax.axis_index("col") * cols
    chain_rows = lax.dynamic_slice_in_dim(chains, row_start, rows)
    chain_cols = lax.dynamic_slice_in_dim(chains, col_start, cols)
    mask_rows = lax.dynamic_slice_in_dim(token_mask, row_start, rows).astype(jnp.float32)
    mask_cols = lax.dynamic_slice_in_dim(token_mask, col_start, cols).astype(jnp.float32)
    same = (chain_rows[:, None] == chain_cols[None, :]).astype(jnp.float32)
    state = pair + same[..., None] * chain_bias
    pmask = mask_rows[:, None] * mask_cols[None, :]
    normed, left, right = project(state, pmask, proj_weight[0])
    left_rows, right_rows = (
        lax.all_gather(left, "col", axis=1, tiled=True),
        lax.all_gather(right, "col", axis=1, tiled=True),
    )
    every = jnp.einsum(
        "ikh,jkh->ijh",
        left_rows,
        lax.all_gather(right_rows, "row", axis=0, tiled=True),
        preferred_element_type=jnp.float32,
    )
    tri = lax.dynamic_slice_in_dim(every, col_start, cols, 1)
    state = finish(state, normed, tri, gate_weight[0], out_weight[0])
    normed, left, right = project(state, pmask, proj_weight[1])
    left_rows = lax.all_gather(left, "col", axis=1, tiled=True)
    left_cols = lax.all_to_all(left_rows, "row", split_axis=1, concat_axis=0, tiled=True)
    tri = jnp.einsum(
        "kih,kjh->ijh",
        left_cols,
        lax.all_gather(right, "row", axis=0, tiled=True),
        preferred_element_type=jnp.float32,
    )
    return finish(state, normed, tri, gate_weight[1], out_weight[1])


def tile_norm(values):
    mean = jnp.mean(values, -1, keepdims=True)
    centred = values - mean
    var = jnp.mean(centred * centred, -1, keepdims=True)
    return centred * lax.rsqrt(var + 1e-05)


def gate_of(values):
    return 0.5 * jnp.tanh(0.5 * values) + 0.5


def dot(values, weight):
    return jnp.dot(values, weight, preferred_element_type=jnp.float32)


def rounded(values):
    return values.astype(jnp.bfloat16).astype(jnp.float32)


def table(row, out):
    tokens, width = out.shape
    at = lax.broadcasted_iota(jnp.int32, (tokens, tokens), 0)
    lane = lax.broadcasted_iota(jnp.int32, (tokens, tokens), 1)
    spread = jnp.where(at == lane, jnp.broadcast_to(row[...].astype(jnp.float32), (tokens, tokens)), 0.0)
    out[...] = jnp.broadcast_to(jnp.sum(spread, -1, keepdims=True), (tokens, width))


def edges(masks, items, chains, mask, bias, weights, start, gates, left, right):
    rows, cols, width = items[0][2].shape
    tokens = chains.shape[0]
    me = lax.axis_index("row")
    col = lax.axis_index("col")
    bias_v = bias[...]
    hidden = left.shape[-1]
    firsts = [pl.multiple_of(each * cols, cols) for each in (col, 1 - col)]
    chain_cols = [chains[pl.ds(first, cols), :] for first in firsts]
    mask_cols = [mask[pl.ds(first, cols), :] for first in firsts]
    states, pmasks = [], []
    for slot, half, block in items:
        for t in range(rows):
            token = (me ^ masks[slot]) * rows + t
            same = chain_cols[half] == chains[pl.ds(token, 1), :]
            states.append(block[t] + jnp.where(same, bias_v, 0.0))
            pmasks.append(mask_cols[half] * mask[pl.ds(token, 1), :])
    state = jnp.concatenate(states, 0)
    pmask = jnp.concatenate(pmasks, 0)
    proj = dot(tile_norm(state).astype(jnp.bfloat16), weights[0])
    lft = rounded(gate_of(proj[:, :hidden]) * proj[:, hidden : 2 * hidden] * pmask)
    rgt = rounded(gate_of(proj[:, 2 * hidden : 3 * hidden]) * proj[:, 3 * hidden : 4 * hidden] * pmask)
    size = rows * cols
    for n, (slot, half, _) in enumerate(items):
        span, part = pl.ds(slot * size, size), slice(n * size, (n + 1) * size)
        start[half, span, :] = state[part]
        gates[half, span, :] = proj[part, 4 * hidden :]
        for t in range(rows):
            token = (me ^ masks[slot]) * rows + t
            at = n * size + t * cols
            left[half, slot * rows + t] = lft[at : at + cols]
            right[half, pl.ds(token, cols, tokens), :] = rgt[at : at + cols]


def keep_kernel(source, target, sem):
    load = pltpu.make_async_copy(source, target, sem)
    load.start()
    load.wait()


def prep_kernel(masks, halves, early, *refs):
    blocks, refs = refs[: len(early)], refs[len(early) :]
    sources, rest = refs[:7], refs[7:]
    pair, bias, weights, out_w, chains, mask, start, gates, left, right, chains_v, mask_v, sems = rest
    split = sources[2].shape[-1]
    proj_w, gate_w = weights.at[:, :, pl.ds(0, split)], weights.at[:, :, pl.ds(split, weights.shape[-1] - split)]
    loads = []
    for n, (source, target) in enumerate(zip(sources, (pair, bias, proj_w, gate_w, out_w, chains_v, mask_v))):
        loads.append(pltpu.make_async_copy(source, target, sems.at[n]))
    for load in loads:
        load.start()
    for load in loads:
        load.wait()
    table(chains_v, chains)
    table(mask_v, mask)
    items = [(len(masks) - 1, halves[-1], pair[...])] + [(slot, halves[slot], block[...]) for slot, block in zip(early, blocks)]
    edges(masks, items, chains, mask, bias, weights, start, gates, left, right)


def mine_kernel(masks, halves, early, mine, chains, mask, bias, weights, s_in, g_in, l_in, r_in, *outs):
    items = [(slot, halves[slot], mine[slot]) for slot in range(len(masks) - 1) if slot not in early]
    edges(masks, items, chains, mask, bias, weights, *outs)


def crop_kernel(
    masks,
    halves,
    other,
    chains,
    mask,
    bias,
    weights,
    out_w,
    start_in,
    gates_in,
    left_in,
    right_in,
    updated,
    start,
    gates,
    left,
    right,
    tris,
    left1,
    right1,
):
    ranks, rows, cols, width = other.shape
    tokens = ranks * rows
    me = lax.axis_index("row")
    col = lax.axis_index("col")
    hidden = left.shape[-1]
    items = [(slot, 1 - halves[slot], other[slot]) for slot in range(ranks)]
    edges(masks, items, chains, mask, bias, weights, start, gates, left, right)

    low = me * rows // 8 * 8
    groups = [col * cols + 8 * n for n in range(cols // 8)] + [low]
    groups = [pl.multiple_of(g, 8) for g in groups]
    count = len(groups)
    block = 8

    real = jnp.sum(mask[...][:, :1]).astype(jnp.int32)
    lower = jnp.where(col == 0, 0, 1)

    def add_terms(acc, half, l, slots):
        cells = [right[half, pl.ds(pl.multiple_of(l * tokens + g, 8), 8), :] for g in groups]
        sums = []
        for k in range(block):
            row = left[half, slots[k // rows] * rows + k % rows, pl.ds(l, 1), :]
            for n in range(count):
                term = row * cells[n]
                sums.append(term if acc is None else acc[k * count + n] + term)
        return tuple(sums)

    def slots_of(step):
        ids = [(step * (block // rows) + n) ^ me for n in range(block // rows)]
        places = [2 * lax.rem(each, ranks // 2) + each // (ranks // 2) for each in ids]
        return [lax.rem(place + ranks - 1, ranks) for place in places]

    def store(slots, values):
        for k in range(block):
            at = slots[k // rows] * rows + k % rows
            for n in range(count):
                tris[pl.ds(pl.multiple_of((n * tokens + at) * 8, 8), 8), :] = values[k * count + n]

    def tri_block(step, carry):
        slots = slots_of(step)
        acc = None
        for l in range(cols):
            acc = add_terms(acc, lower, l, slots)

        def upper(chunk, acc):
            for n in range(4):
                acc = add_terms(acc, 1 - lower, chunk * 4 + n, slots)
            return acc

        store(slots, lax.fori_loop(0, (real - cols + 3) // 4, upper, acc))
        return carry

    def zero_block(step, carry):
        store(slots_of(step), [jnp.zeros((8, hidden), jnp.float32)] * (block * count))
        return carry

    filled = (real + block - 1) // block
    lax.fori_loop(0, filled, tri_block, 0)
    lax.fori_loop(filled, tokens // block, zero_block, 0)

    low_half = jnp.where(low // cols == col, 0, 1)
    low_off = lax.rem(low, cols)
    mask_left = mask[pl.ds(pl.multiple_of(low, 8), 8), :]
    mask_right = mask[pl.ds(pl.multiple_of(col * cols, cols), cols), :]

    def gather(values, n, k):
        if n < count - 1:
            return values[0, pl.ds(k * cols + 8 * n, 8), :]
        return values[low_half, pl.ds(pl.multiple_of(k * cols + low_off, 8), 8), :]

    row_masks = []
    for slot in range(ranks):
        for t in range(rows):
            row_masks.append(mask[pl.ds((me ^ masks[slot]) * rows + t, 1), :])

    cells = [(n, k) for n in range(count) for k in range(tokens)]
    tnorm = tile_norm(tris[...]).astype(jnp.bfloat16)
    gate = gate_of(jnp.concatenate([gather(gates, n, k) for n, k in cells], 0))
    state = jnp.concatenate([gather(start, n, k) for n, k in cells], 0)
    state = state + gate * dot(tnorm, out_w[0])
    normed = tile_norm(state).astype(jnp.bfloat16)
    edge_rows = (count - 1) * tokens * 8
    proj_r = dot(normed[:edge_rows], weights[1, :, 2 * hidden : 4 * hidden])
    proj_l = dot(normed[edge_rows:], weights[1, :, : 2 * hidden])
    ends = [(n + 1) * tokens * 8 for n in range(count - 1)]
    own = [slice(end - rows * 8, end) for end in ends]
    own_state = jnp.concatenate([state[part] for part in own], 0)
    own_logit = dot(jnp.concatenate([normed[part] for part in own], 0), weights[1, :, 4 * hidden :])
    pm = jnp.concatenate([mask_left * m for m in row_masks], 0)
    left1[...] = rounded(gate_of(proj_l[:, :hidden]) * proj_l[:, hidden:] * pm)
    pm = jnp.concatenate([mask_right[8 * n : 8 * n + 8] * m for n in range(count - 1) for m in row_masks], 0)
    right1[...] = rounded(gate_of(proj_r[:, :hidden]) * proj_r[:, hidden:] * pm)

    shift = lax.rem(me * rows, 8)
    acc = [[None] * rows for _ in range(count - 1)]
    for k in range(tokens):
        for n in range(count - 1):
            cell = right1[pl.ds((n * tokens + k) * 8, 8), :]
            for t in range(rows):
                term = left1[pl.ds(k * 8 + shift + t, 1), :] * cell
                acc[n][t] = term if k == 0 else acc[n][t] + term
    tri = jnp.concatenate([acc[n][t] for n in range(count - 1) for t in range(rows)], 0)
    tnorm = tile_norm(tri).astype(jnp.bfloat16)
    out = own_state + gate_of(own_logit) * dot(tnorm, out_w[1])
    for n in range(count - 1):
        for t in range(rows):
            at = (n * rows + t) * 8
            updated[t, pl.ds(8 * n, 8), :] = out[at : at + 8]


def exchange(block, bits):
    ranks = lax.axis_size("row")
    hops = [(2 * i + c, 2 * (i ^ bits) + 1 - c) for i in range(ranks) for c in range(2)]
    return lax.ppermute(block, ("row", "col"), hops)


def call(body, inputs, outputs, scratch, name, flops, aliases={}, spaces=None):
    return pl.pallas_call(
        body,
        out_shape=outputs,
        in_specs=[pl.BlockSpec(memory_space=each) for each in spaces or [pltpu.VMEM] * len(inputs)],
        out_specs=[pl.BlockSpec(memory_space=pltpu.VMEM)] * len(outputs),
        scratch_shapes=scratch,
        compiler_params=pltpu.CompilerParams(vmem_limit_bytes=32 << 20),
        input_output_aliases=aliases,
        cost_estimate=pl.CostEstimate(flops=flops, bytes_accessed=1 << 21, transcendentals=0),
        name=name,
    )(*inputs)


def floats(*shapes):
    return [jax.ShapeDtypeStruct(shape, jnp.float32) for shape in shapes]


def like(*arrays):
    return [jax.ShapeDtypeStruct(array.shape, array.dtype) for array in arrays]


def whole_crop_plan(pair, token_mask, chains, chain_bias, proj_weight, gate_weight, out_weight):
    rows, cols, width = pair.shape
    ranks = lax.axis_size("row")
    tokens = token_mask.shape[0]
    hidden = proj_weight.shape[2] // 4
    bias = chain_bias[None, :]
    half = [(2, tokens * cols, width), (2, tokens * cols, width), (2, tokens, cols, hidden), (2, tokens * cols, hidden)]
    half = floats(*half)
    flops = 2 * tokens * cols * width * 5 * hidden
    top = ranks // 2
    masks, halves = [top], [1]
    for bits in range(1, top):
        masks += [bits, bits ^ top]
        halves += [1, 0]
    masks, halves = masks + [0], halves + [0]
    near = [2]
    early = [masks.index(bits) for bits in [top] + near]
    far = exchange(pair, top)
    sent = {bits: exchange(pair, bits) for bits in near}
    kept = call(
        keep_kernel,
        [pltpu.with_memory_space_constraint(pair, pltpu.HBM)],
        like(pair),
        [pltpu.SemaphoreType.DMA],
        "keep",
        flops // ranks,
        spaces=[pltpu.HBM],
    )[0]
    loaded = (pair, bias, proj_weight, gate_weight, out_weight, chains[None, :], token_mask[None, :])
    joined = jax.ShapeDtypeStruct((2, width, 4 * hidden + width), proj_weight.dtype)
    own, bias, weights, out_weight, chains_t, mask_t, *partial = call(
        functools.partial(prep_kernel, masks, halves, early),
        [far, *sent.values()] + [pltpu.with_memory_space_constraint(each, pltpu.HBM) for each in loaded],
        like(pair, bias) + [joined] + like(out_weight) + floats((tokens, width), (tokens, width)) + half,
        [pltpu.VMEM((1, tokens), jnp.int32), pltpu.VMEM((1, tokens), jnp.int32), pltpu.SemaphoreType.DMA((7,))],
        "prep",
        flops // ranks,
        spaces=[pltpu.VMEM] * len(early) + [pltpu.HBM] * 7,
    )
    two = jnp.stack([kept, far])
    parts = [far[None]]
    for bits in range(1, top):
        if bits in sent:
            parts += [sent[bits][None], exchange(far, bits)[None]]
        else:
            parts.append(exchange(two, bits))
    mine = jnp.concatenate(parts + [own[None]], 0)
    other = lax.ppermute(mine, "col", [(0, 1), (1, 0)])
    edge_inputs = (chains_t, mask_t, bias, weights)
    partial = call(
        functools.partial(mine_kernel, masks, halves, early),
        (mine, *edge_inputs, *partial),
        half,
        [],
        "mine",
        flops,
        {n + 5: n for n in range(4)},
    )
    groups = cols // 8 + 1
    extra = [(groups * tokens * 8, hidden), (tokens * 8, hidden), ((groups - 1) * tokens * 8, hidden)]
    return call(
        functools.partial(crop_kernel, masks, halves),
        (other, *edge_inputs, out_weight, *partial),
        floats(pair.shape) + half,
        [pltpu.VMEM(each.shape, jnp.float32) for each in floats(*extra)],
        "crop",
        4 * flops,
        {n + 6: n + 1 for n in range(4)},
    )[0]


def shards(pair, token_mask, *rest):
    tokens = token_mask.shape[0]
    ranks = lax.axis_size("row")
    small = tokens * tokens * pair.shape[2] <= 1 << 18 and ranks & (ranks - 1) == 0 and pair.shape[1] % 8 == 0
    plan = whole_crop_plan if small and lax.axis_size("col") == 2 else sharded_plan
    return plan(pair, token_mask, *rest)


def solution(mesh):
    placed = (P(("group", "row"), "col", None), P("group"), P("group"), P(), P(), P(), P())
    return jax.shard_map(
        shards,
        mesh=mesh,
        in_specs=placed,
        out_specs=P(("group", "row"), "col", None),
        check_vma=False,
    )
```
